32 devices in a mesh: dp: 16 (over z, y, x), mp: 2 (over core).
Axes of the slice: x: 2, y: 2, z: 4, core: 2. Of those that a mesh axis runs over, the one named last changes fastest.
Arguments:
- x_short: bfloat16 [64, 256, 768], P('dp'), may hold values from -6 to 6
- x_long: bfloat16 [32, 512, 768], P('dp'), may hold values from -6 to 6
- len_short: int32 [64], P('dp'), may hold values from 64 to 256, as said below
- len_long: int32 [32], P('dp'), may hold values from 128 to 512, as said below
- boundaries: int32 [15], replicated, may hold values from 1 to 128, as said below
- q_weight: bfloat16 [768, 768], P('dp', 'mp'), may hold values from -0.109375 to 0.109375
- k_weight: bfloat16 [768, 768], P('dp', 'mp'), may hold values from -0.109375 to 0.109375
- v_weight: bfloat16 [768, 768], P('dp', 'mp'), may hold values from -0.21875 to 0.21875
- out_weight: bfloat16 [768, 768], P('dp', 'mp'), may hold values from -0.625 to 0.625
- in_weight: bfloat16 [768, 3072], P('dp', 'mp'), may hold values from -0.21875 to 0.21875
- ff_out_weight: bfloat16 [768, 3072], P('dp', 'mp'), may hold values from -0.15625 to 0.15625
- attn_gain: bfloat16 [768], P('dp'), may hold values from 0.5 to 1.5
- ffn_gain: bfloat16 [768], P('dp'), may hold values from 0.5 to 1.5
- bias_table: bfloat16 [32, 12], P(None, 'mp'), may hold values from -4 to 4
- cot_short: bfloat16 [64, 256, 768], P('dp'), may hold values from -6 to 6
- cot_long: bfloat16 [32, 512, 768], P('dp'), may hold values from -6 to 6
Outputs:
- out_short: bfloat16 [64, 256, 768], P('dp')
- out_long: bfloat16 [32, 512, 768], P('dp')
- grad_short: bfloat16 [64, 256, 768], P('dp')
- grad_long: bfloat16 [32, 512, 768], P('dp')
- grad_q_weight: float32 [768, 768], P('dp', 'mp')
- grad_k_weight: float32 [768, 768], P('dp', 'mp')
- grad_v_weight: float32 [768, 768], P('dp', 'mp')
- grad_out_weight: float32 [768, 768], P('dp', 'mp')
- grad_in_weight: float32 [768, 3072], P('dp', 'mp')
- grad_ff_out_weight: float32 [768, 3072], P('dp', 'mp')
- grad_attn_gain: float32 [768], P('dp')
- grad_ffn_gain: float32 [768], P('dp')
- grad_bias_table: float32 [32, 12], P(None, 'mp')
The draws below stay inside these ranges and needn't reach their ends.
Inputs may be any that keep to these rules, and one draw needn't show every extreme that they name: `len_short`: valid positions at the head of each slot of 256; the rest is padding. `len_long`: valid positions at the head of each slot of 512; the rest is padding. `boundaries`: strictly increasing thresholds on the distance; the first is 1 and the last 128.
All inputs are finite; a program needn't handle non-finite values.
Results may differ from the reference program's by a relative error of at most 0.02.
Values may be sent and summed in bfloat16 or wider, within the bound.
No kernel may reach another device: no remote copies, remote signals or barrier semaphores. Data moves between devices by JAX's collectives and lax.ppermute only.
A program may use at most 192 MiB of HBM per device.

```python
import math
import jax
import jax.numpy as jnp
from jax import lax

D = 768
H = 12
DH = 64
FF = 3072
BUCKETS = 32
DIST = 128
LEN_A = 256
LEN_B = 512
SLOTS_A = 64
SLOTS_B = 32
BOUNDS = 15


def lengths_with_ends(key, slots, length):
    values = jax.random.randint(key, (slots,), length // 4, length + 1, dtype=jnp.int32)
    order = jax.random.permutation(jax.random.fold_in(key, 1), slots)
    values = values.at[order[0]].set(length)
    return values.at[order[1]].set(length // 4).astype(jnp.int32)


def draw_len_short(key, part):
    key = jax.random.fold_in(key, 11)
    return lengths_with_ends(key, SLOTS_A, LEN_A)


def draw_len_long(key, part):
    key = jax.random.fold_in(key, 13)
    return lengths_with_ends(key, SLOTS_B, LEN_B)


def draw_boundaries(key, part):
    key = jax.random.fold_in(key, 17)
    inner = jax.random.permutation(key, DIST - 2)[:BOUNDS - 2].astype(jnp.int32) + 2
    first = jnp.ones((1,), jnp.int32)
    last = jnp.full((1,), DIST, jnp.int32)
    return jnp.concatenate([first, jnp.sort(inner).astype(jnp.int32), last])


def raised(entries, rng, source, target, parts, factor):
    def block_of(axis_at):
        return (jnp.arange(entries.shape[axis_at]) // (entries.shape[axis_at] // parts)).reshape((-1,) + (1,) * (entries.ndim - 1 - axis_at))

    first = jax.random.permutation(rng, parts)[block_of(target)]
    far = (block_of(target) + parts // 2) % parts
    return jnp.where((block_of(source) == first) | (block_of(source) == far), factor * entries, entries)


def levels(key, extent, split, smallest, top_value):
    def one(axis_at, parts):
        heights = jax.random.uniform(jax.random.fold_in(jax.random.fold_in(key, 6), axis_at), (parts,), jnp.float32, smallest / len(split), top_value / len(split))
        return jnp.repeat(jnp.exp(heights), extent[axis_at] // parts).reshape((-1,) + (1,) * (len(extent) - axis_at - 1))

    gain = one(*split[0])
    for cut in split[1:]:
        gain = gain * one(*cut)
    return gain


def normal_values(key, shape, deviation, limit, pieces=(), kind=jnp.bfloat16):
    gain = levels(key, shape, pieces, -0.22, 0.18) if pieces else 1.0
    array = jax.random.normal(key, shape, jnp.float32) * deviation * gain
    return jnp.minimum(jnp.maximum(array, -limit), limit).astype(kind)


def noise_with(own_key, extent, deviation, limit, cuts, heavy, kind=jnp.bfloat16):
    values = deviation * jax.random.normal(own_key, extent, jnp.float32)
    if cuts:
        values = values * levels(own_key, extent, cuts, -0.22, 0.18)
    return jnp.clip(raised(values, jax.random.fold_in(own_key, 3), *heavy), -limit, limit).astype(kind)


def setup_inputs(seed: int = 0) -> dict:
    key_of = jax.random.split(jax.random.key(seed), 17)
    x_short = normal_values(key_of[0], (SLOTS_A, LEN_A, D), 1.0, 6.0, ((0, 16),))
    x_long = normal_values(key_of[1], (SLOTS_B, LEN_B, D), 1.0, 6.0, ((0, 16),))
    len_short = draw_len_short(jax.random.fold_in(key_of[16], 71), 0)
    len_long = draw_len_long(jax.random.fold_in(key_of[16], 71), 0)
    boundaries = draw_boundaries(jax.random.fold_in(key_of[16], 71), 0)
    q_weight = normal_values(key_of[5], (D, H * DH), (4 * D) ** -0.5, 0.109375, ((0, 16), (1, 2)))
    k_weight = normal_values(key_of[6], (D, H * DH), (4 * D) ** -0.5, 0.109375, ((0, 16), (1, 2)))
    v_weight = normal_values(key_of[7], (D, H * DH), D ** -0.5, 0.21875, ((0, 16), (1, 2)))
    out_weight = normal_values(key_of[8], (D, H * DH), (D // 8) ** -0.5, 0.625, ((0, 16), (1, 2)))
    in_weight = normal_values(key_of[9], (D, FF), D ** -0.5, 0.21875, ((0, 16), (1, 2)))
    ff_out_weight = normal_values(key_of[10], (D, FF), (FF // 2) ** -0.5, 0.15625, ((0, 16), (1, 2)))
    attn_gain = jnp.clip(1.0 + 0.1 * jax.random.normal(key_of[11], (D,), jnp.float32), 0.5, 1.5).astype(jnp.bfloat16)
    ffn_gain = jnp.clip(1.0 + 0.1 * jax.random.normal(key_of[12], (D,), jnp.float32), 0.5, 1.5).astype(jnp.bfloat16)
    bias_table = normal_values(key_of[13], (BUCKETS, H), 1.0, 4.0, ((1, 2),))
    cot_short = noise_with(key_of[14], (SLOTS_A, LEN_A, D), 1.0, 6.0, ((0, 16),), (0, 2, 16, 2.0))
    cot_long = noise_with(key_of[15], (SLOTS_B, LEN_B, D), 1.0, 6.0, ((0, 16),), (0, 2, 16, 2.0))
    return dict(x_short=x_short, x_long=x_long, len_short=len_short, len_long=len_long, boundaries=boundaries, q_weight=q_weight, k_weight=k_weight, v_weight=v_weight, out_weight=out_weight, in_weight=in_weight, ff_out_weight=ff_out_weight, attn_gain=attn_gain, ffn_gain=ffn_gain, bias_table=bias_table, cot_short=cot_short, cot_long=cot_long)


EPS = 1e-06
HIGHEST_LEVEL = lax.Precision.HIGHEST

@jax.custom_vjp
def low(v):
    return lax.optimization_barrier(v.astype(jnp.bfloat16)).astype(jnp.float32)

@jax.custom_vjp
def low_back(v):
    return v

def low_keep(v):
    return (low(v), None)

def low_pass(kept, grad):
    return (grad,)

def back_keep(v):
    return (v, None)

def back_low(kept, grad):
    return (low(grad),)
low.defvjp(low_keep, low_pass)
low_back.defvjp(back_keep, back_low)

def bucket_map(length, boundaries):
    places = jnp.arange(length, dtype=jnp.int32)
    dist = places[None, :] - places[:, None]
    half = lax.optimization_barrier(jnp.sum((jnp.abs(dist)[..., None] >= boundaries[None, None, :]).astype(jnp.int32), -1))
    return half + BUCKETS // 2 * (dist > 0).astype(jnp.int32)

def rms_unit(field):
    return field * lax.rsqrt(lax.optimization_barrier(jnp.mean(field * field, -1, keepdims=True)) + EPS)

def layer(weights, x, lengths, bmap):
    q_w, k_w, v_w, o_w, ffn_in_matrix, ffn_out_matrix, gain_a, gain_f, table = weights
    groups, length = (x.shape[0], x.shape[1])
    normed = low(rms_unit(x) * gain_a)

    def project(weight):
        made = jnp.einsum('gld,de->gle', normed, weight, precision=HIGHEST_LEVEL)
        return low_back(low(made)).reshape(groups, length, H, DH)
    queries = project(q_w)
    keys = project(k_w)
    values = project(v_w)
    bias = jnp.transpose(table[bmap], (2, 0, 1))
    scores = jnp.einsum('gihd,gjhd->ghij', queries, keys, precision=HIGHEST_LEVEL) + bias[None]
    scores = low_back(scores)
    valid = jnp.arange(length, dtype=jnp.int32)[None, :] < lengths[:, None]
    scores = jnp.where(valid[:, None, None, :], scores, -1000000000.0)
    probs = low(jax.nn.softmax(scores, -1))
    mixed = jnp.einsum('ghij,gjhd->gihd', probs, values, precision=HIGHEST_LEVEL)
    mixed = low_back(low(mixed)).reshape(groups, length, H * DH)
    attn = low_back(jnp.einsum('gle,fe->glf', mixed, o_w, precision=HIGHEST_LEVEL))
    hidden_activation = x + attn
    ffn_normed_input = low(rms_unit(hidden_activation) * gain_f)
    preactivation = low_back(jnp.einsum('vph,hq->vpq', ffn_normed_input, ffn_in_matrix, precision=HIGHEST_LEVEL))
    active_rows = low(jax.nn.gelu(preactivation, approximate=True))
    return hidden_activation + jnp.einsum('jae,de->jad', active_rows, ffn_out_matrix, precision=HIGHEST_LEVEL)

def run_batch(weights, x, lengths, cot, boundaries, grads):
    slots, length, width = x.shape
    group = math.gcd(slots, max(1, 4096 // length))
    bmap = bucket_map(length, boundaries)
    xs = x.astype(jnp.float32).reshape(slots // group, group, length, width)
    ls = lengths.reshape(slots // group, group)
    cs = cot.astype(jnp.float32).reshape(slots // group, group, length, width)

    def step(total, item):
        xg, lg, cg = item
        out, back = jax.vjp(lambda w, xx: layer(w, xx, lg, bmap), weights, xg)
        grad_w, grad_x = back(cg)
        total = jax.tree.map(lambda a, b: a + b, total, grad_w)
        return (total, (out.astype(jnp.bfloat16), grad_x.astype(jnp.bfloat16)))
    grads, (outs, grad_xs) = lax.scan(step, grads, (xs, ls, cs))
    return (grads, outs.reshape(slots, length, width), grad_xs.reshape(slots, length, width))

def reference(x_short, x_long, len_short, len_long, boundaries, q_weight, k_weight, v_weight, out_weight, in_weight, ff_out_weight, attn_gain, ffn_gain, bias_table, cot_short, cot_long):
    weights = tuple((w.astype(jnp.float32) for w in (q_weight, k_weight, v_weight, out_weight, in_weight, ff_out_weight, attn_gain, ffn_gain, bias_table)))
    grads = jax.tree.map(jnp.zeros_like, weights)
    grads, out_short, grad_short = run_batch(weights, x_short, len_short, cot_short, boundaries, grads)
    grads, out_long, grad_long = run_batch(weights, x_long, len_long, cot_long, boundaries, grads)
    return (out_short, out_long, grad_short, grad_long, grads[0], grads[1], grads[2], grads[3], grads[4], grads[5], grads[6], grads[7], grads[8])
```

```python
import functools

import jax
import jax.numpy as jnp
from jax import lax
from jax.experimental import pallas as pl
from jax.experimental.pallas import tpu as pltpu
from jax.sharding import PartitionSpec as P

DH = 64
LANES = 128
EPS = 1e-06
NEG = -1000000000.0
VMEM_LIMIT = 56 * 1024 * 1024
BF = jnp.bfloat16
F32 = jnp.float32


def dot(left, right):
    return jnp.dot(left, right, preferred_element_type=F32)


def dot_rows(left, right):
    return lax.dot_general(left, right, (((0,), (0,)), ((), ())), preferred_element_type=F32)


def dot_cols(left, right):
    return lax.dot_general(left, right, (((1,), (1,)), ((), ())), preferred_element_type=F32)


def whole(array):
    zeros = (0,) * array.ndim
    return pl.BlockSpec(array.shape, lambda *_: zeros)


def rows_of(array, rows):
    return pl.BlockSpec((rows,) + array.shape[1:], lambda i, *_: (i,) + (0,) * (array.ndim - 1))


def params():
    return pltpu.CompilerParams(vmem_limit_bytes=VMEM_LIMIT)


def out_of(shape, kind):
    return jax.ShapeDtypeStruct(shape, kind)


def distance_buckets(bounds_ref, dist, buckets):
    size = jnp.abs(dist)
    half = jnp.zeros(dist.shape, jnp.int32)
    for b in range(bounds_ref.shape[0]):
        half += (size >= bounds_ref[b]).astype(jnp.int32)
    return half + jnp.where(dist > 0, buckets // 2, 0)


def bases_kernel(bounds_ref, table_ref, near_ref, far_ref):
    heads, _, width = near_ref.shape
    buckets = table_ref.shape[1]
    for ref, sign in ((near_ref, 1), (far_ref, -1)):
        dist = sign * (lax.broadcasted_iota(jnp.int32, (buckets, width), 1) - width // 2)
        marks = distance_buckets(bounds_ref, dist, buckets)
        onehot = (marks == lax.broadcasted_iota(jnp.int32, (buckets, width), 0)).astype(F32)
        line = dot(table_ref[...], onehot.astype(BF))
        row = lax.broadcasted_iota(jnp.int32, (8, width), 0)
        for h in range(heads):
            field = jnp.broadcast_to(line[h : h + 1], (8, width))
            for k in (1, 2, 4):
                field = jnp.where((row & k) != 0, pltpu.roll(field, k, 1), field)
            while field.shape[0] < LANES:
                field = jnp.concatenate([field, pltpu.roll(field, field.shape[0], 1)], 0)
            ref[h] = field


def bias_bases(boundaries, table, heads, width):
    rows = jnp.zeros((8, table.shape[0]), table.dtype).at[: table.shape[1]].set(table.T)
    shape = out_of((heads, LANES, width), F32)
    return pl.pallas_call(
        bases_kernel,
        in_specs=[pl.BlockSpec(memory_space=pltpu.SMEM), pl.BlockSpec(memory_space=pltpu.VMEM)],
        out_specs=[pl.BlockSpec(memory_space=pltpu.VMEM)] * 2,
        out_shape=[shape, shape],
        compiler_params=params(),
    )(boundaries, rows)


def bucket_kernel(bounds_ref, field_ref, sums_ref):
    heads, _, width = field_ref.shape
    buckets = sums_ref.shape[0]
    dist = width // 2 - lax.broadcasted_iota(jnp.int32, (8, width), 1)
    marks = distance_buckets(bounds_ref, dist, buckets)
    row = lax.broadcasted_iota(jnp.int32, (8, width), 0)
    line = jnp.zeros((8, width), F32)
    for h in range(heads):
        field = field_ref[h]
        while field.shape[0] > 8:
            half = field.shape[0] // 2
            field = field[:half] + pltpu.roll(field[half:], width - half, 1)
        for k in (4, 2, 1):
            field = jnp.where((row & k) != 0, pltpu.roll(field, width - k, 1), field)
        line = jnp.where(row == h, jnp.sum(field, 0, keepdims=True), line)
    for b in range(buckets):
        total = jnp.sum(jnp.where(marks == b, line, 0.0), 1, keepdims=True)
        sums_ref[b] = jnp.broadcast_to(total, (8, LANES))


def bucket_sums(boundaries, field, buckets):
    return pl.pallas_call(
        bucket_kernel,
        in_specs=[pl.BlockSpec(memory_space=pltpu.SMEM), pl.BlockSpec(memory_space=pltpu.VMEM)],
        out_specs=pl.BlockSpec(memory_space=pltpu.VMEM),
        out_shape=out_of((buckets, 8, LANES), F32),
        compiler_params=params(),
    )(boundaries, field)[:, :, 0]


def split_low(values, lane, off, rest):
    high = values.astype(BF).astype(F32)
    mid = (values - high).astype(BF).astype(F32)
    low = values - high - mid
    return jnp.where(
        lane == off,
        high,
        jnp.where(lane == off + 1, mid, jnp.where(lane == off + 2, low, rest)),
    )


def three_ones(lane, off):
    return jnp.where((lane >= off) & (lane < off + 3), 1.0, 0.0)


def attend_kernel(
    len_ref, normed_ref, qk_ref, vo_ref, near_ref, aug_ref, k_ref, v_ref, o_ref, attn_ref
):
    length = normed_ref.shape[0]
    width = near_ref.shape[-1]
    cols = k_ref.shape[1]
    valid = len_ref[pl.program_id(0)]
    lane = lax.broadcasted_iota(jnp.int32, (length, LANES), 1)
    place = lax.broadcasted_iota(jnp.int32, (length, LANES), 0)
    masked = jnp.where(place >= valid, NEG, 0.0)
    normed = normed_ref[...]
    for p in range(cols // LANES):
        at = slice(p * LANES, (p + 1) * LANES)
        keys_at = slice(cols + p * LANES, cols + (p + 1) * LANES)
        q = dot(normed, qk_ref[:, at])
        k = dot(normed, qk_ref[:, keys_at])
        v = dot(normed, vo_ref[:, at])
        k_ref[:, at] = k.astype(BF)
        v_ref[:, at] = v.astype(BF)
        mixed = []
        for e in range(2):
            own = (lane >= DH) == (e == 1)
            off = DH * (1 - e)
            h = 2 * p + e
            marker = jnp.where(lane == off + 3, 1.0, 0.0)
            q_own = jnp.where(own, q, marker).astype(BF)
            k_own = jnp.where(own, k, jnp.where(lane == off + 3, masked, 0.0)).astype(BF)
            v_own = jnp.where(own, v, 1.0).astype(BF)
            tops = []
            sums = []
            for a in range(length // LANES):
                rows = slice(a * LANES, (a + 1) * LANES)
                start = width // 2 - a * LANES
                scores = dot_cols(q_own[rows], k_own) + near_ref[h, :, start : start + length]
                top = jnp.max(scores, 1, keepdims=True)
                expo = jnp.exp(scores - top)
                tops.append(jnp.broadcast_to(top, (LANES, LANES)))
                sums.append(dot(expo.astype(BF), v_own))
            sums = jnp.concatenate(sums, 0)
            total = jnp.where(own, pltpu.roll(sums, DH, 1), sums)
            logsum = jnp.concatenate(tops, 0) + jnp.log(total)
            extra = split_low(-logsum, lane, off, marker)
            aug_ref[:, h * LANES : (h + 1) * LANES] = jnp.where(own, q, extra).astype(BF)
            mixed.append(sums / total)
        o_ref[:, at] = jnp.where(lane < DH, mixed[0], mixed[1]).astype(BF)
    attn_ref[...] = dot_cols(o_ref[...], vo_ref[:, cols:]).astype(BF)


def attend(lengths, normed, qk, vo, near, length):
    rows, width = normed.shape
    cols = vo.shape[1] // 2
    slots = rows // length
    shapes = [(rows, 2 * cols), (rows, cols), (rows, cols), (rows, cols), (rows, width)]
    shapes = [out_of(s, BF) for s in shapes]
    return pl.pallas_call(
        attend_kernel,
        grid_spec=pltpu.PrefetchScalarGridSpec(
            num_scalar_prefetch=1,
            grid=(slots,),
            in_specs=[rows_of(normed, length), whole(qk), whole(vo), whole(near)],
            out_specs=[rows_of(s, length) for s in shapes],
        ),
        out_shape=shapes,
        compiler_params=params(),
    )(lengths, normed, qk, vo, near)


def attend_back_kernel(
    len_ref,
    grad_ref,
    normed_ref,
    aug_ref,
    k_ref,
    v_ref,
    o_ref,
    qk_ref,
    vo_ref,
    far_ref,
    *refs,
):
    kept = refs[:-7]
    part_ref, gqk_ref, gvo_ref, gbase_ref, gq_scr, gkv_scr, ds_scr = refs[-7:]
    length = grad_ref.shape[0]
    width = far_ref.shape[-1]
    cols = k_ref.shape[1]
    slot = pl.program_id(0)
    valid = len_ref[slot]

    @pl.when(slot == 0)
    def _():
        for i, ref in enumerate((gqk_ref, gvo_ref, gbase_ref)):
            ref[...] = kept[i][...] if kept else jnp.zeros_like(ref)

    lane = lax.broadcasted_iota(jnp.int32, (length, LANES), 1)
    place = lax.broadcasted_iota(jnp.int32, (length, LANES), 0)
    masked = jnp.where(place >= valid, NEG, 0.0)
    grad = grad_ref[...]
    for p in range(cols // LANES):
        at = slice(p * LANES, (p + 1) * LANES)
        k = k_ref[:, at].astype(F32)
        v = v_ref[:, at].astype(F32)
        o = o_ref[:, at].astype(F32)
        go = dot(grad, vo_ref[:, cols + p * LANES : cols + (p + 1) * LANES]).astype(BF).astype(F32)
        both = go * o
        grads = []
        for e in range(2):
            own = (lane >= DH) == (e == 1)
            off = DH * (1 - e)
            h = 2 * p + e
            q_own = aug_ref[:, h * LANES : (h + 1) * LANES]
            ones = three_ones(lane, off)
            k_own = jnp.where(own, k, jnp.where(lane == off + 3, masked, ones)).astype(BF)
            v_own = jnp.where(own, v, ones).astype(BF)
            delta = jnp.sum(jnp.where(own, both, 0.0), 1, keepdims=True)
            extra = split_low(-delta, lane, off, 0.0)
            g_own = jnp.where(own, go, extra).astype(BF)
            gks = []
            gvs = []
            for a in range(length // LANES):
                rows = slice(a * LANES, (a + 1) * LANES)
                start = width // 2 - a * LANES
                span = slice(start, start + length)
                probs = jnp.exp(dot_cols(k_own[rows], q_own) + far_ref[h, :, span])
                ds = probs * dot_cols(v_own[rows], g_own)
                gbase_ref[h, :, span] += ds
                ds = ds.astype(BF)
                ds_scr[rows, :] = ds
                gvs.append(dot(probs.astype(BF), g_own))
                gks.append(dot(ds, q_own))
            gq = dot_rows(ds_scr[...], k_own)
            grads.append((gq, jnp.concatenate(gks, 0), jnp.concatenate(gvs, 0)))
        first = lane < DH
        gq, gk, gv = (jnp.where(first, a, b).astype(BF) for a, b in zip(*grads))
        gq_scr[:, at] = gq
        gq_scr[:, cols + p * LANES : cols + (p + 1) * LANES] = gk
        gkv_scr[:, at] = gv
    normed = normed_ref[...]
    gqk = gq_scr[...]
    gv = gkv_scr[...]
    part_ref[...] = (dot_cols(gqk, qk_ref[...]) + dot_cols(gv, vo_ref[:, :cols])).astype(BF)
    gqk_ref[...] += dot_rows(normed, gqk)
    gvo_ref[:, :cols] += dot_rows(normed, gv)
    gvo_ref[:, cols:] += dot_rows(grad, o_ref[...])


def attend_back(lengths, grad, normed, aug, k, v, o, qk, vo, far, kept, length):
    rows, width = normed.shape
    cols = vo.shape[1] // 2
    slots = rows // length
    part = out_of((rows, width), BF)
    totals = [out_of(qk.shape, F32), out_of(vo.shape, F32), out_of(far.shape, F32)]
    return pl.pallas_call(
        attend_back_kernel,
        grid_spec=pltpu.PrefetchScalarGridSpec(
            num_scalar_prefetch=1,
            grid=(slots,),
            in_specs=[rows_of(a, length) for a in (grad, normed, aug, k, v, o)]
            + [whole(a) for a in (qk, vo, far) + tuple(kept)],
            out_specs=[rows_of(part, length)] + [whole(t) for t in totals],
            scratch_shapes=[
                pltpu.VMEM((length, 2 * cols), BF),
                pltpu.VMEM((length, cols), BF),
                pltpu.VMEM((length, length), BF),
            ],
        ),
        out_shape=[part] + totals,
        compiler_params=params(),
    )(lengths, grad, normed, aug, k, v, o, qk, vo, far, *kept)


def gelu_parts(x):
    c = 0.7978845608028654
    d = c * 0.044715
    square = x * x
    t = jnp.tanh(x * (c + d * square))
    half = 0.5 + 0.5 * t
    slope = half + (0.5 * x) * (1.0 - t * t) * (c + 3.0 * d * square)
    return x * half, slope


def ffn_kernel(normed_ref, g_ref, win_ref, wout_ref, *refs):
    kept = refs[:-4]
    out_ref, gn_ref, gin_ref, gout_ref = refs[-4:]

    @pl.when(pl.program_id(0) == 0)
    def _():
        gin_ref[...] = jnp.zeros_like(gin_ref)
        gout_ref[...] = jnp.zeros_like(gout_ref)

    normed = normed_ref[...]
    g = g_ref[...]
    act, slope = gelu_parts(dot(normed, win_ref[...]))
    act = act.astype(BF)
    gpre = (dot(g, wout_ref[...]) * slope).astype(BF)
    out = dot_cols(act, wout_ref[...])
    gn = dot_cols(gpre, win_ref[...])
    if kept:
        out += kept[0][...]
        gn += kept[1][...]
    out_ref[...] = out.astype(out_ref.dtype)
    gn_ref[...] = gn.astype(gn_ref.dtype)
    gout_ref[...] += dot_rows(g, act)
    gin_ref[...] += dot_rows(normed, gpre)


def ffn(normed, g, win, wout, kept, kind, tile=512):
    rows, width = normed.shape
    field = out_of((rows, width), kind)
    weight = out_of(win.shape, F32)
    return pl.pallas_call(
        ffn_kernel,
        grid=(rows // tile,),
        in_specs=[rows_of(normed, tile), rows_of(g, tile), whole(win), whole(wout)]
        + [rows_of(a, tile) for a in kept],
        out_specs=[rows_of(field, tile), rows_of(field, tile), whole(weight), whole(weight)],
        out_shape=[field, field, weight, weight],
        compiler_params=params(),
    )(normed, g, win, wout, *kept)


def send_xor(array, mask, size):
    return lax.ppermute(array, "dp", [(i, i ^ mask) for i in range(size)])


def exchange(array, size):
    return [
        lax.ppermute(array, "mp", [(i, i ^ k) for i in range(size)]) for k in range(1, size)
    ]


def group_sum(array, size):
    total = array.astype(F32)
    for other in exchange(array, size):
        total = total + other.astype(F32)
    return total


def stages(size, swap):
    bits = [1 << b for b in range(size.bit_length() - 1)]
    low, high = bits[:2], bits[2:]
    groups = [high[i : i + 2] for i in range(0, len(high), 2)]
    return groups + [[b] for b in (low[::-1] if swap else low)]


def combos(bits):
    masks = [0]
    for b in bits:
        masks = masks + [m | b for m in masks]
    return masks


def gather(part, size, me, swap):
    held = part[(None,) * (size.bit_length() - 1)]
    axes = size.bit_length() - 1
    for bits in stages(size, swap):
        got = [held] + [send_xor(held, m, size) for m in combos(bits)[1:]]
        for b in bits:
            axis = axes - b.bit_length()
            mine = (me & b) == 0
            pairs = [(got[2 * i], got[2 * i + 1]) for i in range(len(got) // 2)]
            got = [
                jnp.concatenate([jnp.where(mine, p, q), jnp.where(mine, q, p)], axis)
                for p, q in pairs
            ]
        held = got[0]
    return held.reshape((size * part.shape[0],) + part.shape[1:])


def scatter(total, size, me, swap):
    axes = size.bit_length() - 1
    held = total.reshape((2,) * axes + (total.shape[0] // size,) + total.shape[1:])
    for bits in reversed(stages(size, swap)):
        got = []
        for m in combos(bits):
            piece = held
            for b in bits:
                at = jnp.where(((me ^ m) & b) == 0, 0, 1)
                piece = lax.dynamic_slice_in_dim(piece, at, 1, axes - b.bit_length())
            got.append(piece if m == 0 else send_xor(piece.astype(BF), m, size))
        held = got[0]
        for piece in got[1:]:
            held = held + piece.astype(F32)
    return held.reshape((total.shape[0] // size,) + total.shape[1:])


def scatter_both(total, size, me):
    half = total.shape[1] // 2
    return scatter(total[:, :half], size, me, False), scatter(total[:, half:], size, me, True)


def small_sum(array, size):
    bits = [1 << b for b in range(size.bit_length() - 1)]
    for i in range(0, len(bits), 2):
        total = array
        for m in combos(bits[i : i + 2])[1:]:
            total = total + send_xor(array, m, size)
        array = total
    return array


def rms_parts(field):
    scale = lax.rsqrt(jnp.mean(field * field, -1, keepdims=True) + EPS)
    return (scale, field * scale)


def norm_back(grad_unit, unit, scale):
    return scale * (grad_unit - unit * jnp.mean(grad_unit * unit, -1, keepdims=True))


def pad_cols(array, cols):
    return jnp.pad(array, ((0, 0), (0, cols - array.shape[1]))) if cols > array.shape[1] else array


def on_device(
    sizes,
    x_short,
    x_long,
    len_short,
    len_long,
    boundaries,
    q_weight,
    k_weight,
    v_weight,
    out_weight,
    in_weight,
    ff_out_weight,
    attn_gain,
    ffn_gain,
    bias_table,
    cot_short,
    cot_long,
):
    dp, mp = sizes
    me = lax.axis_index("dp")
    width = x_short.shape[2]
    heads = bias_table.shape[1]
    real = heads * DH
    cols = -(-real // LANES) * LANES
    chunks = 3
    units = in_weight.shape[1] // chunks
    span = 2 * max(x_short.shape[1], x_long.shape[1])

    gains = small_gather(jnp.stack([attn_gain, ffn_gain]).astype(F32), dp, me)
    gain_a, gain_f = gains[0], gains[1]
    padded = [pad_cols(w, cols) for w in (q_weight, k_weight, v_weight, out_weight)]
    qk = gather(jnp.concatenate(padded[:2], 1), dp, me, False)
    vo = gather(jnp.concatenate(padded[2:], 1), dp, me, True)
    ffn_weights = []
    for c in range(chunks):
        at = slice(c * units, (c + 1) * units)
        ffn_weights.append(
            (gather(in_weight[:, at], dp, me, False), gather(ff_out_weight[:, at], dp, me, True))
        )

    near, far = bias_bases(boundaries, bias_table, cols // DH, span)

    batches = []
    for x, lengths, cot in ((x_short, len_short, cot_short), (x_long, len_long, cot_long)):
        length = x.shape[1]
        field = x.reshape(-1, width).astype(F32)
        normed = (rms_parts(field)[1] * gain_a).astype(BF)
        aug, k, v, o, attn = attend(lengths, normed, qk, vo, near, length)
        batches.append((x, lengths, cot, length, normed, aug, k, v, o, attn))

    middles = []
    for x, lengths, cot, length, normed, aug, k, v, o, attn in batches:
        middle = x.reshape(-1, width).astype(F32) + group_sum(attn, mp)
        middles.append(middle)
    middle = jnp.concatenate(middles, 0)
    scale_f, unit_f = rms_parts(middle)
    normed_f = (unit_f * gain_f).astype(BF)
    g = jnp.concatenate([cot_short.reshape(-1, width), cot_long.reshape(-1, width)], 0)
    kept = ()
    grads_f = []
    for c in range(chunks):
        out, gn, gin, gout = ffn(
            normed_f, g, *ffn_weights[c], kept, BF if c == chunks - 1 else F32
        )
        kept = (out, gn)
        grads_f.append((scatter(gin, dp, me, False), scatter(gout, dp, me, True)))
    grad_in_weight = jnp.concatenate([a for a, _ in grads_f], 1)
    grad_ff_out_weight = jnp.concatenate([b for _, b in grads_f], 1)
    out = (middle + group_sum(out, mp)).astype(BF)
    grad_norm_f = group_sum(gn, mp)
    grad_gain_f = jnp.sum(grad_norm_f * unit_f, 0)
    grad_mid = g.astype(F32) + norm_back(grad_norm_f * gain_f, unit_f, scale_f)
    grad_attn = grad_mid.astype(BF)

    split = x_short.shape[0] * x_short.shape[1]
    kept = ()
    parts = []
    for i, (x, lengths, cot, length, normed, aug, k, v, o, attn) in enumerate(batches):
        rows = slice(0, split) if i == 0 else slice(split, None)
        part, *kept = attend_back(
            lengths, grad_attn[rows], normed, aug, k, v, o, qk, vo, far, kept, length
        )
        parts.append(part)
    gqk, gvo, gbase = kept
    shares_qk = scatter(gqk, dp, me, False)
    shares_vo = scatter(gvo, dp, me, True)
    table_grad = bucket_sums(boundaries, gbase, bias_table.shape[0])[:, :heads]

    grad_xs = []
    grad_gain_a = 0.0
    for i, (x, lengths, cot, length, normed, aug, k, v, o, attn) in enumerate(batches):
        rows = slice(0, split) if i == 0 else slice(split, None)
        scale_a, unit_a = rms_parts(x.reshape(-1, width).astype(F32))
        grad_norm_a = group_sum(parts[i], mp)
        grad_gain_a = grad_gain_a + jnp.sum(grad_norm_a * unit_a, 0)
        grad_x = grad_mid[rows] + norm_back(grad_norm_a * gain_a, unit_a, scale_a)
        grad_xs.append(grad_x.astype(BF).reshape(x.shape))

    small = jnp.concatenate([grad_gain_a, grad_gain_f, table_grad.reshape(-1)])
    small = small_sum(small, dp)
    share = width // dp
    gain_a_grad = lax.dynamic_slice_in_dim(small, me * share, share)
    gain_f_grad = lax.dynamic_slice_in_dim(small, width + me * share, share)
    table_grad = small[2 * width :].reshape(table_grad.shape)
    return (
        out[:split].reshape(x_short.shape),
        out[split:].reshape(x_long.shape),
        grad_xs[0],
        grad_xs[1],
        shares_qk[:, :real],
        shares_qk[:, cols : cols + real],
        shares_vo[:, :real],
        shares_vo[:, cols : cols + real],
        grad_in_weight,
        grad_ff_out_weight,
        gain_a_grad,
        gain_f_grad,
        table_grad,
    )


def small_gather(part, size, me):
    rows, share = part.shape
    wide = jnp.zeros((rows, share * size), part.dtype)
    return small_sum(lax.dynamic_update_slice_in_dim(wide, part, me * share, 1), size)


def solution(mesh):
    sizes = (mesh.shape["dp"], mesh.shape["mp"])
    return jax.shard_map(
        functools.partial(on_device, sizes),
        mesh=mesh,
        in_specs=(
            P("dp", None, None),
            P("dp", None, None),
            P("dp"),
            P("dp"),
            P(),
            P("dp", "mp"),
            P("dp", "mp"),
            P("dp", "mp"),
            P("dp", "mp"),
            P("dp", "mp"),
            P("dp", "mp"),
            P("dp"),
            P("dp"),
            P(None, "mp"),
            P("dp", None, None),
            P("dp", None, None),
        ),
        out_specs=(
            P("dp", None, None),
            P("dp", None, None),
            P("dp", None, None),
            P("dp", None, None),
            P("dp", "mp"),
            P("dp", "mp"),
            P("dp", "mp"),
            P("dp", "mp"),
            P("dp", "mp"),
            P("dp", "mp"),
            P("dp"),
            P("dp"),
            P(None, "mp"),
        ),
        check_vma=False,
    )
```

```python
import functools

import jax
import jax.numpy as jnp
from jax import lax
from jax.experimental import pallas as pl
from jax.experimental.pallas import tpu as pltpu
from jax.sharding import PartitionSpec as P

DH = 64
LANES = 128
EPS = 1e-06
NEG = -1000000000.0
VMEM_LIMIT = 56 * 1024 * 1024
BF = jnp.bfloat16
F32 = jnp.float32
ANY = pl.BlockSpec(memory_space=pl.ANY)
SMEM = pl.BlockSpec(memory_space=pltpu.SMEM)
VMEM = pl.BlockSpec(memory_space=pltpu.VMEM)


def dot(left, right):
    return jnp.dot(left, right, preferred_element_type=F32)


def dot_rows(left, right):
    return lax.dot_general(left, right, (((0,), (0,)), ((), ())), preferred_element_type=F32)


def dot_cols(left, right):
    return lax.dot_general(left, right, (((1,), (1,)), ((), ())), preferred_element_type=F32)


def tiles(array, rows):
    return pl.BlockSpec((rows,) + array.shape[1:], lambda i: (i,) + (0,) * (array.ndim - 1))


def fixed(array):
    return pl.BlockSpec(array.shape, lambda i: (0,) * array.ndim)


def pair_tiles(pair, rows):
    count = pair[0].shape[0] // rows
    rest = (0,) * (pair[0].ndim - 1)
    shape = (rows,) + pair[0].shape[1:]
    return [
        pl.BlockSpec(shape, lambda i: (jnp.minimum(i, count - 1),) + rest),
        pl.BlockSpec(shape, lambda i: (jnp.maximum(i - count, 0),) + rest),
    ]


def pick(count, first, second):
    return jnp.where(pl.program_id(0) < count, first[...], second[...])


def out_of(shape, kind):
    return jax.ShapeDtypeStruct(tuple(shape), kind)


def call(kernel, outs, args, *, ins=None, out_specs=None, grid=None, scratch=(), flops=0, after=()):
    ins = list(ins or [VMEM] * len(args))
    extra = {} if grid is None else {"grid": grid}

    def body(*refs):
        kernel(*refs[: len(args)], *refs[len(args) + len(after) :])

    moved = sum(o.size * o.dtype.itemsize for o in outs) + sum(a.size * a.dtype.itemsize for a in args)
    return pl.pallas_call(
        body,
        out_shape=list(outs),
        in_specs=ins + [ANY] * len(after),
        out_specs=list(out_specs or [VMEM] * len(outs)),
        scratch_shapes=list(scratch),
        compiler_params=pltpu.CompilerParams(vmem_limit_bytes=VMEM_LIMIT),
        cost_estimate=pl.CostEstimate(flops=int(flops), bytes_accessed=int(moved), transcendentals=0),
        **extra,
    )(*args, *after)


class Ring:
    def __init__(self, sizes):
        self.dp, self.mp = sizes
        self.me = lax.axis_index("dp")
        self.odd = lax.axis_index("mp") & 1
        self.quarter = self.dp // 4
        j = jnp.arange(self.dp, dtype=jnp.int32)
        first = (j // self.quarter) & 1
        last = j // (2 * self.quarter)
        low = jnp.where(self.odd == 0, first + 2 * last, 2 * first + last)
        self.places = self.me ^ (4 * (j % self.quarter) + low)
        rel = self.me ^ j
        bit0, bit1 = rel & 1, (rel >> 1) & 1
        first, last = jnp.where(self.odd == 0, bit0, bit1), jnp.where(self.odd == 0, bit1, bit0)
        self.spots = (rel >> 2) + self.quarter * (first + 2 * last)

    def far(self, array, step):
        return lax.ppermute(array, "dp", [(i, i ^ (4 * step)) for i in range(self.dp)])

    def near(self, array, masks):
        pairs = [
            (i * self.mp + c, (i ^ masks[c & 1]) * self.mp + c)
            for i in range(self.dp)
            for c in range(self.mp)
        ]
        return lax.ppermute(array, ("dp", "mp"), pairs)

    def exchange(self, array):
        return [
            lax.ppermute(array, "mp", [(i, i ^ k) for i in range(self.mp)])
            for k in range(1, self.mp)
        ]


def join_kernel(*refs):
    sources, out = refs[:-1], refs[-1]
    at = 0
    for ref in sources:
        out[at : at + ref.shape[0]] = ref[...]
        at += ref.shape[0]


def join(parts, after=()):
    count = sum(p.shape[0] for p in parts)
    shape = (count,) + parts[0].shape[1:]
    return call(join_kernel, [out_of(shape, parts[0].dtype)], parts, after=after)[0]


def aligned(rows):
    return rows % 16 == 0


def blocks_of(ring, held, got):
    if aligned(held.shape[1]):
        return (held, got)
    blocks = jnp.take(jnp.concatenate([held, got], 0), ring.spots, axis=0)
    return (blocks.reshape((-1,) + held.shape[2:]),)


def load_start(places, sources, to, sem, cols):
    copies = []
    if len(sources) == 2:
        half, rows, _ = sources[0].shape
        for j in range(2 * half):
            at = pl.multiple_of(places[j] * rows, 16)
            block = sources[j // half].at[j % half, :, cols]
            copies.append(pltpu.make_async_copy(block, to.at[pl.ds(at, rows)], sem.at[j]))
    else:
        copies.append(pltpu.make_async_copy(sources[0].at[:, cols], to, sem.at[0]))
    for c in copies:
        c.start()
    return copies


def load(places, sources, to, sem, cols):
    for c in load_start(places, sources, to, sem, cols):
        c.wait()


def emit(places, total, keep, send, extra=None):
    half, rows, _ = keep.shape
    for j in range(2 * half):
        at = pl.multiple_of(places[j] * rows, 16)
        block = total[pl.ds(at, rows), :]
        if extra is not None:
            block = block + extra
        if j < half:
            keep[j] = block
        else:
            send[j - half] = block.astype(BF)


def emitted(ring, rows, cols):
    share = rows // ring.dp
    if aligned(share):
        shape = (ring.dp // 2, share, cols)
        return [out_of(shape, F32), out_of(shape, BF)]
    return [out_of((rows, cols), F32)]


def halves(ring, outs, extra=None):
    if len(outs) == 2:
        return outs
    blocks = outs[0].reshape(ring.dp, -1, outs[0].shape[1])
    if extra is not None:
        blocks = blocks + extra
    blocks = jnp.take(blocks, ring.places, axis=0)
    return blocks[: ring.dp // 2], blocks[ring.dp // 2 :].astype(BF)


def fold_kernel(keep_ref, got_ref, *refs):
    quarter = got_ref.shape[0] // 2
    keep, sends = refs[0], refs[1:]
    for j in range(quarter):
        keep[j] = keep_ref[j] + got_ref[j].astype(F32)
    for j in range(quarter):
        total = (keep_ref[quarter + j] + got_ref[quarter + j].astype(F32)).astype(BF)
        sends[0][j] = total


def fold(keep, got, after=()):
    quarter = keep.shape[0] // 2
    shape = (quarter,) + keep.shape[1:]
    return call(fold_kernel, [out_of(shape, F32), out_of(shape, BF)], [keep, got], after=after)


def part_kernel(keep_ref, got_ref, keep, *sends):
    keep[...] = keep_ref[0] + got_ref[0].astype(F32)
    for j, send in enumerate(sends):
        send[...] = (keep_ref[j + 1] + got_ref[j + 1].astype(F32)).astype(BF)


def part(keep, got, after=()):
    shape = keep.shape[1:]
    outs = [out_of(shape, F32)] + [out_of(shape, BF)] * (keep.shape[0] - 1)
    return call(part_kernel, outs, [keep, got], after=after)


def final_kernel(spans, groups, keep, *refs):
    got, outs = refs[:groups], refs[groups:]
    for out, span in zip(outs, spans):
        at = 0
        for start, stop in span:
            total = keep[:, start:stop]
            for g in got:
                total = total + g[:, start:stop].astype(F32)
            out[:, at : at + stop - start] = total
            at += stop - start


def final(keep, got, spans, after=()):
    outs = [out_of((keep.shape[0], sum(b - a for a, b in span)), F32) for span in spans]
    return call(functools.partial(final_kernel, spans, len(got)), outs, [keep, *got], after=after)


def distance_buckets(bounds_ref, dist, buckets):
    size = jnp.abs(dist)
    half = jnp.zeros(dist.shape, jnp.int32)
    for b in range(bounds_ref.shape[0]):
        half += (size >= bounds_ref[b]).astype(jnp.int32)
    return half + jnp.where(dist > 0, buckets // 2, 0)


def bases_kernel(bounds_ref, table_ref, near_ref, far_ref):
    heads, _, width = near_ref.shape
    buckets = table_ref.shape[1]
    for ref, sign in ((near_ref, 1), (far_ref, -1)):
        dist = sign * (lax.broadcasted_iota(jnp.int32, (8, width), 1) - width // 2)
        marks = distance_buckets(bounds_ref, dist, buckets)
        marks = jnp.concatenate([marks] * (buckets // 8), 0)
        onehot = (marks == lax.broadcasted_iota(jnp.int32, (buckets, width), 0)).astype(F32)
        line = dot(table_ref[...], onehot.astype(BF))
        row = lax.broadcasted_iota(jnp.int32, (8, width), 0)
        for h in range(heads):
            field = jnp.broadcast_to(line[h : h + 1], (8, width))
            for k in (1, 2, 4):
                field = jnp.where((row & k) != 0, pltpu.roll(field, k, 1), field)
            while field.shape[0] < LANES:
                field = jnp.concatenate([field, pltpu.roll(field, field.shape[0], 1)], 0)
            ref[h] = field


def bias_bases(boundaries, table, heads, width):
    rows = jnp.zeros((8, table.shape[0]), table.dtype).at[: table.shape[1]].set(table.T)
    shape = out_of((heads, LANES, width), F32)
    return call(bases_kernel, [shape, shape], [boundaries, rows], ins=[SMEM, VMEM])


def bucket_field(bounds_ref, fields, buckets, first):
    width = fields[0].shape[-1]
    dist = width // 2 - lax.broadcasted_iota(jnp.int32, (8, width), 1)
    marks = distance_buckets(bounds_ref, dist, buckets)
    row = lax.broadcasted_iota(jnp.int32, (8, width), 0)
    line = jnp.zeros((8, width), F32)
    for h, field in enumerate(fields):
        while field.shape[0] > 8:
            half = field.shape[0] // 2
            field = field[:half] + pltpu.roll(field[half:], width - half, 1)
        for k in (4, 2, 1):
            field = jnp.where((row & k) != 0, pltpu.roll(field, width - k, 1), field)
        line = jnp.where(row == h, jnp.sum(field, 0, keepdims=True), line)
    lane = lax.broadcasted_iota(jnp.int32, (8, LANES), 1)
    out = jnp.zeros((8, LANES), F32)
    for b in range(buckets):
        total = jnp.sum(jnp.where(marks == b, line, 0.0), 1, keepdims=True)
        out = jnp.where(lane == first + b, total, out)
    return out


def split_low(values, lane, off, rest):
    high = values.astype(BF).astype(F32)
    mid = (values - high).astype(BF).astype(F32)
    low = values - high - mid
    return jnp.where(
        lane == off,
        high,
        jnp.where(lane == off + 1, mid, jnp.where(lane == off + 2, low, rest)),
    )


def three_ones(lane, off):
    return jnp.where((lane >= off) & (lane < off + 3), 1.0, 0.0)


def slots_of(batches):
    at = 0
    for b, (slots, length) in enumerate(batches):
        for s in range(slots):
            yield b, s, length, slice(at, at + length)
            at += length


def attend_kernel(batches, pair, halves, *refs):
    places, lens = refs[0], refs[1 : 1 + len(batches)]
    refs = refs[1 + len(batches) :]
    normed_ref, near_ref = refs[:2]
    sources = refs[2 : 2 + halves]
    aug_ref, k_ref, v_ref, o_ref, w_scr, sem = refs[2 + halves :]
    width = near_ref.shape[-1]
    load(places, sources, w_scr, sem, pl.ds(pair * 3 * LANES, 3 * LANES))
    for b, s, length, span in slots_of(batches):
        valid = lens[b][s]
        lane = lax.broadcasted_iota(jnp.int32, (length, LANES), 1)
        place = lax.broadcasted_iota(jnp.int32, (length, LANES), 0)
        masked = jnp.where(place >= valid, NEG, 0.0)
        qkv = dot(normed_ref[span, :], w_scr[...])
        q, k, v = (qkv[:, i * LANES : (i + 1) * LANES] for i in range(3))
        k_ref[span, :] = k.astype(BF)
        v_ref[span, :] = v.astype(BF)
        mixed = []
        for e in range(2):
            own = (lane >= DH) == (e == 1)
            off = DH * (1 - e)
            marker = jnp.where(lane == off + 3, 1.0, 0.0)
            q_own = jnp.where(own, q, marker).astype(BF)
            k_own = jnp.where(own, k, jnp.where(lane == off + 3, masked, 0.0)).astype(BF)
            v_own = jnp.where(own, v, 1.0).astype(BF)
            tops = []
            sums = []
            for a in range(length // LANES):
                rows = slice(a * LANES, (a + 1) * LANES)
                start = width // 2 - a * LANES
                scores = dot_cols(q_own[rows], k_own) + near_ref[e, :, start : start + length]
                top = jnp.max(scores, 1, keepdims=True)
                expo = jnp.exp(scores - top)
                tops.append(jnp.broadcast_to(top, (LANES, LANES)))
                sums.append(dot(expo.astype(BF), v_own))
            sums = jnp.concatenate(sums, 0)
            total = jnp.where(own, pltpu.roll(sums, DH, 1), sums)
            logsum = jnp.concatenate(tops, 0) + jnp.log(total)
            extra = split_low(-logsum, lane, off, marker)
            aug_ref[span, e * LANES : (e + 1) * LANES] = jnp.where(own, q, extra).astype(BF)
            mixed.append(sums / total)
        o_ref[span, :] = jnp.where(lane < DH, mixed[0], mixed[1]).astype(BF)


def pair_of(near, pair):
    return pl.BlockSpec((2,) + near.shape[1:], lambda i: (pair, 0, 0))


def attend(ring, batches, lens, normed, weights, near, pair, after=()):
    rows, width = normed.shape
    shapes = [out_of((rows, c * LANES), BF) for c in (2, 1, 1, 1)]
    return call(
        functools.partial(attend_kernel, batches, pair, len(weights)),
        shapes,
        [ring.places, *lens, normed, near, *weights],
        ins=[SMEM] * (1 + len(lens)) + [fixed(normed), pair_of(near, pair)] + [ANY] * len(weights),
        out_specs=[fixed(s) for s in shapes],
        grid=(1,),
        scratch=[pltpu.VMEM((width, 3 * LANES), BF), pltpu.SemaphoreType.DMA((ring.dp,))],
        flops=1e10,
        after=after,
    )


def attend_back_kernel(batches, *refs):
    lens = refs[: len(batches)]
    go_ref, aug_ref, k_ref, v_ref, o_ref, far_ref, grads_ref, gbase_ref, ds_scr = refs[len(batches) :]
    width = far_ref.shape[-1]
    gbase_ref[...] = jnp.zeros_like(gbase_ref)
    for b, s, length, span in slots_of(batches):
        valid = lens[b][s]
        lane = lax.broadcasted_iota(jnp.int32, (length, LANES), 1)
        place = lax.broadcasted_iota(jnp.int32, (length, LANES), 0)
        masked = jnp.where(place >= valid, NEG, 0.0)
        k = k_ref[span, :].astype(F32)
        v = v_ref[span, :].astype(F32)
        go = go_ref[span, :].astype(F32)
        both = go * o_ref[span, :].astype(F32)
        grads = []
        for e in range(2):
            own = (lane >= DH) == (e == 1)
            off = DH * (1 - e)
            q_own = aug_ref[span, e * LANES : (e + 1) * LANES]
            ones = three_ones(lane, off)
            k_own = jnp.where(own, k, jnp.where(lane == off + 3, masked, ones)).astype(BF)
            v_own = jnp.where(own, v, ones).astype(BF)
            delta = jnp.sum(jnp.where(own, both, 0.0), 1, keepdims=True)
            g_own = jnp.where(own, go, split_low(-delta, lane, off, 0.0)).astype(BF)
            gks = []
            gvs = []
            for a in range(length // LANES):
                rows = slice(a * LANES, (a + 1) * LANES)
                start = width // 2 - a * LANES
                cols = slice(start, start + length)
                probs = jnp.exp(dot_cols(k_own[rows], q_own) + far_ref[e, :, cols])
                ds = probs * dot_cols(v_own[rows], g_own)
                gbase_ref[e, :, cols] += ds
                ds = ds.astype(BF)
                ds_scr[e, rows, :length] = ds
                gvs.append(dot(probs.astype(BF), g_own))
                gks.append(dot(ds, q_own))
            gq = dot_rows(ds_scr[e, :length, :length], k_own)
            grads.append((gq, jnp.concatenate(gks, 0), jnp.concatenate(gvs, 0)))
        first = lane < DH
        for i, (a, b) in enumerate(zip(*grads)):
            grads_ref[span, i * LANES : (i + 1) * LANES] = jnp.where(first, a, b).astype(BF)


def attend_back(batches, lens, go, aug, k, v, o, far, pair, after=()):
    rows = go.shape[0]
    longest = max(length for _, length in batches)
    outs = [out_of((rows, 3 * LANES), BF), out_of((2,) + far.shape[1:], F32)]
    go_spec = pl.BlockSpec((rows, LANES), lambda i: (0, pair))
    return call(
        functools.partial(attend_back_kernel, batches),
        outs,
        [*lens, go, aug, k, v, o, far],
        ins=[SMEM] * len(lens) + [go_spec] + [fixed(a) for a in (aug, k, v, o)] + [pair_of(far, pair)],
        out_specs=[fixed(o) for o in outs],
        grid=(1,),
        scratch=[pltpu.VMEM((2, longest, longest), BF)],
        flops=2e10,
        after=after,
    )


def project_out_kernel(halves, pairs, places, *refs):
    o_refs, refs = refs[:pairs], refs[pairs:]
    sources, (attn_ref, w_scr, sem) = refs[:halves], refs[halves:]
    cols = pairs * LANES

    @pl.when(pl.program_id(0) == 0)
    def _():
        load(places, sources, w_scr, sem, pl.ds(3 * cols, cols))

    o = jnp.concatenate([r[...] for r in o_refs], 1)
    attn_ref[...] = dot_cols(o, w_scr[...]).astype(BF)


def project_out(ring, mixed, weights, width, tile=512):
    rows = mixed[0].shape[0]
    pairs = len(mixed)
    out = out_of((rows, width), BF)
    return call(
        functools.partial(project_out_kernel, len(weights), pairs),
        [out],
        [ring.places, *mixed, *weights],
        ins=[SMEM] + [tiles(m, tile) for m in mixed] + [ANY] * len(weights),
        out_specs=[tiles(out, tile)],
        grid=(rows // tile,),
        scratch=[pltpu.VMEM((width, pairs * LANES), BF), pltpu.SemaphoreType.DMA((ring.dp,))],
        flops=2 * rows * width * pairs * LANES,
    )[0]


def rms_parts(field):
    scale = lax.rsqrt(jnp.mean(field * field, -1, keepdims=True) + EPS)
    return (scale, field * scale)


def norm_back(grad_unit, unit, scale):
    return scale * (grad_unit - unit * jnp.mean(grad_unit * unit, -1, keepdims=True))


def total_of(count, refs):
    total = pick(count, *refs[:2]).astype(F32)
    for r in refs[2:]:
        total = total + r[...].astype(F32)
    return total


def norm_kernel(count, gain_ref, short_ref, long_ref, normed_ref):
    unit = rms_parts(pick(count, short_ref, long_ref).astype(F32))[1]
    normed_ref[...] = (unit * gain_ref[0:1, :]).astype(BF)


def norm(gains, xs, tile=512, after=()):
    out = out_of((xs[0].shape[0] + xs[1].shape[0], xs[0].shape[1]), BF)
    return call(
        functools.partial(norm_kernel, xs[0].shape[0] // tile),
        [out],
        [gains, *xs],
        ins=[fixed(gains)] + pair_tiles(xs, tile),
        out_specs=[tiles(out, tile)],
        grid=(out.shape[0] // tile,),
        after=after,
    )[0]


def store_pair(count, first, second, value):
    @pl.when(pl.program_id(0) < count)
    def _():
        first[...] = value

    @pl.when(pl.program_id(0) >= count)
    def _():
        second[...] = value


def add_kernel(count, addends, *refs):
    store_pair(count, *refs[addends:], total_of(count, refs[:addends]).astype(BF))


def add_all(xs, fields, tile=512, after=()):
    outs = [out_of(x.shape, BF) for x in xs]
    return call(
        functools.partial(add_kernel, xs[0].shape[0] // tile, 2 + len(fields)),
        outs,
        [*xs, *fields],
        ins=pair_tiles(xs, tile) + [tiles(f, tile) for f in fields],
        out_specs=pair_tiles(outs, tile),
        grid=((xs[0].shape[0] + xs[1].shape[0]) // tile,),
        after=after,
    )


def input_grad_kernel(count, gain_ref, short_ref, long_ref, mid_ref, *refs):
    scale, unit = rms_parts(pick(count, short_ref, long_ref).astype(F32))
    grad = refs[0][...].astype(F32)
    for r in refs[1:-2]:
        grad = grad + r[...].astype(F32)
    value = mid_ref[...] + norm_back(grad * gain_ref[0:1, :], unit, scale)
    store_pair(count, *refs[-2:], value.astype(BF))


def input_grad(gains, xs, mid, fields, tile=512, after=()):
    outs = [out_of(x.shape, BF) for x in xs]
    return call(
        functools.partial(input_grad_kernel, xs[0].shape[0] // tile),
        outs,
        [gains, *xs, mid, *fields],
        ins=[fixed(gains)] + pair_tiles(xs, tile) + [tiles(f, tile) for f in (mid, *fields)],
        out_specs=pair_tiles(outs, tile),
        grid=(mid.shape[0] // tile,),
        after=after,
    )


def gelu_parts(x):
    c = 0.7978845608028654
    d = c * 0.044715
    square = x * x
    t = jnp.tanh(x * (c + d * square))
    half = 0.5 + 0.5 * t
    slope = half + (0.5 * x) * (1.0 - t * t) * (c + 3.0 * d * square)
    return x * half, slope


def ffn_first_kernel(halves, addends, emits, count, places, gain_ref, *refs):
    g_refs, refs = refs[:2], refs[2:]
    x_refs, refs = refs[:addends], refs[addends:]
    sources, refs = refs[:halves], refs[halves:]
    normed_ref, out_ref, gn_ref = refs[:3]
    grads, (w_scr, total, sem) = refs[3 : 3 + emits], refs[3 + emits :]
    units = w_scr.shape[1] // 2
    step = pl.program_id(0)

    @pl.when(step == 0)
    def _():
        total[...] = jnp.zeros_like(total)
        load(places, sources, w_scr, sem, pl.ds(0, 2 * units))

    normed = (rms_parts(total_of(count, x_refs))[1] * gain_ref[1:2, :]).astype(BF)
    normed_ref[...] = normed
    g = pick(count, *g_refs)
    win, wout = w_scr[:, :units], w_scr[:, units:]
    act, slope = gelu_parts(dot(normed, win))
    act = act.astype(BF)
    gpre = (dot(g, wout) * slope).astype(BF)
    out_ref[...] = dot_cols(act, wout)
    gn_ref[...] = dot_cols(gpre, win)
    total[:, :units] += dot_rows(normed, gpre)
    total[:, units:] += dot_rows(g, act)

    @pl.when(step == pl.num_programs(0) - 1)
    def _():
        if emits == 2:
            emit(places, total, *grads)
        else:
            grads[0][...] = total[...]


def ffn_first(ring, gains, gs, xs, fields, weights, units, tile=512, after=()):
    rows, width = fields[0].shape
    normed, field = out_of((rows, width), BF), out_of((rows, width), F32)
    grads = emitted(ring, width, 2 * units)
    addends = 2 + len(fields)
    count = xs[0].shape[0] // tile
    return call(
        functools.partial(ffn_first_kernel, len(weights), addends, len(grads), count),
        [normed, field, field] + grads,
        [ring.places, gains, *gs, *xs, *fields, *weights],
        ins=[SMEM, fixed(gains)]
        + pair_tiles(gs, tile)
        + pair_tiles(xs, tile)
        + [tiles(a, tile) for a in fields]
        + [ANY] * len(weights),
        out_specs=[tiles(normed, tile), tiles(field, tile), tiles(field, tile)]
        + [fixed(o) for o in grads],
        grid=(rows // tile,),
        scratch=[
            pltpu.VMEM((width, 2 * units), BF),
            pltpu.VMEM((width, 2 * units), F32),
            pltpu.SemaphoreType.DMA((ring.dp,)),
        ],
        flops=12 * rows * width * units,
        after=after,
    )


def ffn_next_kernel(halves, count, places, normed_ref, *refs):
    g_refs, (out_in, gn_in), refs = refs[:2], refs[2:4], refs[4:]
    sources, refs = refs[:halves], refs[halves:]
    out_ref, gn_ref, act_ref, gpre_ref, w_scr, sem = refs
    units = w_scr.shape[1] // 2

    @pl.when(pl.program_id(0) == 0)
    def _():
        load(places, sources, w_scr, sem, pl.ds(0, 2 * units))

    win, wout = w_scr[:, :units], w_scr[:, units:]
    act, slope = gelu_parts(dot(normed_ref[...], win))
    act = act.astype(BF)
    gpre = (dot(pick(count, *g_refs), wout) * slope).astype(BF)
    act_ref[...] = act
    gpre_ref[...] = gpre
    out_ref[...] = (out_in[...] + dot_cols(act, wout)).astype(BF)
    gn_ref[...] = (gn_in[...] + dot_cols(gpre, win)).astype(BF)


def ffn_next(ring, normed, gs, out, gn, weights, units, tile=512, after=()):
    rows, width = normed.shape
    outs = [out_of((rows, width), BF)] * 2 + [out_of((rows, units), BF)] * 2
    return call(
        functools.partial(ffn_next_kernel, len(weights), gs[0].shape[0] // tile),
        outs,
        [ring.places, normed, *gs, out, gn, *weights],
        ins=[SMEM, tiles(normed, tile)]
        + pair_tiles(gs, tile)
        + [tiles(out, tile), tiles(gn, tile)]
        + [ANY] * len(weights),
        out_specs=[tiles(o, tile) for o in outs],
        grid=(rows // tile,),
        scratch=[pltpu.VMEM((width, 2 * units), BF), pltpu.SemaphoreType.DMA((ring.dp,))],
        flops=8 * rows * width * units,
        after=after,
    )


def ffn_grads_kernel(emits, count, places, normed_ref, *refs):
    g_refs, (gpre_ref, act_ref) = refs[:2], refs[2:4]
    grads, total = refs[4:-1], refs[-1]
    step = pl.program_id(0)
    units = act_ref.shape[1]

    @pl.when(step == 0)
    def _():
        total[...] = jnp.zeros_like(total)

    total[:, :units] += dot_rows(normed_ref[...], gpre_ref[...])
    total[:, units:] += dot_rows(pick(count, *g_refs), act_ref[...])

    @pl.when(step == pl.num_programs(0) - 1)
    def _():
        if emits == 2:
            emit(places, total, *grads)
        else:
            grads[0][...] = total[...]


def ffn_grads(ring, normed, gs, gpre, act, tile=512, after=()):
    rows, width = normed.shape
    cols = 2 * act.shape[1]
    outs = emitted(ring, width, cols)
    return call(
        functools.partial(ffn_grads_kernel, len(outs), gs[0].shape[0] // tile),
        outs,
        [ring.places, normed, *gs, gpre, act],
        ins=[SMEM, tiles(normed, tile)]
        + pair_tiles(gs, tile)
        + [tiles(gpre, tile), tiles(act, tile)],
        out_specs=[fixed(o) for o in outs],
        grid=(rows // tile,),
        scratch=[pltpu.VMEM((width, cols), F32)],
        flops=2 * rows * width * cols,
        after=after,
    )


def middle_back_kernel(halves, groups, pairs, count, places, gain_ref, *refs):
    g_refs, refs = refs[:2], refs[2:]
    x_refs, refs = refs[: groups + 2], refs[groups + 2 :]
    gn_refs, refs = refs[:groups], refs[groups:]
    sources, (mid_ref, attn_ref, go_ref, gain_out, w_scr, sem) = refs[:halves], refs[halves:]
    cols = pairs * LANES

    @pl.when(pl.program_id(0) == 0)
    def _():
        gain_out[...] = jnp.zeros_like(gain_out)
        load(places, sources, w_scr, sem, pl.ds(3 * cols, cols))

    scale, unit = rms_parts(total_of(count, x_refs))
    gn = gn_refs[0][...].astype(F32)
    for r in gn_refs[1:]:
        gn = gn + r[...].astype(F32)
    gain_out[...] += jnp.sum((gn * unit).reshape(-1, 8, unit.shape[1]), 0)
    mid = pick(count, *g_refs).astype(F32) + norm_back(gn * gain_ref[1:2, :], unit, scale)
    mid_ref[...] = mid
    grad = mid.astype(BF)
    attn_ref[...] = grad
    go_ref[...] = dot(grad, w_scr[...]).astype(BF)


def middle_back(ring, gains, gs, xs, fields, gns, weights, pairs, tile=512, after=()):
    rows, width = fields[0].shape
    cols = pairs * LANES
    outs = [out_of((rows, width), F32), out_of((rows, width), BF), out_of((rows, cols), BF)]
    gain = out_of((8, width), F32)
    return call(
        functools.partial(
            middle_back_kernel, len(weights), len(gns), pairs, xs[0].shape[0] // tile
        ),
        outs + [gain],
        [ring.places, gains, *gs, *xs, *fields, *gns, *weights],
        ins=[SMEM, fixed(gains)]
        + pair_tiles(gs, tile)
        + pair_tiles(xs, tile)
        + [tiles(a, tile) for a in (*fields, *gns)]
        + [ANY] * len(weights),
        out_specs=[tiles(o, tile) for o in outs] + [fixed(gain)],
        grid=(rows // tile,),
        scratch=[pltpu.VMEM((width, cols), BF), pltpu.SemaphoreType.DMA((ring.dp,))],
        flops=2 * rows * width * cols,
        after=after,
    )


def input_back_kernel(halves, pairs, count, places, short_ref, long_ref, *refs):
    g_refs, refs = refs[:pairs], refs[pairs:]
    sources, (part_ref, gain_out, w_scr, sem) = refs[:halves], refs[halves:]

    @pl.when(pl.program_id(0) == 0)
    def _():
        gain_out[...] = jnp.zeros_like(gain_out)
        load(places, sources, w_scr, sem, pl.ds(0, 3 * pairs * LANES))

    part = dot_cols(jnp.concatenate([r[...] for r in g_refs], 1), w_scr[...])
    unit = rms_parts(pick(count, short_ref, long_ref).astype(F32))[1]
    gain_out[...] += jnp.sum((part * unit).reshape(-1, 8, unit.shape[1]), 0)
    part_ref[...] = part.astype(BF)


def input_back(ring, xs, grads, weights, tile=512, after=()):
    rows, width = grads[0].shape[0], xs[0].shape[1]
    pairs = len(grads)
    out, gain = out_of((rows, width), BF), out_of((8, width), F32)
    return call(
        functools.partial(input_back_kernel, len(weights), pairs, xs[0].shape[0] // tile),
        [out, gain],
        [ring.places, *xs, *grads, *weights],
        ins=[SMEM] + pair_tiles(xs, tile) + [tiles(a, tile) for a in grads] + [ANY] * len(weights),
        out_specs=[tiles(out, tile), fixed(gain)],
        grid=(rows // tile,),
        scratch=[pltpu.VMEM((width, 3 * pairs * LANES), BF), pltpu.SemaphoreType.DMA((ring.dp,))],
        flops=2 * rows * width * 3 * pairs * LANES,
        after=after,
    )


def last_kernel(emits, pairs, buckets, places, bounds, normed_ref, grad_ref, gain_f, gain_a, *refs):
    g_refs, refs = refs[:pairs], refs[pairs:]
    o_refs, refs = refs[:pairs], refs[pairs:]
    bases, refs = refs[:pairs], refs[pairs:]
    grads, refs = refs[:emits], refs[emits:]
    table_ref, total = refs
    step = pl.program_id(0)
    cols = pairs * LANES

    @pl.when(step == 0)
    def _():
        total[...] = jnp.zeros_like(total)

    normed = normed_ref[...]
    grad = grad_ref[...]
    total[:, : 3 * cols] += dot_rows(normed, jnp.concatenate([r[...] for r in g_refs], 1))
    total[:, 3 * cols : 4 * cols] += dot_rows(grad, jnp.concatenate([r[...] for r in o_refs], 1))

    @pl.when(step == pl.num_programs(0) - 1)
    def _():
        row = lax.broadcasted_iota(jnp.int32, (LANES, total.shape[0]), 0)
        both = jnp.where(
            row == 0,
            jnp.sum(gain_a[...], 0, keepdims=True),
            jnp.where(row == 1, jnp.sum(gain_f[...], 0, keepdims=True), 0.0),
        )
        total[:, 4 * cols :] = jnp.transpose(both)
        fields = [ref[e] for ref in bases for e in range(2)]
        table = bucket_field(bounds, fields, buckets, 8)
        table_ref[...] = table
        if emits == 2:
            rows = grads[0].shape[1]
            table = jnp.concatenate([table, jnp.zeros((rows - 8, LANES), F32)], 0)
            table = jnp.concatenate([jnp.zeros((rows, 4 * cols), F32), table], 1)
            emit(places, total, *grads, extra=table)
        else:
            grads[0][...] = total[...]


def last_grads(ring, boundaries, buckets, normed, grad, gain_f, gain_a, grads, mixed, bases, tile=512):
    rows, width = normed.shape
    pairs = len(grads)
    cols = 4 * pairs * LANES + LANES
    outs = emitted(ring, width, cols)
    table = out_of((8, LANES), F32)
    *outs, table = call(
        functools.partial(last_kernel, len(outs), pairs, buckets),
        outs + [table],
        [ring.places, boundaries, normed, grad, gain_f, gain_a, *grads, *mixed, *bases],
        ins=[SMEM, SMEM, tiles(normed, tile), tiles(grad, tile), fixed(gain_f), fixed(gain_a)]
        + [tiles(a, tile) for a in (*grads, *mixed)]
        + [fixed(b) for b in bases],
        out_specs=[fixed(o) for o in outs] + [fixed(table)],
        grid=(rows // tile,),
        scratch=[pltpu.VMEM((width, cols), F32)],
        flops=2 * rows * width * cols,
    )
    share = width // ring.dp
    table = jnp.pad(table, ((0, share - 8), (cols - LANES, 0)))
    return halves(ring, outs, table)


def pad_cols(array, cols):
    return jnp.pad(array, ((0, 0), (0, cols - array.shape[1]))) if cols > array.shape[1] else array


def small_sum(array, size):
    bits = [1 << b for b in range(size.bit_length() - 1)]
    for i in range(0, len(bits), 2):
        masks = [0]
        for b in bits[i : i + 2]:
            masks = masks + [m | b for m in masks]
        total = array
        for m in masks[1:]:
            total = total + lax.ppermute(array, "dp", [(i, i ^ m) for i in range(size)])
        array = total
    return array


def small_gather(part, size, me):
    rows, share = part.shape
    wide = jnp.zeros((rows, share * size), part.dtype)
    return small_sum(lax.dynamic_update_slice_in_dim(wide, part, me * share, 1), size)


def on_device(
    sizes,
    x_short,
    x_long,
    len_short,
    len_long,
    boundaries,
    q_weight,
    k_weight,
    v_weight,
    out_weight,
    in_weight,
    ff_out_weight,
    attn_gain,
    ffn_gain,
    bias_table,
    cot_short,
    cot_long,
):
    ring = Ring(sizes)
    quarter = ring.quarter
    width = x_short.shape[2]
    buckets, heads = bias_table.shape
    real = heads * DH
    cols = -(-real // LANES) * LANES
    pairs = cols // LANES
    units = in_weight.shape[1] // 2
    span = 2 * max(x_short.shape[1], x_long.shape[1])
    batches = [x.shape[:2] for x in (x_short, x_long)]
    lens = (len_short, len_long)

    xs = [x.reshape(-1, width) for x in (x_short, x_long)]
    gs = [g.reshape(-1, width) for g in (cot_short, cot_long)]

    padded = [pad_cols(w, cols) for w in (q_weight, k_weight, v_weight, out_weight)]
    pieces = [w[:, p * LANES : (p + 1) * LANES] for p in range(pairs) for w in padded[:3]]
    own = jnp.concatenate(pieces + [padded[3]], 1)[None]
    got = [ring.far(own, s) for s in range(1, quarter)]
    gains = small_gather(jnp.stack([attn_gain, ffn_gain]).astype(F32), ring.dp, ring.me)
    near, far = bias_bases(boundaries, bias_table, cols // DH, span)
    normed = norm(gains, xs)
    held = join([own] + got, after=[near, normed])
    got = ring.near(held, (1, 2))
    ffn_own = [
        jnp.concatenate([w[:, at : at + units] for w in (in_weight, ff_out_weight)], 1)[None]
        for at in (0, units)
    ]
    own1 = join([ffn_own[0]], after=[held])
    got1 = [ring.far(own1, s) for s in range(1, quarter)]
    held = join([held, got])
    qkvo = blocks_of(ring, held, ring.near(held, (2, 1)))

    fwd = []
    after = ()
    for p in range(pairs):
        if p == 1:
            held1 = join([own1] + got1, after=[fwd[-1][0]])
            got1 = ring.near(held1, (1, 2))
            own2 = join([ffn_own[1]], after=[held1])
            got2 = [ring.far(own2, s) for s in range(1, quarter)]
            after = [held1, own2]
        if p == pairs - 1:
            held1 = join([held1, got1], after=[fwd[-1][0]])
            got1 = ring.near(held1, (2, 1))
            held2 = join([own2] + got2, after=[held1])
            got2 = ring.near(held2, (1, 2))
            after = [held1, held2]
        fwd.append(attend(ring, batches, lens, normed, qkvo, near, p, after=after))
    attn = project_out(ring, [f[3] for f in fwd], qkvo, width)
    fields = [attn] + ring.exchange(attn)
    held2 = join([held2, got2], after=[attn])
    got2 = ring.near(held2, (2, 1))
    first, second = blocks_of(ring, held1, got1), blocks_of(ring, held2, got2)

    normed_f, out, gn, *grad1 = ffn_first(
        ring, gains, gs, xs, fields, first, units, after=[held2]
    )
    keep1, send = halves(ring, grad1)
    got1 = ring.near(send, (2, 1))
    out, gn, act, gpre = ffn_next(ring, normed_f, gs, out, gn, second, units)
    gns = [gn] + ring.exchange(gn)
    outs = [out] + ring.exchange(out)
    keep1, send = fold(keep1, got1, after=[gn])
    got1 = ring.near(send, (1, 2))
    keep2, send = halves(ring, ffn_grads(ring, normed_f, gs, gpre, act, after=[keep1]))
    got2 = ring.near(send, (2, 1))
    mid, grad_attn, go, gain_f = middle_back(
        ring, gains, gs, xs, fields, gns, qkvo, pairs, after=[keep2]
    )

    back = []
    for p in range(pairs):
        if p == 0:
            keep1, *sends = part(keep1, got1, after=[go])
            got1 = [ring.far(s, i + 1) for i, s in enumerate(sends)]
            keep2, send = fold(keep2, got2, after=[keep1])
            got2 = ring.near(send, (1, 2))
            after = [keep2]
        if p == 1:
            keep2, *sends = part(keep2, got2, after=[back[-1][0]])
            got2 = [ring.far(s, i + 1) for i, s in enumerate(sends)]
            in1, out1 = final(keep1, got1, [[(0, units)], [(units, 2 * units)]])
            after = [keep2, in1]
        aug, k, v, o = fwd[p]
        back.append(attend_back(batches, lens, go, aug, k, v, o, far, p, after=after))

    grads = [b[0] for b in back]
    gna, gain_a = input_back(ring, xs, grads, qkvo)
    gnas = [gna] + ring.exchange(gna)
    keep, send = last_grads(
        ring,
        boundaries,
        buckets,
        normed,
        grad_attn,
        gain_f,
        gain_a,
        grads,
        [f[3] for f in fwd],
        [b[1] for b in back],
    )
    got = ring.near(send, (2, 1))
    grad_xs = input_grad(gains, xs, mid, gnas, after=[keep])
    keep, send = fold(keep, got, after=[grad_xs[0]])
    got = ring.near(send, (1, 2))
    ys = add_all(xs, [*fields, *outs], after=[keep])
    keep, *sends = part(keep, got, after=[ys[0]])
    got = [ring.far(s, i + 1) for i, s in enumerate(sends)]
    in2, out2 = final(keep2, got2, [[(0, units)], [(units, 2 * units)]], after=[keep])
    step = 3 * LANES
    at = [
        [(p * step + i * LANES, p * step + (i + 1) * LANES) for p in range(pairs)] for i in range(3)
    ]
    at += [[(3 * cols, 4 * cols)], [(4 * cols, 4 * cols + LANES)]]
    gq, gk, gv, go, small = final(keep, got, at)
    gain_a_grad = small[:, 0]
    for other in ring.exchange(gain_a_grad):
        gain_a_grad = gain_a_grad + other
    table_grad = small[:8, 8 : 8 + buckets].T[:, :heads]
    return (
        ys[0].reshape(x_short.shape),
        ys[1].reshape(x_long.shape),
        grad_xs[0].reshape(x_short.shape),
        grad_xs[1].reshape(x_long.shape),
        gq[:, :real],
        gk[:, :real],
        gv[:, :real],
        go[:, :real],
        jnp.concatenate([in1, in2], 1),
        jnp.concatenate([out1, out2], 1),
        gain_a_grad,
        small[:, 1],
        table_grad,
    )


def solution(mesh):
    sizes = (mesh.shape["dp"], mesh.shape["mp"])
    return jax.shard_map(
        functools.partial(on_device, sizes),
        mesh=mesh,
        in_specs=(
            P("dp", None, None),
            P("dp", None, None),
            P("dp"),
            P("dp"),
            P(),
            P("dp", "mp"),
            P("dp", "mp"),
            P("dp", "mp"),
            P("dp", "mp"),
            P("dp", "mp"),
            P("dp", "mp"),
            P("dp"),
            P("dp"),
            P(None, "mp"),
            P("dp", None, None),
            P("dp", None, None),
        ),
        out_specs=(
            P("dp", None, None),
            P("dp", None, None),
            P("dp", None, None),
            P("dp", None, None),
            P("dp", "mp"),
            P("dp", "mp"),
            P("dp", "mp"),
            P("dp", "mp"),
            P("dp", "mp"),
            P("dp", "mp"),
            P("dp"),
            P("dp"),
            P(None, "mp"),
        ),
        check_vma=False,
    )
```

```python
import functools

import jax
import jax.numpy as jnp
from jax import lax
from jax.experimental import pallas as pl
from jax.experimental.pallas import tpu as pltpu
from jax.sharding import PartitionSpec as P

DH = 64
LANES = 128
EPS = 1e-06
NEG = -1000000000.0
VMEM_LIMIT = 56 * 1024 * 1024
BF = jnp.bfloat16
F32 = jnp.float32
ANY = pl.BlockSpec(memory_space=pl.ANY)
SMEM = pl.BlockSpec(memory_space=pltpu.SMEM)
VMEM = pl.BlockSpec(memory_space=pltpu.VMEM)


def dot(left, right):
    return jnp.dot(left, right, preferred_element_type=F32)


def dot_rows(left, right):
    return lax.dot_general(left, right, (((0,), (0,)), ((), ())), preferred_element_type=F32)


def dot_cols(left, right):
    return lax.dot_general(left, right, (((1,), (1,)), ((), ())), preferred_element_type=F32)


def tiles(array, rows):
    return pl.BlockSpec((rows,) + array.shape[1:], lambda i: (i,) + (0,) * (array.ndim - 1))


def fixed(array):
    return pl.BlockSpec(array.shape, lambda i: (0,) * array.ndim)


def pair_tiles(pair, rows):
    count = pair[0].shape[0] // rows
    rest = (0,) * (pair[0].ndim - 1)
    shape = (rows,) + pair[0].shape[1:]
    return [
        pl.BlockSpec(shape, lambda i: (jnp.minimum(i, count - 1),) + rest),
        pl.BlockSpec(shape, lambda i: (jnp.maximum(i - count, 0),) + rest),
    ]


def pick(count, first, second):
    return jnp.where(pl.program_id(0) < count, first[...], second[...])


def out_of(shape, kind):
    return jax.ShapeDtypeStruct(tuple(shape), kind)


def call(kernel, outs, args, *, ins=None, out_specs=None, grid=None, scratch=(), us=2, after=(), through=()):
    ins = list(ins or [VMEM] * len(args))
    out_specs = list(out_specs or [VMEM] * len(outs))
    extra = {} if grid is None else {"grid": grid}
    idle = len(after) + len(through)

    def body(*refs):
        given, made = refs[: len(args)], refs[len(args) + idle :]
        kernel(*given, *made[: len(outs)], *made[len(outs) + len(through) :])

    return pl.pallas_call(
        body,
        out_shape=list(outs) + [out_of(t.shape, t.dtype) for t in through],
        in_specs=ins + [ANY] * idle,
        out_specs=out_specs + [ANY] * len(through),
        scratch_shapes=list(scratch),
        compiler_params=pltpu.CompilerParams(vmem_limit_bytes=VMEM_LIMIT),
        input_output_aliases={len(args) + len(after) + i: len(outs) + i for i in range(len(through))},
        cost_estimate=pl.CostEstimate(flops=int(us * 1e9), bytes_accessed=1000, transcendentals=0),
        **extra,
    )(*args, *after, *through)


class Ring:
    def __init__(self, sizes):
        self.dp, self.mp = sizes
        self.me = lax.axis_index("dp")
        self.odd = lax.axis_index("mp") & 1
        self.quarter = self.dp // 4
        j = jnp.arange(self.dp, dtype=jnp.int32)
        first = (j // self.quarter) & 1
        last = j // (2 * self.quarter)
        low = jnp.where(self.odd == 0, first + 2 * last, 2 * first + last)
        self.order = self.me ^ (4 * (j % self.quarter) + low)
        rel = self.me ^ j
        bit0, bit1 = rel & 1, (rel >> 1) & 1
        first, last = jnp.where(self.odd == 0, bit0, bit1), jnp.where(self.odd == 0, bit1, bit0)
        self.spots = (rel >> 2) + self.quarter * (first + 2 * last)
        lead = (lax.axis_index("mp") == 0).astype(jnp.int32)
        self.places = jnp.concatenate([self.order, lead[None]])

    def far(self, array):
        return [
            lax.ppermute(array, "dp", [(i, i ^ (4 * step)) for i in range(self.dp)])
            for step in range(1, self.quarter)
        ]

    def far_all(self, arrays):
        return [
            lax.ppermute(a, "dp", [(i, i ^ (4 * (step + 1))) for i in range(self.dp)])
            for step, a in enumerate(arrays)
        ]

    def near(self, array, masks):
        pairs = [
            (i * self.mp + c, (i ^ masks[c & 1]) * self.mp + c)
            for i in range(self.dp)
            for c in range(self.mp)
        ]
        return lax.ppermute(array, ("dp", "mp"), pairs)

    def first(self, array):
        return self.near(array, (1, 2))

    def last(self, array):
        return self.near(array, (2, 1))

    def exchange(self, array):
        return [
            lax.ppermute(array, "mp", [(i, i ^ k) for i in range(self.mp)])
            for k in range(1, self.mp)
        ]


def join_kernel(plan, *refs):
    sources, outs = refs[: -len(plan)], refs[-len(plan) :]
    for (chosen, start, stop), out in zip(plan, outs):
        at = 0
        for i in chosen:
            count = sources[i].shape[0]
            out[at : at + count] = sources[i][:, :, start:stop]
            at += count


def join(arrays, plan, after=(), through=()):
    outs = []
    for chosen, start, stop in plan:
        count = sum(arrays[i].shape[0] for i in chosen)
        outs.append(out_of((count, arrays[0].shape[1], stop - start), arrays[0].dtype))
    return call(functools.partial(join_kernel, plan), outs, arrays, after=after, through=through)


def aligned(rows):
    return rows % 16 == 0


def blocks_of(ring, held, got):
    if aligned(held.shape[1]):
        return (held, got)
    blocks = jnp.take(jnp.concatenate([held, got], 0), ring.spots, axis=0)
    return (blocks.reshape((-1,) + held.shape[2:]),)


def load_start(places, sources, to, sem, cols):
    copies = []
    if len(sources) == 2:
        half, rows, _ = sources[0].shape
        for j in range(2 * half):
            at = pl.multiple_of(places[j] * rows, 16)
            block = sources[j // half].at[j % half, :, cols]
            copies.append(pltpu.make_async_copy(block, to.at[pl.ds(at, rows)], sem.at[j]))
    else:
        copies.append(pltpu.make_async_copy(sources[0].at[:, cols], to, sem.at[0]))
    for c in copies:
        c.start()
    return copies


def load(places, sources, to, sem, cols):
    for c in load_start(places, sources, to, sem, cols):
        c.wait()


def load_all(places, refs, to, sem, plan):
    step = len(refs) // len(plan)
    copies = []
    to_at = 0
    for i, (at, count) in enumerate(plan):
        there = to.at[:, pl.ds(to_at, count)]
        copies += load_start(places, refs[i * step : (i + 1) * step], there, sem.at[i], pl.ds(at, count))
        to_at += count
    for c in copies:
        c.wait()


def emit(places, total, keep, send, extra=None):
    half, rows, _ = keep.shape
    for j in range(2 * half):
        at = pl.multiple_of(places[j] * rows, 16)
        block = total[pl.ds(at, rows), :]
        if extra is not None:
            block = block + extra
        if j < half:
            keep[j] = block
        else:
            send[j - half] = block.astype(BF)


def emitted(ring, rows, cols):
    share = rows // ring.dp
    if aligned(share):
        shape = (ring.dp // 2, share, cols)
        return [out_of(shape, F32), out_of(shape, BF)]
    return [out_of((rows, cols), F32)]


def halves(ring, outs, extra=None):
    if len(outs) == 2:
        return outs
    blocks = outs[0].reshape(ring.dp, -1, outs[0].shape[1])
    if extra is not None:
        blocks = blocks + extra
    blocks = jnp.take(blocks, ring.order, axis=0)
    return blocks[: ring.dp // 2], blocks[ring.dp // 2 :].astype(BF)


def fold_kernel(modes, *refs):
    ins, outs = refs[: 2 * len(modes)], refs[2 * len(modes) :]
    for mode in modes:
        keep, got = ins[:2]
        ins = ins[2:]
        count = got.shape[0] if mode else got.shape[0] // 2
        if mode:
            outs[0][...] = keep[0] + got[0].astype(F32)
            for j in range(1, count):
                outs[j][...] = (keep[j] + got[j].astype(F32)).astype(BF)
            outs = outs[count:]
        else:
            outs[0][...] = keep[:count] + got[:count].astype(F32)
            outs[1][...] = (keep[count:] + got[count:].astype(F32)).astype(BF)
            outs = outs[2:]


def fold(*items, after=(), through=()):
    outs = []
    args = []
    for keep, got, mode in items:
        args += [keep, got]
        if mode:
            shape = keep.shape[1:]
            outs += [out_of(shape, F32)] + [out_of(shape, BF)] * (keep.shape[0] - 1)
        else:
            shape = (keep.shape[0] // 2,) + keep.shape[1:]
            outs += [out_of(shape, F32), out_of(shape, BF)]
    kernel = functools.partial(fold_kernel, [m for *_, m in items])
    return call(kernel, outs, args, after=after, through=through)


def final_kernel(counts, plan, scaled, gain_ref, *refs):
    weights, refs = refs[: len(scaled)], refs[len(scaled) :]
    fields = []
    for count in counts:
        total = refs[0][...]
        for r in refs[1:count]:
            total = total + r[...].astype(F32)
        fields.append(total)
        refs = refs[count:]
    outs, gain_out = refs[:-1], refs[-1]
    sums = jnp.zeros(gain_out.shape, F32)
    for i, (out, spans) in enumerate(zip(outs, plan)):
        at = 0
        for f, start, stop in spans:
            value = fields[f][:, start:stop]
            there = slice(at, at + stop - start)
            if i in scaled:
                kept = weights[scaled.index(i)][:, there].astype(F32)
                sums += jnp.sum(value * kept, 1, keepdims=True)
                value = value * gain_ref[...]
            out[:, there] = value
            at += stop - start
    gain_out[...] = sums


def final(items, plan, scaled, gain, weights, after=()):
    rows = gain.shape[0]
    outs = [out_of((rows, sum(b - a for _, a, b in spans)), F32) for spans in plan]
    outs.append(out_of((rows, LANES), F32))
    kernel = functools.partial(final_kernel, [len(i) for i in items], plan, scaled)
    return call(kernel, outs, [gain, *weights, *[a for i in items for a in i]], after=after)


def distance_buckets(bounds_ref, dist, buckets):
    size = jnp.abs(dist)
    half = jnp.zeros(dist.shape, jnp.int32)
    for b in range(bounds_ref.shape[0]):
        half += (size >= bounds_ref[b]).astype(jnp.int32)
    return half + jnp.where(dist > 0, buckets // 2, 0)


def bases_kernel(bounds_ref, table_ref, near_ref, far_ref):
    heads, _, width = near_ref.shape
    buckets = table_ref.shape[1]
    for ref, sign in ((near_ref, 1), (far_ref, -1)):
        dist = sign * (lax.broadcasted_iota(jnp.int32, (8, width), 1) - width // 2)
        marks = distance_buckets(bounds_ref, dist, buckets)
        marks = jnp.concatenate([marks] * (buckets // 8), 0)
        onehot = (marks == lax.broadcasted_iota(jnp.int32, (buckets, width), 0)).astype(F32)
        line = dot(table_ref[...], onehot.astype(BF))
        row = lax.broadcasted_iota(jnp.int32, (8, width), 0)
        for h in range(heads):
            field = jnp.broadcast_to(line[h : h + 1], (8, width))
            for k in (1, 2, 4):
                field = jnp.where((row & k) != 0, pltpu.roll(field, k, 1), field)
            while field.shape[0] < LANES:
                field = jnp.concatenate([field, pltpu.roll(field, field.shape[0], 1)], 0)
            ref[h] = field


def bias_bases(boundaries, table, heads, width):
    rows = jnp.zeros((8, table.shape[0]), table.dtype).at[: table.shape[1]].set(table.T)
    shape = out_of((heads, LANES, width), F32)
    return call(bases_kernel, [shape, shape], [boundaries, rows], ins=[SMEM, VMEM])


def bucket_field(bounds_ref, fields, buckets, first):
    width = fields[0].shape[-1]
    dist = width // 2 - lax.broadcasted_iota(jnp.int32, (8, width), 1)
    marks = distance_buckets(bounds_ref, dist, buckets)
    row = lax.broadcasted_iota(jnp.int32, (8, width), 0)
    line = jnp.zeros((8, width), F32)
    for h, field in enumerate(fields):
        while field.shape[0] > 8:
            half = field.shape[0] // 2
            field = field[:half] + pltpu.roll(field[half:], width - half, 1)
        for k in (4, 2, 1):
            field = jnp.where((row & k) != 0, pltpu.roll(field, width - k, 1), field)
        line = jnp.where(row == h, jnp.sum(field, 0, keepdims=True), line)
    lane = lax.broadcasted_iota(jnp.int32, (8, LANES), 1)
    out = jnp.zeros((8, LANES), F32)
    for b in range(buckets):
        total = jnp.sum(jnp.where(marks == b, line, 0.0), 1, keepdims=True)
        out = jnp.where(lane == first + b, total, out)
    return out


def split_low(values, lane, off, rest):
    high = values.astype(BF).astype(F32)
    mid = (values - high).astype(BF).astype(F32)
    low = values - high - mid
    return jnp.where(
        lane == off,
        high,
        jnp.where(lane == off + 1, mid, jnp.where(lane == off + 2, low, rest)),
    )


def three_ones(lane, off):
    return jnp.where((lane >= off) & (lane < off + 3), 1.0, 0.0)


def slots_of(batches):
    at = 0
    for b, (slots, length) in enumerate(batches):
        for s in range(slots):
            yield b, s, length, slice(at, at + length)
            at += length


def attend_kernel(batches, at, halves, *refs):
    places, lens = refs[0], refs[1 : 1 + len(batches)]
    refs = refs[1 + len(batches) :]
    normed_ref, near_ref = refs[:2]
    sources = refs[2 : 2 + halves]
    aug_ref, k_ref, v_ref, o_ref, w_scr, sem = refs[2 + halves :]
    width = near_ref.shape[-1]
    load(places, sources, w_scr, sem, pl.ds(at, 3 * LANES))
    for b, s, length, span in slots_of(batches):
        valid = lens[b][s]
        lane = lax.broadcasted_iota(jnp.int32, (length, LANES), 1)
        place = lax.broadcasted_iota(jnp.int32, (length, LANES), 0)
        masked = jnp.where(place >= valid, NEG, 0.0)
        qkv = dot(normed_ref[span, :], w_scr[...])
        q, k, v = (qkv[:, i * LANES : (i + 1) * LANES] for i in range(3))
        k_ref[span, :] = k.astype(BF)
        v_ref[span, :] = v.astype(BF)
        mixed = []
        for e in range(2):
            own = (lane >= DH) == (e == 1)
            off = DH * (1 - e)
            marker = jnp.where(lane == off + 3, 1.0, 0.0)
            q_own = jnp.where(own, q, marker).astype(BF)
            k_own = jnp.where(own, k, jnp.where(lane == off + 3, masked, 0.0)).astype(BF)
            v_own = jnp.where(own, v, 1.0).astype(BF)
            start = width // 2
            bias = [
                near_ref[e, :, start - a * LANES : start - a * LANES + length]
                for a in range(length // LANES)
            ]
            scores = dot_cols(q_own, k_own) + jnp.concatenate(bias, 0)
            top = jnp.max(scores, 1, keepdims=True)
            expo = jnp.exp(scores - top)
            sums = dot(expo.astype(BF), v_own)
            total = jnp.where(own, pltpu.roll(sums, DH, 1), sums)
            logsum = top + jnp.log(total)
            extra = split_low(-logsum, lane, off, marker)
            aug_ref[span, e * LANES : (e + 1) * LANES] = jnp.where(own, q, extra).astype(BF)
            mixed.append(sums / total)
        o_ref[span, :] = jnp.where(lane < DH, mixed[0], mixed[1]).astype(BF)


def pair_of(near, pair):
    return pl.BlockSpec((2,) + near.shape[1:], lambda i: (pair, 0, 0))


def attend(ring, batches, lens, normed, weights, at, near, pair, after=()):
    rows, width = normed.shape
    shapes = [out_of((rows, c * LANES), BF) for c in (2, 1, 1, 1)]
    return call(
        functools.partial(attend_kernel, batches, at, len(weights)),
        shapes,
        [ring.places, *lens, normed, near, *weights],
        ins=[SMEM] * (1 + len(lens)) + [fixed(normed), pair_of(near, pair)] + [ANY] * len(weights),
        out_specs=[fixed(s) for s in shapes],
        grid=(1,),
        scratch=[pltpu.VMEM((width, 3 * LANES), BF), pltpu.SemaphoreType.DMA((ring.dp,))],
        us=10,
        after=after,
    )


def attend_back_kernel(batches, *refs):
    lens = refs[: len(batches)]
    go_ref, aug_ref, k_ref, v_ref, o_ref, far_ref, grads_ref, gbase_ref = refs[len(batches) :]
    width = far_ref.shape[-1]
    gbase_ref[...] = jnp.zeros_like(gbase_ref)
    for b, s, length, span in slots_of(batches):
        valid = lens[b][s]
        lane = lax.broadcasted_iota(jnp.int32, (length, LANES), 1)
        place = lax.broadcasted_iota(jnp.int32, (length, LANES), 0)
        masked = jnp.where(place >= valid, NEG, 0.0)
        k = k_ref[span, :].astype(F32)
        v = v_ref[span, :].astype(F32)
        go = go_ref[span, :].astype(F32)
        both = go * o_ref[span, :].astype(F32)
        grads = []
        for e in range(2):
            own = (lane >= DH) == (e == 1)
            off = DH * (1 - e)
            q_own = aug_ref[span, e * LANES : (e + 1) * LANES]
            ones = three_ones(lane, off)
            k_own = jnp.where(own, k, jnp.where(lane == off + 3, masked, ones)).astype(BF)
            v_own = jnp.where(own, v, ones).astype(BF)
            delta = jnp.sum(jnp.where(own, both, 0.0), 1, keepdims=True)
            g_own = jnp.where(own, go, split_low(-delta, lane, off, 0.0)).astype(BF)
            cols = [
                slice(width // 2 - a * LANES, width // 2 - a * LANES + length)
                for a in range(length // LANES)
            ]
            bias = jnp.concatenate([far_ref[e, :, c] for c in cols], 0)
            probs = jnp.exp(dot_cols(k_own, q_own) + bias)
            ds = probs * dot_cols(v_own, g_own)
            for a, c in enumerate(cols):
                gbase_ref[e, :, c] += ds[a * LANES : (a + 1) * LANES]
            ds = ds.astype(BF)
            gv = dot(probs.astype(BF), g_own)
            grads.append((dot_rows(ds, k_own), dot(ds, q_own), gv))
        first = lane < DH
        for i, (a, b) in enumerate(zip(*grads)):
            grads_ref[span, i * LANES : (i + 1) * LANES] = jnp.where(first, a, b).astype(BF)


def attend_back(batches, lens, go, aug, k, v, o, far, pair, after=()):
    rows = go.shape[0]
    outs = [out_of((rows, 3 * LANES), BF), out_of((2,) + far.shape[1:], F32)]
    go_spec = pl.BlockSpec((rows, LANES), lambda i: (0, pair))
    return call(
        functools.partial(attend_back_kernel, batches),
        outs,
        [*lens, go, aug, k, v, o, far],
        ins=[SMEM] * len(lens) + [go_spec] + [fixed(a) for a in (aug, k, v, o)] + [pair_of(far, pair)],
        out_specs=[fixed(o) for o in outs],
        grid=(1,),
        us=10,
        after=after,
    )


def project_out_kernel(halves, pairs, at, places, *refs):
    o_refs, refs = refs[:pairs], refs[pairs:]
    sources, (attn_ref, w_scr, sem) = refs[:halves], refs[halves:]
    cols = pairs * LANES

    @pl.when(pl.program_id(0) == 0)
    def _():
        load(places, sources, w_scr, sem, pl.ds(at, cols))

    o = jnp.concatenate([r[...] for r in o_refs], 1)
    attn_ref[...] = dot_cols(o, w_scr[...]).astype(BF)


def project_out(ring, mixed, weights, at, width, tile=512, after=()):
    rows = mixed[0].shape[0]
    pairs = len(mixed)
    out = out_of((rows, width), BF)
    return call(
        functools.partial(project_out_kernel, len(weights), pairs, at),
        [out],
        [ring.places, *mixed, *weights],
        ins=[SMEM] + [tiles(m, tile) for m in mixed] + [ANY] * len(weights),
        out_specs=[tiles(out, tile)],
        grid=(rows // tile,),
        scratch=[pltpu.VMEM((width, pairs * LANES), BF), pltpu.SemaphoreType.DMA((ring.dp,))],
        us=6,
        after=after,
    )[0]


def rms_parts(field):
    scale = lax.rsqrt(jnp.mean(field * field, -1, keepdims=True) + EPS)
    return (scale, field * scale)


def norm_back(grad_unit, unit, scale):
    return scale * (grad_unit - unit * jnp.mean(grad_unit * unit, -1, keepdims=True))


def norm_kernel(count, short_ref, long_ref, unit_ref):
    unit_ref[...] = rms_parts(pick(count, short_ref, long_ref).astype(F32))[1].astype(BF)


def norm(xs, tile=512, after=()):
    out = out_of((xs[0].shape[0] + xs[1].shape[0], xs[0].shape[1]), BF)
    return call(
        functools.partial(norm_kernel, xs[0].shape[0] // tile),
        [out],
        xs,
        ins=pair_tiles(xs, tile),
        out_specs=[tiles(out, tile)],
        grid=(out.shape[0] // tile,),
        us=5,
        after=after,
    )[0]


def sum_of(refs):
    total = refs[0][...].astype(F32)
    for r in refs[1:]:
        total = total + r[...].astype(F32)
    return total


def add_kernel(count, addends, *refs):
    value = sum_of(refs[:addends]).astype(BF)

    @pl.when(pl.program_id(0) < count)
    def _():
        refs[-2][...] = value

    @pl.when(pl.program_id(0) >= count)
    def _():
        refs[-1][...] = value


def add_all(shapes, fields, tile=512, after=()):
    outs = [out_of(s, BF) for s in shapes]
    return call(
        functools.partial(add_kernel, shapes[0][0] // tile, len(fields)),
        outs,
        fields,
        ins=[tiles(f, tile) for f in fields],
        out_specs=pair_tiles(outs, tile),
        grid=((shapes[0][0] + shapes[1][0]) // tile,),
        us=5,
        after=after,
    )


def gelu_parts(x):
    c = 0.7978845608028654
    d = c * 0.044715
    square = x * x
    t = jnp.tanh(x * (c + d * square))
    half = 0.5 + 0.5 * t
    slope = half + (0.5 * x) * (1.0 - t * t) * (c + 3.0 * d * square)
    return x * half, slope


def ffn_first_kernel(halves, groups, emits, count, places, *refs):
    g_refs, x_refs, refs = refs[:2], refs[2:4], refs[4:]
    attn_refs, refs = refs[:groups], refs[groups:]
    sources, refs = refs[:halves], refs[halves:]
    unit_ref, scale_ref, out_ref, gn_ref = refs[:4]
    grads, (w_scr, total, sem) = refs[4 : 4 + emits], refs[4 + emits :]
    units = w_scr.shape[1] // 2
    step = pl.program_id(0)

    @pl.when(step == 0)
    def _():
        total[...] = jnp.zeros_like(total)
        load_all(places, sources, w_scr, sem, [(0, units), (0, units)])

    middle = pick(count, *x_refs).astype(F32) + sum_of(attn_refs)
    scale, unit = rms_parts(middle)
    unit = unit.astype(BF)
    unit_ref[...] = unit
    scale_ref[...] = jnp.broadcast_to(scale, scale_ref.shape)
    g = pick(count, *g_refs)
    win, wout = w_scr[:, :units], w_scr[:, units:]
    act, slope = gelu_parts(dot(unit, win))
    act = act.astype(BF)
    gpre = (dot(g, wout) * slope).astype(BF)
    lead = places[places.shape[0] - 1].astype(F32)
    out_ref[...] = dot_cols(act, wout) + lead * middle
    gn_ref[...] = dot_cols(gpre, win)
    total[:, :units] += dot_rows(unit, gpre)
    total[:, units:] += dot_rows(g, act)

    @pl.when(step == pl.num_programs(0) - 1)
    def _():
        if emits == 2:
            emit(places, total, *grads)
        else:
            grads[0][...] = total[...]


def ffn_first(ring, gs, xs, fields, weights, units, tile=512, after=()):
    rows, width = fields[0].shape
    unit, field = out_of((rows, width), BF), out_of((rows, width), F32)
    outs = [unit, out_of((rows, LANES), F32), field, field]
    grads = emitted(ring, width, 2 * units)
    return call(
        functools.partial(
            ffn_first_kernel, len(weights), len(fields), len(grads), xs[0].shape[0] // tile
        ),
        outs + grads,
        [ring.places, *gs, *xs, *fields, *weights],
        ins=[SMEM]
        + pair_tiles(gs, tile)
        + pair_tiles(xs, tile)
        + [tiles(a, tile) for a in fields]
        + [ANY] * len(weights),
        out_specs=[tiles(o, tile) for o in outs] + [fixed(o) for o in grads],
        grid=(rows // tile,),
        scratch=[
            pltpu.VMEM((width, 2 * units), BF),
            pltpu.VMEM((width, 2 * units), F32),
            pltpu.SemaphoreType.DMA((2, ring.dp)),
        ],
        us=25,
        after=after,
    )


def ffn_next_kernel(halves, count, places, unit_ref, scale_ref, *refs):
    g_refs, (out_in, gn_in), refs = refs[:2], refs[2:4], refs[4:]
    sources, refs = refs[:halves], refs[halves:]
    out_ref, mid_ref, act_ref, gpre_ref, w_scr, sem = refs
    units = w_scr.shape[1] // 2

    @pl.when(pl.program_id(0) == 0)
    def _():
        load(places, sources, w_scr, sem, pl.ds(0, 2 * units))

    win, wout = w_scr[:, :units], w_scr[:, units:]
    unit = unit_ref[...]
    g = pick(count, *g_refs)
    act, slope = gelu_parts(dot(unit, win))
    act = act.astype(BF)
    gpre = (dot(g, wout) * slope).astype(BF)
    act_ref[...] = act
    gpre_ref[...] = gpre
    out_ref[...] = (out_in[...] + dot_cols(act, wout)).astype(BF)
    lead = places[places.shape[0] - 1].astype(F32)
    back = norm_back(gn_in[...] + dot_cols(gpre, win), unit.astype(F32), scale_ref[:, :1])
    mid_ref[...] = (back + lead * g.astype(F32)).astype(BF)


def ffn_next(ring, unit, scale, gs, out, gn, weights, units, tile=512, after=()):
    rows, width = unit.shape
    outs = [out_of((rows, width), BF)] * 2 + [out_of((rows, units), BF)] * 2
    return call(
        functools.partial(ffn_next_kernel, len(weights), gs[0].shape[0] // tile),
        outs,
        [ring.places, unit, scale, *gs, out, gn, *weights],
        ins=[SMEM, tiles(unit, tile), tiles(scale, tile)]
        + pair_tiles(gs, tile)
        + [tiles(out, tile), tiles(gn, tile)]
        + [ANY] * len(weights),
        out_specs=[tiles(o, tile) for o in outs],
        grid=(rows // tile,),
        scratch=[pltpu.VMEM((width, 2 * units), BF), pltpu.SemaphoreType.DMA((ring.dp,))],
        us=17,
        after=after,
    )


def in_grad_kernel(unit_ref, gpre_ref, total_ref):
    part = dot_rows(unit_ref[...], gpre_ref[...])

    @pl.when(pl.program_id(0) == 0)
    def _():
        total_ref[...] = part

    @pl.when(pl.program_id(0) > 0)
    def _():
        total_ref[...] += part


def in_grad(unit, gpre, tile=1024, after=()):
    rows, width = unit.shape
    out = out_of((width, gpre.shape[1]), F32)
    return call(
        in_grad_kernel,
        [out],
        [unit, gpre],
        ins=[tiles(unit, tile), tiles(gpre, tile)],
        out_specs=[fixed(out)],
        grid=(rows // tile,),
        us=6,
        after=after,
    )[0]


def middle_kernel(halves, groups, pairs, emits, count, at, places, *refs):
    g_refs, mid_refs, refs = refs[:2], refs[2 : 2 + groups], refs[2 + groups :]
    act_ref, in_ref, refs = refs[0], refs[1], refs[2:]
    o_refs, refs = refs[:pairs], refs[pairs:]
    sources, refs = refs[:halves], refs[halves:]
    go_ref, grads, (w_scr, total, sem) = refs[0], refs[1 : 1 + emits], refs[1 + emits :]
    units = act_ref.shape[1]
    cols = pairs * LANES
    step = pl.program_id(0)

    @pl.when(step == 0)
    def _():
        total[:, units:] = jnp.zeros((total.shape[0], total.shape[1] - units), F32)
        total[:, :units] = in_ref[...]
        load(places, sources, w_scr, sem, pl.ds(at, cols))

    grad = sum_of(mid_refs).astype(BF)
    go_ref[...] = dot(grad, w_scr[...]).astype(BF)
    o = jnp.concatenate([r[...] for r in o_refs], 1)
    total[:, 2 * units :] += dot_rows(grad, o)
    total[:, units : 2 * units] += dot_rows(pick(count, *g_refs), act_ref[...])

    @pl.when(step == pl.num_programs(0) - 1)
    def _():
        if emits == 2:
            emit(places, total, *grads)
        else:
            grads[0][...] = total[...]


def middle_back(ring, gs, mids, act, grad_in, mixed, weights, at, tile=512, after=()):
    rows, width = mids[0].shape
    pairs = len(mixed)
    cols = pairs * LANES
    units = act.shape[1]
    go = out_of((rows, cols), BF)
    grads = emitted(ring, width, 2 * units + cols)
    return call(
        functools.partial(
            middle_kernel, len(weights), len(mids), pairs, len(grads), gs[0].shape[0] // tile, at
        ),
        [go] + grads,
        [ring.places, *gs, *mids, act, grad_in, *mixed, *weights],
        ins=[SMEM]
        + pair_tiles(gs, tile)
        + [tiles(a, tile) for a in (*mids, act)]
        + [fixed(grad_in)]
        + [tiles(a, tile) for a in mixed]
        + [ANY] * len(weights),
        out_specs=[tiles(go, tile)] + [fixed(g) for g in grads],
        grid=(rows // tile,),
        scratch=[
            pltpu.VMEM((width, cols), BF),
            pltpu.VMEM((width, 2 * units + cols), F32),
            pltpu.SemaphoreType.DMA((ring.dp,)),
        ],
        us=9,
        after=after,
    )


def input_back_kernel(plan, groups, pairs, count, places, short_ref, long_ref, *refs):
    mid_refs, refs = refs[:groups], refs[groups:]
    g_refs, refs = refs[:pairs], refs[pairs:]
    sources, (part_ref, w_scr, sem) = refs[:-3], refs[-3:]

    @pl.when(pl.program_id(0) == 0)
    def _():
        load_all(places, sources, w_scr, sem, plan)

    part = dot_cols(jnp.concatenate([r[...] for r in g_refs], 1), w_scr[...])
    scale, unit = rms_parts(pick(count, short_ref, long_ref).astype(F32))
    lead = places[places.shape[0] - 1].astype(F32)
    part_ref[...] = (norm_back(part, unit, scale) + lead * sum_of(mid_refs)).astype(BF)


def input_back(ring, xs, mids, grads, weights, plan, tile=512, after=()):
    rows, width = grads[0].shape[0], xs[0].shape[1]
    pairs = len(grads)
    out = out_of((rows, width), BF)
    return call(
        functools.partial(input_back_kernel, plan, len(mids), pairs, xs[0].shape[0] // tile),
        [out],
        [ring.places, *xs, *mids, *grads, *weights],
        ins=[SMEM]
        + pair_tiles(xs, tile)
        + [tiles(a, tile) for a in (*mids, *grads)]
        + [ANY] * len(weights),
        out_specs=[tiles(out, tile)],
        grid=(rows // tile,),
        scratch=[
            pltpu.VMEM((width, 3 * pairs * LANES), BF),
            pltpu.SemaphoreType.DMA((len(plan), ring.dp)),
        ],
        us=9,
        after=after,
    )[0]


def last_kernel(emits, pairs, buckets, places, bounds, unit_ref, *refs):
    g_refs, refs = refs[:pairs], refs[pairs:]
    bases, refs = refs[:pairs], refs[pairs:]
    grads, refs = refs[:emits], refs[emits:]
    table_ref, total = refs
    step = pl.program_id(0)
    cols = 3 * pairs * LANES

    @pl.when(step == 0)
    def _():
        total[...] = jnp.zeros_like(total)

    total[:, :cols] += dot_rows(unit_ref[...], jnp.concatenate([r[...] for r in g_refs], 1))

    @pl.when(step == pl.num_programs(0) - 1)
    def _():
        fields = [ref[e] for ref in bases for e in range(2)]
        table = bucket_field(bounds, fields, buckets, 0)
        table_ref[...] = table
        if emits == 2:
            rows = grads[0].shape[1]
            table = jnp.concatenate([table, jnp.zeros((rows - 8, LANES), F32)], 0)
            table = jnp.concatenate([jnp.zeros((rows, cols), F32), table], 1)
            emit(places, total, *grads, extra=table)
        else:
            grads[0][...] = total[...]


def last_grads(ring, boundaries, buckets, unit, grads, bases, tile=512, after=()):
    rows, width = unit.shape
    pairs = len(grads)
    cols = 3 * pairs * LANES + LANES
    outs = emitted(ring, width, cols)
    table = out_of((8, LANES), F32)
    *outs, table = call(
        functools.partial(last_kernel, len(outs), pairs, buckets),
        outs + [table],
        [ring.places, boundaries, unit, *grads, *bases],
        ins=[SMEM, SMEM, tiles(unit, tile)]
        + [tiles(a, tile) for a in grads]
        + [fixed(b) for b in bases],
        out_specs=[fixed(o) for o in outs] + [fixed(table)],
        grid=(rows // tile,),
        scratch=[pltpu.VMEM((width, cols), F32)],
        us=9,
        after=after,
    )
    share = width // ring.dp
    table = jnp.pad(table, ((0, share - 8), (cols - LANES, 0)))
    return halves(ring, outs, table)


def pad_cols(array, cols):
    return jnp.pad(array, ((0, 0), (0, cols - array.shape[1]))) if cols > array.shape[1] else array


def on_device(
    sizes,
    x_short,
    x_long,
    len_short,
    len_long,
    boundaries,
    q_weight,
    k_weight,
    v_weight,
    out_weight,
    in_weight,
    ff_out_weight,
    attn_gain,
    ffn_gain,
    bias_table,
    cot_short,
    cot_long,
):
    ring = Ring(sizes)
    quarter = ring.quarter
    width = x_short.shape[2]
    buckets, heads = bias_table.shape
    real = heads * DH
    cols = -(-real // LANES) * LANES
    pairs = cols // LANES
    units = in_weight.shape[1] // 2
    span = 2 * max(x_short.shape[1], x_long.shape[1])
    batches = [x.shape[:2] for x in (x_short, x_long)]
    lens = (len_short, len_long)

    xs = [x.reshape(-1, width) for x in (x_short, x_long)]
    gs = [g.reshape(-1, width) for g in (cot_short, cot_long)]

    col_a, col_f = (v.astype(F32)[:, None] for v in (attn_gain, ffn_gain))
    padded = [pad_cols(w, cols) for w in (q_weight, k_weight, v_weight, out_weight)]
    scaled = [(w.astype(F32) * col_a).astype(BF) for w in padded[:3]]
    pieces = [w[:, p * LANES : (p + 1) * LANES] for p in range(pairs) for w in scaled]
    own = jnp.concatenate(pieces + [padded[3]], 1)[None]
    win = (in_weight.astype(F32) * col_f).astype(BF)
    own1, own2 = (
        jnp.concatenate([w[:, at : at + units] for w in (win, ff_out_weight)], 1)[None]
        for at in (0, units)
    )

    step = 3 * LANES
    both = list(range(quarter))
    wide = own.shape[2]

    got = ring.far(own)
    near, far = bias_bases(boundaries, bias_table, cols // DH, span)
    held, own1 = join([own, *got], [(both, 0, wide)], after=[near], through=[own1])
    got = ring.first(held)
    got1 = ring.far(own1)
    unit = norm(xs, after=[held])
    head, rest = join([held, got], [((0, 1), 0, step), ((0, 1), step, wide)], after=[unit])
    qkv = blocks_of(ring, head, ring.last(head))
    rest = blocks_of(ring, rest, ring.last(rest))
    held1, own2 = join([own1, *got1], [(both, 0, 2 * units)], after=[head], through=[own2])
    got1 = ring.first(held1)
    got2 = ring.far(own2)

    fwd = []
    after = [held1]
    for p in range(pairs):
        weights, at = (rest, (p - 1) * step) if p else (qkv, 0)
        fwd.append(attend(ring, batches, lens, unit, weights, at, near, p, after=after))
        if p == 0:
            plan = [((0, 1), 0, units), ((0, 1), units, 2 * units)]
            helds = join([held1, got1], plan, after=[fwd[0][0]])
            gots = [ring.last(h) for h in helds]
            after = helds
        if p == min(1, pairs - 1):
            held2 = join([own2, *got2], [(both, 0, 2 * units)], after=[fwd[p][0]])[0]
            got2 = ring.first(held2)
            after = [held2]
    (held2,) = join([held2, got2], [((0, 1), 0, 2 * units)], after=[fwd[-1][0], *gots])
    got2 = ring.last(held2)
    mixed = [f[3] for f in fwd]
    out_at = (pairs - 1) * step
    attn = project_out(ring, mixed, rest, out_at, width, after=[held2])
    fields = [attn] + ring.exchange(attn)
    first = [b for h, g in zip(helds, gots) for b in blocks_of(ring, h, g)]
    second = blocks_of(ring, held2, got2)

    unit_f, scale, out, gn, *grad1 = ffn_first(ring, gs, xs, fields, first, units)
    keep1, send = halves(ring, grad1)
    got1 = ring.last(send)
    out, mid, act, gpre = ffn_next(ring, unit_f, scale, gs, out, gn, second, units)
    keep1, send, mid, out = fold((keep1, got1, 0), through=[mid, out])
    mids = [mid] + ring.exchange(mid)
    outs = [out] + ring.exchange(out)
    got1 = ring.first(send)
    grad_in = in_grad(unit_f, gpre, after=[keep1])
    go, *grad2 = middle_back(ring, gs, mids, act, grad_in, mixed, rest, out_at)
    keep2, send = halves(ring, grad2)
    got2 = ring.last(send)
    keep1, *sends = fold((keep1, got1, 1), after=[go])
    got1 = ring.far_all(sends)

    back = []
    after = [keep1]
    for p in range(pairs):
        aug, k, v, o = fwd[p]
        back.append(attend_back(batches, lens, go, aug, k, v, o, far, p, after=after))
        if p == min(1, pairs - 1):
            keep2, send = fold((keep2, got2, 0), after=[back[-1][0], *got1])
            got2 = ring.first(send)
            after = [keep2]
    keep2, *sends = fold((keep2, got2, 1), after=[back[-1][0]])
    got2 = ring.far_all(sends)

    grads = [b[0] for b in back]
    keep, send = last_grads(
        ring, boundaries, buckets, unit, grads, [b[1] for b in back], after=[keep2]
    )
    got = ring.last(send)
    plan = [(0, step), (0, (pairs - 1) * step)][: 2 if pairs > 1 else 1]
    weights = [*qkv, *rest][: len(plan) * len(qkv)]
    part = input_back(ring, xs, mids, grads, weights, plan, after=[keep])
    keep, send, part = fold((keep, got, 0), through=[part])
    got = ring.first(send)
    parts = [part] + ring.exchange(part)
    shapes = [x.shape for x in xs]
    ys = add_all(shapes, outs, after=[keep])
    keep, *sends = fold((keep, got, 1), after=[ys[0]])
    got = ring.far_all(sends)
    grad_xs = add_all(shapes, parts, after=[keep])
    plan = [
        [(0, 0, units), (1, 0, units)],
        [(0, units, 2 * units), (1, units, 2 * units)],
        [(1, 2 * units, 2 * units + cols)],
    ]
    grad_in, grad_ff, grad_o, gain_f = final(
        [[keep1, *got1], [keep2, *got2]], plan, [0], col_f, [in_weight], after=[keep]
    )
    plan = [
        [(0, p * step + i * LANES, p * step + (i + 1) * LANES) for p in range(pairs)]
        for i in range(3)
    ]
    plan.append([(0, pairs * step, pairs * step + LANES)])
    gq, gk, gv, table, gain_a = final([[keep, *got]], plan, [0, 1, 2], col_a, padded[:3])
    gain = jnp.stack([gain_a[:, 0], gain_f[:, 0]])
    for other in ring.exchange(gain):
        gain = gain + other
    return (
        ys[0].reshape(x_short.shape),
        ys[1].reshape(x_long.shape),
        grad_xs[0].reshape(x_short.shape),
        grad_xs[1].reshape(x_long.shape),
        gq[:, :real],
        gk[:, :real],
        gv[:, :real],
        grad_o[:, :real],
        grad_in,
        grad_ff,
        gain[0],
        gain[1],
        table[:heads, :buckets].T,
    )


def solution(mesh):
    sizes = (mesh.shape["dp"], mesh.shape["mp"])
    return jax.shard_map(
        functools.partial(on_device, sizes),
        mesh=mesh,
        in_specs=(
            P("dp", None, None),
            P("dp", None, None),
            P("dp"),
            P("dp"),
            P(),
            P("dp", "mp"),
            P("dp", "mp"),
            P("dp", "mp"),
            P("dp", "mp"),
            P("dp", "mp"),
            P("dp", "mp"),
            P("dp"),
            P("dp"),
            P(None, "mp"),
            P("dp", None, None),
            P("dp", None, None),
        ),
        out_specs=(
            P("dp", None, None),
            P("dp", None, None),
            P("dp", None, None),
            P("dp", None, None),
            P("dp", "mp"),
            P("dp", "mp"),
            P("dp", "mp"),
            P("dp", "mp"),
            P("dp", "mp"),
            P("dp", "mp"),
            P("dp"),
            P("dp"),
            P(None, "mp"),
        ),
        check_vma=False,
    )
```

```python
import functools

import jax
import jax.numpy as jnp
from jax import lax
from jax.experimental import pallas as pl
from jax.experimental.pallas import tpu as pltpu
from jax.sharding import PartitionSpec as P

DH = 64
LANES = 128
EPS = 1e-06
NEG = -1000000000.0
BF = jnp.bfloat16
F32 = jnp.float32
ANY = pl.BlockSpec(memory_space=pl.ANY)
SMEM = pl.BlockSpec(memory_space=pltpu.SMEM)
VMEM = pl.BlockSpec(memory_space=pltpu.VMEM)


def dot(left, right):
    return jnp.dot(left, right, preferred_element_type=F32)


def dot_rows(left, right):
    return lax.dot_general(left, right, (((0,), (0,)), ((), ())), preferred_element_type=F32)


def dot_cols(left, right):
    return lax.dot_general(left, right, (((1,), (1,)), ((), ())), preferred_element_type=F32)


def tiles(array, rows):
    return pl.BlockSpec((rows,) + array.shape[1:], lambda i: (i,) + (0,) * (array.ndim - 1))


def fixed(array):
    return pl.BlockSpec(array.shape, lambda i: (0,) * array.ndim)


def pair_tiles(pair, rows):
    count = pair[0].shape[0] // rows
    rest = (0,) * (pair[0].ndim - 1)
    shape = (rows,) + pair[0].shape[1:]
    return [
        pl.BlockSpec(shape, lambda i: (jnp.minimum(i, count - 1),) + rest),
        pl.BlockSpec(shape, lambda i: (jnp.maximum(i - count, 0),) + rest),
    ]


def pick(count, first, second):
    return jnp.where(pl.program_id(0) < count, first[...], second[...])


def out_of(shape, kind):
    return jax.ShapeDtypeStruct(tuple(shape), kind)


def call(kernel, outs, args, *, ins=None, out_specs=None, grid=None, scratch=(), us=0.001, mib=4, after=(), through=()):
    ins = list(ins or [VMEM] * len(args))
    out_specs = list(out_specs or [VMEM] * len(outs))
    extra = {} if grid is None else {"grid": grid}
    idle = len(after) + len(through)

    def body(*refs):
        given, made = refs[: len(args)], refs[len(args) + idle :]
        kernel(*given, *made[: len(outs)], *made[len(outs) + len(through) :])

    return pl.pallas_call(
        body,
        out_shape=list(outs) + [out_of(t.shape, t.dtype) for t in through],
        in_specs=ins + [ANY] * idle,
        out_specs=out_specs + [ANY] * len(through),
        scratch_shapes=list(scratch),
        compiler_params=pltpu.CompilerParams(vmem_limit_bytes=mib << 20),
        input_output_aliases={len(args) + len(after) + i: len(outs) + i for i in range(len(through))},
        cost_estimate=pl.CostEstimate(flops=int(us * 1e9), bytes_accessed=1000, transcendentals=0),
        **extra,
    )(*args, *after, *through)


class Ring:
    def __init__(self, sizes):
        self.dp, self.mp = sizes
        self.me = lax.axis_index("dp")
        self.odd = lax.axis_index("mp") & 1
        self.quarter = self.dp // 4
        j = jnp.arange(self.dp, dtype=jnp.int32)
        first = (j // self.quarter) & 1
        last = j // (2 * self.quarter)
        low = jnp.where(self.odd == 0, first + 2 * last, 2 * first + last)
        self.order = self.me ^ (4 * (j % self.quarter) + low)
        rel = self.me ^ j
        bit0, bit1 = rel & 1, (rel >> 1) & 1
        first, last = jnp.where(self.odd == 0, bit0, bit1), jnp.where(self.odd == 0, bit1, bit0)
        self.spots = (rel >> 2) + self.quarter * (first + 2 * last)
        lead = (lax.axis_index("mp") == 0).astype(jnp.int32)
        self.places = jnp.concatenate([self.order, lead[None]])

    def far(self, array):
        return [
            lax.ppermute(array, "dp", [(i, i ^ (4 * step)) for i in range(self.dp)])
            for step in range(1, self.quarter)
        ]

    def far_all(self, arrays):
        return [
            lax.ppermute(a, "dp", [(i, i ^ (4 * (step + 1))) for i in range(self.dp)])
            for step, a in enumerate(arrays)
        ]

    def near(self, array, masks):
        pairs = [
            (i * self.mp + c, (i ^ masks[c & 1]) * self.mp + c)
            for i in range(self.dp)
            for c in range(self.mp)
        ]
        return lax.ppermute(array, ("dp", "mp"), pairs)

    def first(self, array):
        return self.near(array, (1, 2))

    def last(self, array):
        return self.near(array, (2, 1))

    def exchange(self, array):
        return [
            lax.ppermute(array, "mp", [(i, i ^ k) for i in range(self.mp)])
            for k in range(1, self.mp)
        ]


def join_kernel(plan, *refs):
    sources, outs = refs[: -len(plan)], refs[-len(plan) :]
    for (chosen, start, stop), out in zip(plan, outs):
        at = 0
        for i in chosen:
            count = sources[i].shape[0]
            out[at : at + count] = sources[i][:, :, start:stop]
            at += count


def join(arrays, plan, after=(), through=()):
    outs = []
    for chosen, start, stop in plan:
        count = sum(arrays[i].shape[0] for i in chosen)
        outs.append(out_of((count, arrays[0].shape[1], stop - start), arrays[0].dtype))
    return call(functools.partial(join_kernel, plan), outs, arrays, after=after, through=through)


def aligned(rows):
    return rows % 16 == 0


def blocks_of(ring, held, got):
    if aligned(held.shape[1]):
        return (held, got)
    blocks = jnp.take(jnp.concatenate([held, got], 0), ring.spots, axis=0)
    return (blocks.reshape((-1,) + held.shape[2:]),)


def load_start(places, sources, to, sem, cols):
    copies = []
    if len(sources) == 2:
        half, rows, _ = sources[0].shape
        for j in range(2 * half):
            at = pl.multiple_of(places[j] * rows, 16)
            block = sources[j // half].at[j % half, :, cols]
            copies.append(pltpu.make_async_copy(block, to.at[pl.ds(at, rows)], sem.at[j]))
    else:
        copies.append(pltpu.make_async_copy(sources[0].at[:, cols], to, sem.at[0]))
    for c in copies:
        c.start()
    return copies


def load(places, sources, to, sem, cols):
    for c in load_start(places, sources, to, sem, cols):
        c.wait()


def load_all(places, refs, to, sem, plan):
    step = len(refs) // len(plan)
    copies = []
    to_at = 0
    for i, (at, count) in enumerate(plan):
        there = to.at[:, pl.ds(to_at, count)]
        copies += load_start(places, refs[i * step : (i + 1) * step], there, sem.at[i], pl.ds(at, count))
        to_at += count
    for c in copies:
        c.wait()


def emit(places, total, keep, send, extra=None):
    half, rows, _ = keep.shape
    for j in range(2 * half):
        at = pl.multiple_of(places[j] * rows, 16)
        block = total[pl.ds(at, rows), :]
        if extra is not None:
            block = block + extra
        if j < half:
            keep[j] = block
        else:
            send[j - half] = block.astype(BF)


def emitted(ring, rows, cols):
    share = rows // ring.dp
    if aligned(share):
        shape = (ring.dp // 2, share, cols)
        return [out_of(shape, F32), out_of(shape, BF)]
    return [out_of((rows, cols), F32)]


def halves(ring, outs, extra=None):
    if len(outs) == 2:
        return outs
    blocks = outs[0].reshape(ring.dp, -1, outs[0].shape[1])
    if extra is not None:
        blocks = blocks + extra
    blocks = jnp.take(blocks, ring.order, axis=0)
    return blocks[: ring.dp // 2], blocks[ring.dp // 2 :].astype(BF)


def fold_kernel(modes, *refs):
    ins, outs = refs[: 2 * len(modes)], refs[2 * len(modes) :]
    for mode in modes:
        keep, got = ins[:2]
        ins = ins[2:]
        count = got.shape[0] if mode else got.shape[0] // 2
        if mode:
            outs[0][...] = keep[0] + got[0].astype(F32)
            for j in range(1, count):
                outs[j][...] = (keep[j] + got[j].astype(F32)).astype(BF)
            outs = outs[count:]
        else:
            outs[0][...] = keep[:count] + got[:count].astype(F32)
            outs[1][...] = (keep[count:] + got[count:].astype(F32)).astype(BF)
            outs = outs[2:]


def fold(*items, after=(), through=()):
    outs = []
    args = []
    for keep, got, mode in items:
        args += [keep, got]
        if mode:
            shape = keep.shape[1:]
            outs += [out_of(shape, F32)] + [out_of(shape, BF)] * (keep.shape[0] - 1)
        else:
            shape = (keep.shape[0] // 2,) + keep.shape[1:]
            outs += [out_of(shape, F32), out_of(shape, BF)]
    kernel = functools.partial(fold_kernel, [m for *_, m in items])
    return call(kernel, outs, args, after=after, through=through)


def final_kernel(counts, plan, scaled, carried, gain_ref, *refs):
    carry, refs = refs[:carried], refs[carried:]
    weights, refs = refs[: len(scaled)], refs[len(scaled) :]
    fields = []
    for count in counts:
        total = refs[0][...]
        for r in refs[1:count]:
            total = total + r[...].astype(F32)
        fields.append(total)
        refs = refs[count:]
    outs, gain_out = refs[:-1], refs[-1]
    sums = jnp.zeros(gain_out.shape, F32)
    for i, (out, spans) in enumerate(zip(outs, plan)):
        at = 0
        for f, start, stop in spans:
            value = fields[f][:, start:stop]
            there = slice(at, at + stop - start)
            if i in scaled:
                kept = weights[scaled.index(i)][:, there].astype(F32)
                sums += jnp.sum(value * kept, 1, keepdims=True)
                value = value * gain_ref[...]
            out[:, there] = value
            at += stop - start
    if carried:
        lane = lax.broadcasted_iota(jnp.int32, sums.shape, 1)
        sums = jnp.where(lane == 0, sums, carry[0][...])
    gain_out[...] = sums


def final(items, plan, scaled, gain, weights, carry=(), after=()):
    rows = gain.shape[0]
    outs = [out_of((rows, sum(b - a for _, a, b in spans)), F32) for spans in plan]
    outs.append(out_of((rows, LANES), F32))
    kernel = functools.partial(final_kernel, [len(i) for i in items], plan, scaled, len(carry))
    args = [gain, *carry, *weights, *[a for i in items for a in i]]
    return call(kernel, outs, args, after=after)


def distance_buckets(bounds_ref, dist, buckets):
    size = jnp.abs(dist)
    half = jnp.zeros(dist.shape, jnp.int32)
    for b in range(bounds_ref.shape[0]):
        half += (size >= bounds_ref[b]).astype(jnp.int32)
    return half + jnp.where(dist > 0, buckets // 2, 0)


def bias_base(bounds_ref, table_ref, first, sign, to):
    width = to.shape[2]
    buckets = table_ref.shape[1]
    dist = sign * (lax.broadcasted_iota(jnp.int32, (8, width), 1) - width // 2)
    marks = distance_buckets(bounds_ref, dist, buckets)
    marks = jnp.concatenate([marks] * (buckets // 8), 0)
    onehot = (marks == lax.broadcasted_iota(jnp.int32, (buckets, width), 0)).astype(F32)
    line = dot(table_ref[...], onehot.astype(BF))
    row = lax.broadcasted_iota(jnp.int32, (8, width), 0)
    for e in range(2):
        field = jnp.broadcast_to(line[first + e : first + e + 1], (8, width))
        for k in (1, 2, 4):
            field = jnp.where((row & k) != 0, pltpu.roll(field, k, 1), field)
        while field.shape[0] < LANES:
            field = jnp.concatenate([field, pltpu.roll(field, field.shape[0], 1)], 0)
        to[e] = field


def bucket_field(bounds_ref, fields, buckets, first):
    width = fields[0].shape[-1]
    dist = width // 2 - lax.broadcasted_iota(jnp.int32, (8, width), 1)
    marks = distance_buckets(bounds_ref, dist, buckets)
    row = lax.broadcasted_iota(jnp.int32, (8, width), 0)
    line = jnp.zeros((8, width), F32)
    for h, field in enumerate(fields, first):
        while field.shape[0] > 8:
            half = field.shape[0] // 2
            field = field[:half] + pltpu.roll(field[half:], width - half, 1)
        for k in (4, 2, 1):
            field = jnp.where((row & k) != 0, pltpu.roll(field, width - k, 1), field)
        line = jnp.where(row == h, jnp.sum(field, 0, keepdims=True), line)
    lane = lax.broadcasted_iota(jnp.int32, (8, LANES), 1)
    out = jnp.zeros((8, LANES), F32)
    for b in range(buckets):
        total = jnp.sum(jnp.where(marks == b, line, 0.0), 1, keepdims=True)
        out = jnp.where(lane == b, total, out)
    return out


def split_low(values, lane, off, rest):
    high = values.astype(BF).astype(F32)
    mid = (values - high).astype(BF).astype(F32)
    low = values - high - mid
    return jnp.where(
        lane == off,
        high,
        jnp.where(lane == off + 1, mid, jnp.where(lane == off + 2, low, rest)),
    )


def three_ones(lane, off):
    return jnp.where((lane >= off) & (lane < off + 3), 1.0, 0.0)


def slots_of(batches):
    at = 0
    for b, (slots, length) in enumerate(batches):
        for s in range(slots):
            yield b, s, length, slice(at, at + length)
            at += length


def attend_kernel(batches, pair, at, halves, *refs):
    places, bounds, lens = refs[0], refs[1], refs[2 : 2 + len(batches)]
    refs = refs[2 + len(batches) :]
    normed_ref, table_ref = refs[:2]
    sources = refs[2 : 2 + halves]
    aug_ref, k_ref, v_ref, o_ref, w_scr, near_ref, sem = refs[2 + halves :]
    width = near_ref.shape[-1]
    copies = load_start(places, sources, w_scr, sem, pl.ds(at, 3 * LANES))
    bias_base(bounds, table_ref, 2 * pair, 1, near_ref)
    for c in copies:
        c.wait()
    for b, s, length, span in slots_of(batches):
        valid = lens[b][s]
        lane = lax.broadcasted_iota(jnp.int32, (length, LANES), 1)
        place = lax.broadcasted_iota(jnp.int32, (length, LANES), 0)
        masked = jnp.where(place >= valid, NEG, 0.0)
        qkv = dot(normed_ref[span, :], w_scr[...])
        q, k, v = (qkv[:, i * LANES : (i + 1) * LANES] for i in range(3))
        k_ref[span, :] = k.astype(BF)
        v_ref[span, :] = v.astype(BF)
        mixed = []
        for e in range(2):
            own = (lane >= DH) == (e == 1)
            off = DH * (1 - e)
            marker = jnp.where(lane == off + 3, 1.0, 0.0)
            q_own = jnp.where(own, q, marker).astype(BF)
            k_own = jnp.where(own, k, jnp.where(lane == off + 3, masked, 0.0)).astype(BF)
            v_own = jnp.where(own, v, 1.0).astype(BF)
            start = width // 2
            bias = [
                near_ref[e, :, start - a * LANES : start - a * LANES + length]
                for a in range(length // LANES)
            ]
            scores = dot_cols(q_own, k_own) + jnp.concatenate(bias, 0)
            top = jnp.max(scores, 1, keepdims=True)
            expo = jnp.exp(scores - top)
            sums = dot(expo.astype(BF), v_own)
            total = jnp.where(own, pltpu.roll(sums, DH, 1), sums)
            logsum = top + jnp.log(total)
            extra = split_low(-logsum, lane, off, marker)
            aug_ref[span, e * LANES : (e + 1) * LANES] = jnp.where(own, q, extra).astype(BF)
            mixed.append(sums / total)
        o_ref[span, :] = jnp.where(lane < DH, mixed[0], mixed[1]).astype(BF)


def attend(ring, batches, lens, boundaries, table, unit, weights, at, pair, after=()):
    rows, width = unit.shape
    shapes = [out_of((rows, c * LANES), BF) for c in (2, 1, 1, 1)]
    span = 2 * max(length for _, length in batches)
    return call(
        functools.partial(attend_kernel, batches, pair, at, len(weights)),
        shapes,
        [ring.places, boundaries, *lens, unit, table, *weights],
        ins=[SMEM] * (2 + len(lens)) + [fixed(unit), fixed(table)] + [ANY] * len(weights),
        out_specs=[fixed(s) for s in shapes],
        grid=(1,),
        scratch=[
            pltpu.VMEM((width, 3 * LANES), BF),
            pltpu.VMEM((2, LANES, span), F32),
            pltpu.SemaphoreType.DMA((ring.dp,)),
        ],
        us=10,
        mib=16,
        after=after,
    )


def attend_back_kernel(batches, pair, priors, emits, *refs):
    lens, refs = refs[: len(batches)], refs[len(batches) :]
    bounds, places, unit_ref, go_ref, aug_ref, k_ref, v_ref, o_ref, bias_ref = refs[:9]
    totals, (table_in, grads_ref, table_ref) = refs[9 : 9 + priors], refs[9 + priors : 12 + priors]
    outs, (far_ref, gbase_ref, total) = refs[12 + priors : -3], refs[-3:]
    width = far_ref.shape[-1]
    bias_base(bounds, bias_ref, 2 * pair, -1, far_ref)
    gbase_ref[...] = jnp.zeros_like(gbase_ref)
    for b, s, length, span in slots_of(batches):
        valid = lens[b][s]
        lane = lax.broadcasted_iota(jnp.int32, (length, LANES), 1)
        place = lax.broadcasted_iota(jnp.int32, (length, LANES), 0)
        masked = jnp.where(place >= valid, NEG, 0.0)
        k = k_ref[span, :].astype(F32)
        v = v_ref[span, :].astype(F32)
        go = go_ref[span, :].astype(F32)
        both = go * o_ref[span, :].astype(F32)
        grads = []
        for e in range(2):
            own = (lane >= DH) == (e == 1)
            off = DH * (1 - e)
            q_own = aug_ref[span, e * LANES : (e + 1) * LANES]
            ones = three_ones(lane, off)
            k_own = jnp.where(own, k, jnp.where(lane == off + 3, masked, ones)).astype(BF)
            v_own = jnp.where(own, v, ones).astype(BF)
            delta = jnp.sum(jnp.where(own, both, 0.0), 1, keepdims=True)
            g_own = jnp.where(own, go, split_low(-delta, lane, off, 0.0)).astype(BF)
            cols = [
                slice(width // 2 - a * LANES, width // 2 - a * LANES + length)
                for a in range(length // LANES)
            ]
            bias = jnp.concatenate([far_ref[e, :, c] for c in cols], 0)
            probs = jnp.exp(dot_cols(k_own, q_own) + bias)
            ds = probs * dot_cols(v_own, g_own)
            for a, c in enumerate(cols):
                gbase_ref[e, :, c] += ds[a * LANES : (a + 1) * LANES]
            ds = ds.astype(BF)
            gv = dot(probs.astype(BF), g_own)
            grads.append((dot_rows(ds, k_own), dot(ds, q_own), gv))
        first = lane < DH
        for i, (a, b) in enumerate(zip(*grads)):
            grads_ref[span, i * LANES : (i + 1) * LANES] = jnp.where(first, a, b).astype(BF)
    table = table_in[...] + bucket_field(
        bounds, [gbase_ref[0], gbase_ref[1]], bias_ref.shape[1], 2 * pair
    )
    table_ref[...] = table
    part = dot_rows(unit_ref[...], grads_ref[...])
    if not emits:
        outs[0][...] = part
        return
    step = 3 * LANES
    for i, ref in enumerate(totals):
        total[:, i * step : (i + 1) * step] = ref[...]
    at = priors * step
    total[:, at : at + step] = part
    extra = None
    if total.shape[1] > at + step:
        total[:, at + step :] = jnp.zeros((total.shape[0], LANES), F32)
        rows = outs[0].shape[1]
        extra = jnp.concatenate([table, jnp.zeros((rows - 8, LANES), F32)], 0) if emits == 2 else None
        extra = jnp.concatenate([jnp.zeros((rows, at + step), F32), extra], 1) if emits == 2 else None
    if emits == 2:
        emit(places, total, *outs, extra=extra)
    else:
        outs[0][...] = total[...]


def attend_back(
    ring, batches, lens, boundaries, bias, unit, go, fwd, pair, table, priors, last, after=()
):
    rows, width = unit.shape
    step = 3 * LANES
    span = 2 * max(length for _, length in batches)
    go_spec = pl.BlockSpec((rows, LANES), lambda i: (0, pair))
    cols = step * (1 + len(priors)) + LANES if last else step
    outs = [out_of((rows, step), BF), out_of((8, LANES), F32)]
    made = emitted(ring, width, cols) if last else [out_of((width, step), F32)]
    emits = len(made) if last else 0
    grads, table, *made = call(
        functools.partial(attend_back_kernel, batches, pair, len(priors), emits),
        outs + made,
        [*lens, boundaries, ring.places, unit, go, *fwd, bias, *priors, table],
        ins=[SMEM] * (len(lens) + 2)
        + [fixed(unit), go_spec]
        + [fixed(a) for a in (*fwd, bias, *priors, table)],
        out_specs=[fixed(o) for o in outs + made],
        grid=(1,),
        scratch=[
            pltpu.VMEM((2, LANES, span), F32),
            pltpu.VMEM((2, LANES, span), F32),
            pltpu.VMEM((width, cols) if last else (8, LANES), F32),
        ],
        us=10,
        mib=20,
        after=after,
    )
    if last:
        share = width // ring.dp
        made = halves(ring, made, jnp.pad(table, ((0, share - 8), (cols - LANES, 0))))
    return grads, table, made


def project_out_kernel(halves, pairs, at, places, *refs):
    o_refs, refs = refs[:pairs], refs[pairs:]
    sources, (attn_ref, w_scr, sem) = refs[:halves], refs[halves:]
    cols = pairs * LANES

    @pl.when(pl.program_id(0) == 0)
    def _():
        load(places, sources, w_scr, sem, pl.ds(at, cols))

    o = jnp.concatenate([r[...] for r in o_refs], 1)
    attn_ref[...] = dot_cols(o, w_scr[...]).astype(BF)


def project_out(ring, mixed, weights, at, width, tile=512, after=()):
    rows = mixed[0].shape[0]
    pairs = len(mixed)
    out = out_of((rows, width), BF)
    return call(
        functools.partial(project_out_kernel, len(weights), pairs, at),
        [out],
        [ring.places, *mixed, *weights],
        ins=[SMEM] + [tiles(m, tile) for m in mixed] + [ANY] * len(weights),
        out_specs=[tiles(out, tile)],
        grid=(rows // tile,),
        scratch=[pltpu.VMEM((width, pairs * LANES), BF), pltpu.SemaphoreType.DMA((ring.dp,))],
        us=6,
        mib=10,
        after=after,
    )[0]


def rms_parts(field):
    scale = lax.rsqrt(jnp.mean(field * field, -1, keepdims=True) + EPS)
    return (scale, field * scale)


def norm_back(grad_unit, unit, scale):
    return scale * (grad_unit - unit * jnp.mean(grad_unit * unit, -1, keepdims=True))


def norm_kernel(count, short_ref, long_ref, unit_ref):
    unit_ref[...] = rms_parts(pick(count, short_ref, long_ref).astype(F32))[1].astype(BF)


def norm(xs, tile=512, after=()):
    out = out_of((xs[0].shape[0] + xs[1].shape[0], xs[0].shape[1]), BF)
    return call(
        functools.partial(norm_kernel, xs[0].shape[0] // tile),
        [out],
        xs,
        ins=pair_tiles(xs, tile),
        out_specs=[tiles(out, tile)],
        grid=(out.shape[0] // tile,),
        us=5,
        mib=8,
        after=after,
    )[0]


def sum_of(refs):
    total = refs[0][...].astype(F32)
    for r in refs[1:]:
        total = total + r[...].astype(F32)
    return total


def add_kernel(count, addends, *refs):
    value = sum_of(refs[:addends]).astype(BF)

    @pl.when(pl.program_id(0) < count)
    def _():
        refs[-2][...] = value

    @pl.when(pl.program_id(0) >= count)
    def _():
        refs[-1][...] = value


def add_all(shapes, fields, tile=512, after=()):
    outs = [out_of(s, BF) for s in shapes]
    return call(
        functools.partial(add_kernel, shapes[0][0] // tile, len(fields)),
        outs,
        fields,
        ins=[tiles(f, tile) for f in fields],
        out_specs=pair_tiles(outs, tile),
        grid=((shapes[0][0] + shapes[1][0]) // tile,),
        after=after,
    )


def gelu_parts(x):
    c = 0.7978845608028654
    d = c * 0.044715
    square = x * x
    t = jnp.tanh(x * (c + d * square))
    half = 0.5 + 0.5 * t
    slope = half + (0.5 * x) * (1.0 - t * t) * (c + 3.0 * d * square)
    return x * half, slope


def ffn_first_kernel(halves, groups, emits, count, places, *refs):
    g_refs, x_refs, refs = refs[:2], refs[2:4], refs[4:]
    attn_refs, refs = refs[:groups], refs[groups:]
    sources, refs = refs[:halves], refs[halves:]
    unit_ref, scale_ref, out_ref, gn_ref = refs[:4]
    grads, (w_scr, total, sem) = refs[4 : 4 + emits], refs[4 + emits :]
    units = w_scr.shape[1] // 2
    step = pl.program_id(0)

    @pl.when(step == 0)
    def _():
        total[...] = jnp.zeros_like(total)
        load_all(places, sources, w_scr, sem, [(0, units), (0, units)])

    middle = pick(count, *x_refs).astype(F32) + sum_of(attn_refs)
    scale, unit = rms_parts(middle)
    unit = unit.astype(BF)
    unit_ref[...] = unit
    scale_ref[...] = jnp.broadcast_to(scale, scale_ref.shape)
    g = pick(count, *g_refs)
    win, wout = w_scr[:, :units], w_scr[:, units:]
    act, slope = gelu_parts(dot(unit, win))
    act = act.astype(BF)
    gpre = (dot(g, wout) * slope).astype(BF)
    lead = places[places.shape[0] - 1].astype(F32)
    out_ref[...] = dot_cols(act, wout) + lead * middle
    gn_ref[...] = dot_cols(gpre, win)
    total[:, :units] += dot_rows(unit, gpre)
    total[:, units:] += dot_rows(g, act)

    @pl.when(step == pl.num_programs(0) - 1)
    def _():
        if emits == 2:
            emit(places, total, *grads)
        else:
            grads[0][...] = total[...]


def ffn_first(ring, gs, xs, fields, weights, units, tile=512, after=()):
    rows, width = fields[0].shape
    unit, field = out_of((rows, width), BF), out_of((rows, width), F32)
    outs = [unit, out_of((rows, LANES), F32), field, field]
    grads = emitted(ring, width, 2 * units)
    return call(
        functools.partial(
            ffn_first_kernel, len(weights), len(fields), len(grads), xs[0].shape[0] // tile
        ),
        outs + grads,
        [ring.places, *gs, *xs, *fields, *weights],
        ins=[SMEM]
        + pair_tiles(gs, tile)
        + pair_tiles(xs, tile)
        + [tiles(a, tile) for a in fields]
        + [ANY] * len(weights),
        out_specs=[tiles(o, tile) for o in outs] + [fixed(o) for o in grads],
        grid=(rows // tile,),
        scratch=[
            pltpu.VMEM((width, 2 * units), BF),
            pltpu.VMEM((width, 2 * units), F32),
            pltpu.SemaphoreType.DMA((2, ring.dp)),
        ],
        us=25,
        mib=40,
        after=after,
    )


def ffn_next_kernel(halves, count, places, unit_ref, scale_ref, *refs):
    g_refs, (out_in, gn_in), refs = refs[:2], refs[2:4], refs[4:]
    sources, refs = refs[:halves], refs[halves:]
    out_ref, mid_ref, act_ref, gpre_ref, w_scr, sem = refs
    units = w_scr.shape[1] // 2

    @pl.when(pl.program_id(0) == 0)
    def _():
        load(places, sources, w_scr, sem, pl.ds(0, 2 * units))

    win, wout = w_scr[:, :units], w_scr[:, units:]
    unit = unit_ref[...]
    g = pick(count, *g_refs)
    act, slope = gelu_parts(dot(unit, win))
    act = act.astype(BF)
    gpre = (dot(g, wout) * slope).astype(BF)
    act_ref[...] = act
    gpre_ref[...] = gpre
    out_ref[...] = (out_in[...] + dot_cols(act, wout)).astype(BF)
    lead = places[places.shape[0] - 1].astype(F32)
    back = norm_back(gn_in[...] + dot_cols(gpre, win), unit.astype(F32), scale_ref[:, :1])
    mid_ref[...] = (back + lead * g.astype(F32)).astype(BF)


def ffn_next(ring, unit, scale, gs, out, gn, weights, units, tile=512, after=()):
    rows, width = unit.shape
    outs = [out_of((rows, width), BF)] * 2 + [out_of((rows, units), BF)] * 2
    return call(
        functools.partial(ffn_next_kernel, len(weights), gs[0].shape[0] // tile),
        outs,
        [ring.places, unit, scale, *gs, out, gn, *weights],
        ins=[SMEM, tiles(unit, tile), tiles(scale, tile)]
        + pair_tiles(gs, tile)
        + [tiles(out, tile), tiles(gn, tile)]
        + [ANY] * len(weights),
        out_specs=[tiles(o, tile) for o in outs],
        grid=(rows // tile,),
        scratch=[pltpu.VMEM((width, 2 * units), BF), pltpu.SemaphoreType.DMA((ring.dp,))],
        us=17,
        mib=36,
        after=after,
    )


def in_grad_kernel(unit_ref, gpre_ref, total_ref):
    part = dot_rows(unit_ref[...], gpre_ref[...])

    @pl.when(pl.program_id(0) == 0)
    def _():
        total_ref[...] = part

    @pl.when(pl.program_id(0) > 0)
    def _():
        total_ref[...] += part


def in_grad(unit, gpre, tile=1024, after=()):
    rows, width = unit.shape
    out = out_of((width, gpre.shape[1]), F32)
    return call(
        in_grad_kernel,
        [out],
        [unit, gpre],
        ins=[tiles(unit, tile), tiles(gpre, tile)],
        out_specs=[fixed(out)],
        grid=(rows // tile,),
        us=6,
        mib=16,
        after=after,
    )[0]


def middle_kernel(halves, groups, pairs, emits, count, at, places, *refs):
    g_refs, mid_refs, refs = refs[:2], refs[2 : 2 + groups], refs[2 + groups :]
    act_ref, in_ref, refs = refs[0], refs[1], refs[2:]
    o_refs, refs = refs[:pairs], refs[pairs:]
    sources, refs = refs[:halves], refs[halves:]
    go_ref, grads, (w_scr, total, sem) = refs[0], refs[1 : 1 + emits], refs[1 + emits :]
    units = act_ref.shape[1]
    cols = pairs * LANES
    step = pl.program_id(0)

    @pl.when(step == 0)
    def _():
        total[:, units:] = jnp.zeros((total.shape[0], total.shape[1] - units), F32)
        total[:, :units] = in_ref[...]
        load(places, sources, w_scr, sem, pl.ds(at, cols))

    grad = sum_of(mid_refs).astype(BF)
    go_ref[...] = dot(grad, w_scr[...]).astype(BF)
    o = jnp.concatenate([r[...] for r in o_refs], 1)
    total[:, 2 * units :] += dot_rows(grad, o)
    total[:, units : 2 * units] += dot_rows(pick(count, *g_refs), act_ref[...])

    @pl.when(step == pl.num_programs(0) - 1)
    def _():
        if emits == 2:
            emit(places, total, *grads)
        else:
            grads[0][...] = total[...]


def middle_back(ring, gs, mids, act, grad_in, mixed, weights, at, tile=512, after=()):
    rows, width = mids[0].shape
    pairs = len(mixed)
    cols = pairs * LANES
    units = act.shape[1]
    go = out_of((rows, cols), BF)
    grads = emitted(ring, width, 2 * units + cols)
    return call(
        functools.partial(
            middle_kernel, len(weights), len(mids), pairs, len(grads), gs[0].shape[0] // tile, at
        ),
        [go] + grads,
        [ring.places, *gs, *mids, act, grad_in, *mixed, *weights],
        ins=[SMEM]
        + pair_tiles(gs, tile)
        + [tiles(a, tile) for a in (*mids, act)]
        + [fixed(grad_in)]
        + [tiles(a, tile) for a in mixed]
        + [ANY] * len(weights),
        out_specs=[tiles(go, tile)] + [fixed(g) for g in grads],
        grid=(rows // tile,),
        scratch=[
            pltpu.VMEM((width, cols), BF),
            pltpu.VMEM((width, 2 * units + cols), F32),
            pltpu.SemaphoreType.DMA((ring.dp,)),
        ],
        us=9,
        mib=28,
        after=after,
    )


def input_back_kernel(plan, groups, pairs, count, places, short_ref, long_ref, *refs):
    mid_refs, refs = refs[:groups], refs[groups:]
    g_refs, refs = refs[:pairs], refs[pairs:]
    sources, (part_ref, w_scr, sem) = refs[:-3], refs[-3:]

    @pl.when(pl.program_id(0) == 0)
    def _():
        load_all(places, sources, w_scr, sem, plan)

    part = dot_cols(jnp.concatenate([r[...] for r in g_refs], 1), w_scr[...])
    scale, unit = rms_parts(pick(count, short_ref, long_ref).astype(F32))
    lead = places[places.shape[0] - 1].astype(F32)
    part_ref[...] = (norm_back(part, unit, scale) + lead * sum_of(mid_refs)).astype(BF)


def input_back(ring, xs, mids, grads, weights, plan, tile=512, after=()):
    rows, width = grads[0].shape[0], xs[0].shape[1]
    pairs = len(grads)
    out = out_of((rows, width), BF)
    return call(
        functools.partial(input_back_kernel, plan, len(mids), pairs, xs[0].shape[0] // tile),
        [out],
        [ring.places, *xs, *mids, *grads, *weights],
        ins=[SMEM]
        + pair_tiles(xs, tile)
        + [tiles(a, tile) for a in (*mids, *grads)]
        + [ANY] * len(weights),
        out_specs=[tiles(out, tile)],
        grid=(rows // tile,),
        scratch=[
            pltpu.VMEM((width, 3 * pairs * LANES), BF),
            pltpu.SemaphoreType.DMA((len(plan), ring.dp)),
        ],
        mib=20,
        after=after,
    )[0]


def pad_cols(array, cols):
    return jnp.pad(array, ((0, 0), (0, cols - array.shape[1]))) if cols > array.shape[1] else array


def on_device(
    sizes,
    x_short,
    x_long,
    len_short,
    len_long,
    boundaries,
    q_weight,
    k_weight,
    v_weight,
    out_weight,
    in_weight,
    ff_out_weight,
    attn_gain,
    ffn_gain,
    bias_table,
    cot_short,
    cot_long,
):
    ring = Ring(sizes)
    quarter = ring.quarter
    width = x_short.shape[2]
    buckets, heads = bias_table.shape
    real = heads * DH
    cols = -(-real // LANES) * LANES
    pairs = cols // LANES
    units = in_weight.shape[1] // 2
    batches = [x.shape[:2] for x in (x_short, x_long)]
    lens = (len_short, len_long)

    xs = [x.reshape(-1, width) for x in (x_short, x_long)]
    gs = [g.reshape(-1, width) for g in (cot_short, cot_long)]

    col_a, col_f = (v.astype(F32)[:, None] for v in (attn_gain, ffn_gain))
    padded = [pad_cols(w, cols) for w in (q_weight, k_weight, v_weight, out_weight)]
    scaled = [(w.astype(F32) * col_a).astype(BF) for w in padded[:3]]
    pieces = [[w[:, p * LANES : (p + 1) * LANES] for w in scaled] for p in range(pairs)]
    own = jnp.concatenate([w for piece in pieces for w in piece] + [padded[3]], 1)[None]
    win = (in_weight.astype(F32) * col_f).astype(BF)
    own1, own2 = (
        jnp.concatenate([w[:, at : at + units] for w in (win, ff_out_weight)], 1)[None]
        for at in (0, units)
    )
    step = 3 * LANES
    z = tuple(range(quarter))
    table = jnp.pad(bias_table.T, ((0, 8 - heads), (0, 0)))

    two = (0, 1)
    wide = own.shape[2]
    got = ring.far(own)
    held, own1 = join([own, *got], [(z, 0, wide)], through=[own1])
    got = ring.first(held)
    got1 = ring.far(own1)
    unit = norm(xs, after=[held])
    cuts = [i * step for i in range(pairs)] + [wide]
    plan = [(two, a, b) for a, b in zip(cuts, cuts[1:])]
    *helds, own2 = join([held, got], plan, after=[unit], through=[own2])
    qkvo = [blocks_of(ring, h, ring.last(h)) for h in helds]

    fwd = []
    after = helds
    half = [(two, 0, units), (two, units, 2 * units)]
    for p in range(pairs):
        fwd.append(
            attend(ring, batches, lens, boundaries, table, unit, qkvo[p], 0, p, after=after)
        )
        if p == 0:
            held1, own2 = join(
                [own1, *got1], [(z, 0, 2 * units)], after=[fwd[0][0]], through=[own2]
            )
            got1 = ring.first(held1)
            got2 = ring.far(own2)
            after = [held1]
        if p == min(1, pairs - 1):
            z2 = tuple(2 + i for i in z)
            *helds, held2 = join(
                [held1, got1, own2, *got2], half + [(z2, 0, 2 * units)], after=[fwd[p][0]]
            )
            gots = [ring.last(h) for h in helds]
            got2 = ring.first(held2)
            after = [held2]
    mixed = [f[3] for f in fwd]
    out_w, out_at = qkvo[-1], step
    attn = project_out(ring, mixed, out_w, out_at, width, after=[got2, *gots])
    fields = [attn] + ring.exchange(attn)
    (held2,) = join([held2, got2], [(two, 0, 2 * units)], after=[attn])
    got2 = ring.last(held2)
    first = [b for h, g in zip(helds, gots) for b in blocks_of(ring, h, g)]
    second = blocks_of(ring, held2, got2)

    unit_f, scale, out, gn, *grad1 = ffn_first(
        ring, gs, xs, fields, first, units, after=[held2]
    )
    keep1, send = halves(ring, grad1)
    got1 = ring.last(send)
    out, mid, act, gpre = ffn_next(ring, unit_f, scale, gs, out, gn, second, units)
    keep1, send, mid, out = fold((keep1, got1, 0), through=[mid, out])
    mids = [mid] + ring.exchange(mid)
    outs = [out] + ring.exchange(out)
    got1 = ring.first(send)
    grad_in = in_grad(unit_f, gpre, after=[keep1])
    go, *grad2 = middle_back(ring, gs, mids, act, grad_in, mixed, out_w, out_at)
    keep2, send = halves(ring, grad2)
    got2 = ring.last(send)
    keep1, *sends = fold((keep1, got1, 1), after=[go])
    got1 = ring.far_all(sends)

    grads = []
    priors = []
    sums = jnp.zeros((8, LANES), F32)
    after = [keep1]
    for p in range(pairs):
        end = p == pairs - 1
        g, sums, made = attend_back(
            ring, batches, lens, boundaries, table, unit, go, fwd[p], p, sums, priors if end else (), end,
            after=after,
        )
        grads.append(g)
        if not end:
            priors.append(made[0])
        if p == min(1, pairs - 1):
            keep2, send = fold((keep2, got2, 0), after=[g, *got1])
            got2 = ring.first(send)
            after = [keep2]
    keep, send = made
    keep2, *sends, send = fold((keep2, got2, 1), through=[send])
    got = ring.last(send)
    got2 = ring.far_all(sends)
    plan = [(0, step)] * pairs
    weights = [w for piece in qkvo for w in piece]
    part = input_back(ring, xs, mids, grads, weights, plan, after=[keep2])
    rows = [slice(0, xs[0].shape[0]), slice(xs[0].shape[0], None)]

    def sums_of(fields):
        return [sum(f[r].astype(F32) for f in fields).astype(BF) for r in rows]

    keep, send, part, *outs = fold((keep, got, 0), through=[part, *outs])
    got = ring.first(send)
    parts = [part] + ring.exchange(part)
    ys = sums_of(outs)
    keep, *sends, part = fold((keep, got, 1), after=ys, through=[parts[0]])
    last = [keep, *ring.far_all(sends)]
    grad_xs = sums_of([part] + parts[1:])
    plan = [
        [(0, 0, units), (1, 0, units)],
        [(0, units, 2 * units), (1, units, 2 * units)],
        [(1, 2 * units, 2 * units + cols)],
    ]
    grad_in, grad_ff, grad_o, gain_f = final(
        [[keep1, *got1], [keep2, *got2]], plan, [0], col_f, [in_weight], after=grad_xs
    )
    plan = [
        [(0, p * step + i * LANES, p * step + (i + 1) * LANES) for p in range(pairs)]
        for i in range(3)
    ]
    plan.append([(0, pairs * step, pairs * step + LANES)])
    gq, gk, gv, sums, gain = final([last], plan, [0, 1, 2], col_a, padded[:3], carry=[gain_f])
    for other in ring.exchange(gain):
        gain = gain + other
    return (
        ys[0].reshape(x_short.shape),
        ys[1].reshape(x_long.shape),
        grad_xs[0].reshape(x_short.shape),
        grad_xs[1].reshape(x_long.shape),
        gq[:, :real],
        gk[:, :real],
        gv[:, :real],
        grad_o[:, :real],
        grad_in,
        grad_ff,
        gain[:, 0],
        gain[:, 1],
        sums[:heads, :buckets].T,
    )


def solution(mesh):
    sizes = (mesh.shape["dp"], mesh.shape["mp"])
    return jax.shard_map(
        functools.partial(on_device, sizes),
        mesh=mesh,
        in_specs=(
            P("dp", None, None),
            P("dp", None, None),
            P("dp"),
            P("dp"),
            P(),
            P("dp", "mp"),
            P("dp", "mp"),
            P("dp", "mp"),
            P("dp", "mp"),
            P("dp", "mp"),
            P("dp", "mp"),
            P("dp"),
            P("dp"),
            P(None, "mp"),
            P("dp", None, None),
            P("dp", None, None),
        ),
        out_specs=(
            P("dp", None, None),
            P("dp", None, None),
            P("dp", None, None),
            P("dp", None, None),
            P("dp", "mp"),
            P("dp", "mp"),
            P("dp", "mp"),
            P("dp", "mp"),
            P("dp", "mp"),
            P("dp", "mp"),
            P("dp"),
            P("dp"),
            P(None, "mp"),
        ),
        check_vma=False,
    )
```

```python
import functools

import jax
import jax.numpy as jnp
from jax import lax
from jax.experimental import pallas as pl
from jax.experimental.pallas import tpu as pltpu
from jax.sharding import PartitionSpec as P

DH = 64
LANES = 128
EPS = 1e-06
NEG = -1000000000.0
BF = jnp.bfloat16
F32 = jnp.float32
ANY = pl.BlockSpec(memory_space=pl.ANY)
HBM = pl.BlockSpec(memory_space=pltpu.HBM)
SMEM = pl.BlockSpec(memory_space=pltpu.SMEM)
VMEM = pl.BlockSpec(memory_space=pltpu.VMEM)


def dot(left, right):
    return jnp.dot(left, right, preferred_element_type=F32)


def dot_rows(left, right):
    return lax.dot_general(left, right, (((0,), (0,)), ((), ())), preferred_element_type=F32)


def dot_cols(left, right):
    return lax.dot_general(left, right, (((1,), (1,)), ((), ())), preferred_element_type=F32)


def tiles(array, rows):
    return pl.BlockSpec((rows,) + array.shape[1:], lambda i: (i,) + (0,) * (array.ndim - 1))


def fixed(array):
    return pl.BlockSpec(array.shape, lambda i: (0,) * array.ndim)


def pair_tiles(pair, rows):
    count = pair[0].shape[0] // rows
    rest = (0,) * (pair[0].ndim - 1)
    shape = (rows,) + pair[0].shape[1:]
    return [
        pl.BlockSpec(shape, lambda i: (jnp.minimum(i, count - 1),) + rest),
        pl.BlockSpec(shape, lambda i: (jnp.maximum(i - count, 0),) + rest),
    ]


def pick(count, first, second):
    return jnp.where(pl.program_id(0) < count, first[...], second[...])


def out_of(shape, kind):
    return jax.ShapeDtypeStruct(tuple(shape), kind)


def call(kernel, outs, args, *, ins=None, out_specs=None, grid=None, scratch=(), us=0.001, mib=4, after=(), through=()):
    ins = list(ins or [VMEM] * len(args))
    out_specs = list(out_specs or [VMEM] * len(outs))
    extra = {} if grid is None else {"grid": grid}
    idle = len(after) + len(through)

    def body(*refs):
        given, made = refs[: len(args)], refs[len(args) + idle :]
        kernel(*given, *made[: len(outs)], *made[len(outs) + len(through) :])

    return pl.pallas_call(
        body,
        out_shape=list(outs) + [out_of(t.shape, t.dtype) for t in through],
        in_specs=ins + [ANY] * idle,
        out_specs=out_specs + [ANY] * len(through),
        scratch_shapes=list(scratch),
        compiler_params=pltpu.CompilerParams(vmem_limit_bytes=mib << 20),
        input_output_aliases={len(args) + len(after) + i: len(outs) + i for i in range(len(through))},
        cost_estimate=pl.CostEstimate(flops=int(us * 1e9), bytes_accessed=1000, transcendentals=0),
        **extra,
    )(*args, *after, *through)


class Ring:
    def __init__(self, sizes):
        self.dp, self.mp = sizes
        self.me = lax.axis_index("dp")
        self.odd = lax.axis_index("mp") & 1
        self.quarter = self.dp // 4
        j = jnp.arange(self.dp, dtype=jnp.int32)
        first = (j // self.quarter) & 1
        last = j // (2 * self.quarter)
        low = jnp.where(self.odd == 0, first + 2 * last, 2 * first + last)
        self.order = self.me ^ (4 * (j % self.quarter) + low)
        rel = self.me ^ j
        bit0, bit1 = rel & 1, (rel >> 1) & 1
        first, last = jnp.where(self.odd == 0, bit0, bit1), jnp.where(self.odd == 0, bit1, bit0)
        self.spots = (rel >> 2) + self.quarter * (first + 2 * last)
        lead = (lax.axis_index("mp") == 0).astype(jnp.int32)
        self.places = jnp.concatenate([self.order, lead[None]])

    def far(self, array):
        return [
            lax.ppermute(array, "dp", [(i, i ^ (4 * step)) for i in range(self.dp)])
            for step in range(1, self.quarter)
        ]

    def far_all(self, arrays):
        return [
            lax.ppermute(a, "dp", [(i, i ^ (4 * (step + 1))) for i in range(self.dp)])
            for step, a in enumerate(arrays)
        ]

    def near(self, array, masks):
        pairs = [
            (i * self.mp + c, (i ^ masks[c & 1]) * self.mp + c)
            for i in range(self.dp)
            for c in range(self.mp)
        ]
        return lax.ppermute(array, ("dp", "mp"), pairs)

    def first(self, array):
        return self.near(array, (1, 2))

    def last(self, array):
        return self.near(array, (2, 1))

    def exchange(self, array):
        return [
            lax.ppermute(array, "mp", [(i, i ^ k) for i in range(self.mp)])
            for k in range(1, self.mp)
        ]


def join_kernel(plan, *refs):
    sources, outs = refs[: -len(plan)], refs[-len(plan) :]
    for (chosen, start, stop), out in zip(plan, outs):
        at = 0
        for i in chosen:
            count = sources[i].shape[0]
            out[at : at + count] = sources[i][:, :, start:stop]
            at += count


def join(arrays, plan, after=(), through=()):
    outs = []
    for chosen, start, stop in plan:
        count = sum(arrays[i].shape[0] for i in chosen)
        outs.append(out_of((count, arrays[0].shape[1], stop - start), arrays[0].dtype))
    return call(functools.partial(join_kernel, plan), outs, arrays, after=after, through=through)


def aligned(rows):
    return rows % 16 == 0


def blocks_of(ring, held, got):
    if aligned(held.shape[1]):
        return (held, got)
    blocks = jnp.take(jnp.concatenate([held, got], 0), ring.spots, axis=0)
    return (blocks.reshape((-1,) + held.shape[2:]),)


def load_start(places, sources, to, sem, cols):
    copies = []
    if len(sources) == 2:
        half, rows, _ = sources[0].shape
        for j in range(2 * half):
            at = pl.multiple_of(places[j] * rows, 16)
            block = sources[j // half].at[j % half, :, cols]
            copies.append(pltpu.make_async_copy(block, to.at[pl.ds(at, rows)], sem.at[j]))
    else:
        copies.append(pltpu.make_async_copy(sources[0].at[:, cols], to, sem.at[0]))
    for c in copies:
        c.start()
    return copies


def load(places, sources, to, sem, cols):
    for c in load_start(places, sources, to, sem, cols):
        c.wait()


def load_all(places, refs, to, sem, plan):
    step = len(refs) // len(plan)
    copies = []
    to_at = 0
    for i, (at, count) in enumerate(plan):
        there = to.at[:, pl.ds(to_at, count)]
        copies += load_start(places, refs[i * step : (i + 1) * step], there, sem.at[i], pl.ds(at, count))
        to_at += count
    for c in copies:
        c.wait()


def emit(places, total, keep, send, extra=None):
    half, rows, _ = keep.shape
    for j in range(2 * half):
        at = pl.multiple_of(places[j] * rows, 16)
        block = total[pl.ds(at, rows), :]
        if extra is not None:
            block = block + extra
        if j < half:
            keep[j] = block
        else:
            send[j - half] = block.astype(BF)


def emitted(ring, rows, cols):
    share = rows // ring.dp
    if aligned(share):
        shape = (ring.dp // 2, share, cols)
        return [out_of(shape, F32), out_of(shape, BF)]
    return [out_of((rows, cols), F32)]


def halves(ring, outs, extra=None):
    if len(outs) == 2:
        return outs
    blocks = outs[0].reshape(ring.dp, -1, outs[0].shape[1])
    if extra is not None:
        blocks = blocks + extra
    blocks = jnp.take(blocks, ring.order, axis=0)
    return blocks[: ring.dp // 2], blocks[ring.dp // 2 :].astype(BF)


def fold_kernel(modes, *refs):
    ins, outs = refs[: 2 * len(modes)], refs[2 * len(modes) :]
    for mode in modes:
        keep, got = ins[:2]
        ins = ins[2:]
        count = got.shape[0] if mode else got.shape[0] // 2
        if mode:
            outs[0][...] = keep[0] + got[0].astype(F32)
            for j in range(1, count):
                outs[j][...] = (keep[j] + got[j].astype(F32)).astype(BF)
            outs = outs[count:]
        else:
            outs[0][...] = keep[:count] + got[:count].astype(F32)
            outs[1][...] = (keep[count:] + got[count:].astype(F32)).astype(BF)
            outs = outs[2:]


def fold(*items, after=(), through=()):
    outs = []
    args = []
    for keep, got, mode in items:
        args += [keep, got]
        if mode:
            shape = keep.shape[1:]
            outs += [out_of(shape, F32)] + [out_of(shape, BF)] * (keep.shape[0] - 1)
        else:
            shape = (keep.shape[0] // 2,) + keep.shape[1:]
            outs += [out_of(shape, F32), out_of(shape, BF)]
    kernel = functools.partial(fold_kernel, [m for *_, m in items])
    return call(kernel, outs, args, after=after, through=through)


def final_kernel(counts, plan, scaled, carried, gain_ref, *refs):
    carry, refs = refs[:carried], refs[carried:]
    weights, refs = refs[: len(scaled)], refs[len(scaled) :]
    fields = []
    for count in counts:
        total = refs[0][...]
        for r in refs[1:count]:
            total = total + r[...].astype(F32)
        fields.append(total)
        refs = refs[count:]
    outs, gain_out = refs[:-1], refs[-1]
    sums = jnp.zeros(gain_out.shape, F32)
    for i, (out, spans) in enumerate(zip(outs, plan)):
        at = 0
        for f, start, stop in spans:
            value = fields[f][:, start:stop]
            there = slice(at, at + stop - start)
            if i in scaled:
                kept = weights[scaled.index(i)][:, there].astype(F32)
                sums += jnp.sum(value * kept, 1, keepdims=True)
                value = value * gain_ref[...]
            out[:, there] = value
            at += stop - start
    if carried:
        lane = lax.broadcasted_iota(jnp.int32, sums.shape, 1)
        sums = jnp.where(lane == 0, sums, carry[0][...])
    gain_out[...] = sums


def final(items, plan, scaled, gain, weights, carry=(), after=()):
    rows = gain.shape[0]
    outs = [out_of((rows, sum(b - a for _, a, b in spans)), F32) for spans in plan]
    outs.append(out_of((rows, LANES), F32))
    kernel = functools.partial(final_kernel, [len(i) for i in items], plan, scaled, len(carry))
    args = [gain, *carry, *weights, *[a for i in items for a in i]]
    return call(kernel, outs, args, after=after)


def distance_buckets(bounds_ref, dist, buckets):
    size = jnp.abs(dist)
    half = jnp.zeros(dist.shape, jnp.int32)
    for b in range(bounds_ref.shape[0]):
        half += (size >= bounds_ref[b]).astype(jnp.int32)
    return half + jnp.where(dist > 0, buckets // 2, 0)


def bias_base(bounds_ref, table_ref, first, sign, to):
    width = to.shape[2]
    buckets = table_ref.shape[1]
    dist = sign * (lax.broadcasted_iota(jnp.int32, (8, width), 1) - width // 2)
    marks = distance_buckets(bounds_ref, dist, buckets)
    marks = jnp.concatenate([marks] * (buckets // 8), 0)
    onehot = (marks == lax.broadcasted_iota(jnp.int32, (buckets, width), 0)).astype(F32)
    line = dot(table_ref[...], onehot.astype(BF))
    row = lax.broadcasted_iota(jnp.int32, (8, width), 0)
    for e in range(2):
        field = jnp.broadcast_to(line[first + e : first + e + 1], (8, width))
        for k in (1, 2, 4):
            field = jnp.where((row & k) != 0, pltpu.roll(field, k, 1), field)
        while field.shape[0] < LANES:
            field = jnp.concatenate([field, pltpu.roll(field, field.shape[0], 1)], 0)
        to[e] = field


def bucket_field(bounds_ref, fields, buckets, first):
    width = fields[0].shape[-1]
    dist = width // 2 - lax.broadcasted_iota(jnp.int32, (8, width), 1)
    marks = distance_buckets(bounds_ref, dist, buckets)
    row = lax.broadcasted_iota(jnp.int32, (8, width), 0)
    line = jnp.zeros((8, width), F32)
    for h, field in enumerate(fields, first):
        while field.shape[0] > 8:
            half = field.shape[0] // 2
            field = field[:half] + pltpu.roll(field[half:], width - half, 1)
        for k in (4, 2, 1):
            field = jnp.where((row & k) != 0, pltpu.roll(field, width - k, 1), field)
        line = jnp.where(row == h, jnp.sum(field, 0, keepdims=True), line)
    lane = lax.broadcasted_iota(jnp.int32, (8, LANES), 1)
    out = jnp.zeros((8, LANES), F32)
    for b in range(buckets):
        total = jnp.sum(jnp.where(marks == b, line, 0.0), 1, keepdims=True)
        out = jnp.where(lane == b, total, out)
    return out


def split_low(values, lane, off, rest):
    high = values.astype(BF).astype(F32)
    mid = (values - high).astype(BF).astype(F32)
    low = values - high - mid
    return jnp.where(
        lane == off,
        high,
        jnp.where(lane == off + 1, mid, jnp.where(lane == off + 2, low, rest)),
    )


def three_ones(lane, off):
    return jnp.where((lane >= off) & (lane < off + 3), 1.0, 0.0)


def slots_of(batches):
    at = 0
    for b, (slots, length) in enumerate(batches):
        for s in range(slots):
            yield b, s, length, slice(at, at + length)
            at += length


def attend_kernel(batches, pair, at, halves, *refs):
    places, bounds, lens = refs[0], refs[1], refs[2 : 2 + len(batches)]
    refs = refs[2 + len(batches) :]
    normed_ref, table_ref = refs[:2]
    sources = refs[2 : 2 + halves]
    aug_ref, k_ref, v_ref, o_ref, w_scr, near_ref, sem = refs[2 + halves :]
    width = near_ref.shape[-1]
    copies = load_start(places, sources, w_scr, sem, pl.ds(at, 3 * LANES))
    bias_base(bounds, table_ref, 2 * pair, 1, near_ref)
    for c in copies:
        c.wait()
    for b, s, length, span in slots_of(batches):
        valid = lens[b][s]
        lane = lax.broadcasted_iota(jnp.int32, (length, LANES), 1)
        place = lax.broadcasted_iota(jnp.int32, (length, LANES), 0)
        masked = jnp.where(place >= valid, NEG, 0.0)
        qkv = dot(normed_ref[span, :], w_scr[...])
        q, k, v = (qkv[:, i * LANES : (i + 1) * LANES] for i in range(3))
        k_ref[span, :] = k.astype(BF)
        v_ref[span, :] = v.astype(BF)
        mixed = []
        for e in range(2):
            own = (lane >= DH) == (e == 1)
            off = DH * (1 - e)
            marker = jnp.where(lane == off + 3, 1.0, 0.0)
            q_own = jnp.where(own, q, marker).astype(BF)
            k_own = jnp.where(own, k, jnp.where(lane == off + 3, masked, 0.0)).astype(BF)
            v_own = jnp.where(own, v, 1.0).astype(BF)
            start = width // 2
            bias = [
                near_ref[e, :, start - a * LANES : start - a * LANES + length]
                for a in range(length // LANES)
            ]
            scores = dot_cols(q_own, k_own) + jnp.concatenate(bias, 0)
            top = jnp.max(scores, 1, keepdims=True)
            expo = jnp.exp(scores - top)
            sums = dot(expo.astype(BF), v_own)
            total = jnp.where(own, pltpu.roll(sums, DH, 1), sums)
            logsum = top + jnp.log(total)
            extra = split_low(-logsum, lane, off, marker)
            aug_ref[span, e * LANES : (e + 1) * LANES] = jnp.where(own, q, extra).astype(BF)
            mixed.append(sums / total)
        o_ref[span, :] = jnp.where(lane < DH, mixed[0], mixed[1]).astype(BF)


def attend(ring, batches, lens, boundaries, table, unit, weights, at, pair, after=()):
    rows, width = unit.shape
    shapes = [out_of((rows, c * LANES), BF) for c in (2, 1, 1, 1)]
    span = 2 * max(length for _, length in batches)
    return call(
        functools.partial(attend_kernel, batches, pair, at, len(weights)),
        shapes,
        [ring.places, boundaries, *lens, unit, table, *weights],
        ins=[SMEM] * (2 + len(lens)) + [fixed(unit), fixed(table)] + [HBM] * len(weights),
        out_specs=[fixed(s) for s in shapes],
        grid=(1,),
        scratch=[
            pltpu.VMEM((width, 3 * LANES), BF),
            pltpu.VMEM((2, LANES, span), F32),
            pltpu.SemaphoreType.DMA((ring.dp,)),
        ],
        mib=16,
        after=after,
    )


def attend_back_kernel(batches, pair, before, priors, emits, *refs):
    lens, refs = refs[: len(batches)], refs[len(batches) :]
    bounds, places, unit_ref, go_ref, aug_ref, k_ref, v_ref, o_ref, bias_ref = refs[:9]
    totals, (table_in, grads_ref, table_ref) = refs[9 : 9 + priors], refs[9 + priors : 12 + priors]
    outs, (far_ref, gbase_ref, total) = refs[12 + priors : -3], refs[-3:]
    width = far_ref.shape[-1]
    bias_base(bounds, bias_ref, 2 * pair, -1, far_ref)
    gbase_ref[...] = jnp.zeros_like(gbase_ref)
    for b, s, length, span in slots_of(batches):
        valid = lens[b][s]
        lane = lax.broadcasted_iota(jnp.int32, (length, LANES), 1)
        place = lax.broadcasted_iota(jnp.int32, (length, LANES), 0)
        masked = jnp.where(place >= valid, NEG, 0.0)
        k = k_ref[span, :].astype(F32)
        v = v_ref[span, :].astype(F32)
        go = go_ref[span, :].astype(F32)
        both = go * o_ref[span, :].astype(F32)
        grads = []
        for e in range(2):
            own = (lane >= DH) == (e == 1)
            off = DH * (1 - e)
            q_own = aug_ref[span, e * LANES : (e + 1) * LANES]
            ones = three_ones(lane, off)
            k_own = jnp.where(own, k, jnp.where(lane == off + 3, masked, ones)).astype(BF)
            v_own = jnp.where(own, v, ones).astype(BF)
            delta = jnp.sum(jnp.where(own, both, 0.0), 1, keepdims=True)
            g_own = jnp.where(own, go, split_low(-delta, lane, off, 0.0)).astype(BF)
            cols = [
                slice(width // 2 - a * LANES, width // 2 - a * LANES + length)
                for a in range(length // LANES)
            ]
            bias = jnp.concatenate([far_ref[e, :, c] for c in cols], 0)
            probs = jnp.exp(dot_cols(k_own, q_own) + bias)
            ds = probs * dot_cols(v_own, g_own)
            for a, c in enumerate(cols):
                gbase_ref[e, :, c] += ds[a * LANES : (a + 1) * LANES]
            ds = ds.astype(BF)
            gv = dot(probs.astype(BF), g_own)
            grads.append((dot_rows(ds, k_own), dot(ds, q_own), gv))
        first = lane < DH
        for i, (a, b) in enumerate(zip(*grads)):
            grads_ref[span, i * LANES : (i + 1) * LANES] = jnp.where(first, a, b).astype(BF)
    table = table_in[...] + bucket_field(
        bounds, [gbase_ref[0], gbase_ref[1]], bias_ref.shape[1], 2 * pair
    )
    table_ref[...] = table
    part = dot_rows(unit_ref[...], grads_ref[...])
    if not emits:
        outs[0][...] = part
        return
    step = 3 * LANES
    at = 0
    for value in [r[...] for r in totals[:before]] + [part] + [r[...] for r in totals[before:]]:
        total[:, at : at + value.shape[1]] = value
        at += value.shape[1]
    extra = None
    if total.shape[1] > at:
        total[:, at:] = jnp.zeros((total.shape[0], LANES), F32)
    if total.shape[1] > at and emits == 2:
        rows = outs[0].shape[1]
        extra = jnp.concatenate([table, jnp.zeros((rows - 8, LANES), F32)], 0)
        extra = jnp.concatenate([jnp.zeros((rows, at), F32), extra], 1)
    if emits == 2:
        emit(places, total, *outs, extra=extra)
    else:
        outs[0][...] = total[...]


def attend_back(
    ring, batches, lens, boundaries, bias, unit, go, fwd, pair, table, before, rest, last, after=()
):
    rows, width = unit.shape
    step = 3 * LANES
    span = 2 * max(length for _, length in batches)
    go_spec = pl.BlockSpec((rows, LANES), lambda i: (0, pair))
    given = rest is None
    priors = [] if given else [*before, *rest]
    cols = step + sum(p.shape[1] for p in priors) + (LANES if last else 0)
    outs = [out_of((rows, step), BF), out_of((8, LANES), F32)]
    made = [out_of((width, step), F32)] if given else emitted(ring, width, cols)
    emits = 0 if given else len(made)
    kernel = functools.partial(attend_back_kernel, batches, pair, len(before), len(priors), emits)
    grads, table, *made = call(
        kernel,
        outs + made,
        [*lens, boundaries, ring.places, unit, go, *fwd, bias, *priors, table],
        ins=[SMEM] * (len(lens) + 2)
        + [fixed(unit), go_spec]
        + [fixed(a) for a in (*fwd, bias, *priors, table)],
        out_specs=[fixed(o) for o in outs + made],
        grid=(1,),
        scratch=[
            pltpu.VMEM((2, LANES, span), F32),
            pltpu.VMEM((2, LANES, span), F32),
            pltpu.VMEM((8, LANES) if given else (width, cols), F32),
        ],
        mib=24,
        after=after,
    )
    if not given:
        share = width // ring.dp
        extra = jnp.pad(table, ((0, share - 8), (cols - LANES, 0))) if last else None
        made = halves(ring, made, extra)
    return grads, table, made


def project_out_kernel(halves, pairs, at, places, *refs):
    o_refs, refs = refs[:pairs], refs[pairs:]
    sources, (attn_ref, w_scr, sem) = refs[:halves], refs[halves:]
    cols = pairs * LANES

    @pl.when(pl.program_id(0) == 0)
    def _():
        load(places, sources, w_scr, sem, pl.ds(at, cols))

    o = jnp.concatenate([r[...] for r in o_refs], 1)
    attn_ref[...] = dot_cols(o, w_scr[...]).astype(BF)


def project_out(ring, mixed, weights, at, width, tile=512, after=()):
    rows = mixed[0].shape[0]
    pairs = len(mixed)
    out = out_of((rows, width), BF)
    return call(
        functools.partial(project_out_kernel, len(weights), pairs, at),
        [out],
        [ring.places, *mixed, *weights],
        ins=[SMEM] + [tiles(m, tile) for m in mixed] + [HBM] * len(weights),
        out_specs=[tiles(out, tile)],
        grid=(rows // tile,),
        scratch=[pltpu.VMEM((width, pairs * LANES), BF), pltpu.SemaphoreType.DMA((ring.dp,))],
        mib=10,
        after=after,
    )[0]


def rms_parts(field):
    scale = lax.rsqrt(jnp.mean(field * field, -1, keepdims=True) + EPS)
    return (scale, field * scale)


def norm_back(grad_unit, unit, scale):
    return scale * (grad_unit - unit * jnp.mean(grad_unit * unit, -1, keepdims=True))


def norm_kernel(count, short_ref, long_ref, unit_ref):
    unit_ref[...] = rms_parts(pick(count, short_ref, long_ref).astype(F32))[1].astype(BF)


def norm(xs, tile=512, after=()):
    out = out_of((xs[0].shape[0] + xs[1].shape[0], xs[0].shape[1]), BF)
    return call(
        functools.partial(norm_kernel, xs[0].shape[0] // tile),
        [out],
        xs,
        ins=pair_tiles(xs, tile),
        out_specs=[tiles(out, tile)],
        grid=(out.shape[0] // tile,),
        mib=8,
        after=after,
    )[0]


def sum_of(refs):
    total = refs[0][...].astype(F32)
    for r in refs[1:]:
        total = total + r[...].astype(F32)
    return total


def add_kernel(count, addends, *refs):
    value = sum_of(refs[:addends]).astype(BF)

    @pl.when(pl.program_id(0) < count)
    def _():
        refs[-2][...] = value

    @pl.when(pl.program_id(0) >= count)
    def _():
        refs[-1][...] = value


def add_all(shapes, fields, tile=512, after=()):
    outs = [out_of(s, BF) for s in shapes]
    return call(
        functools.partial(add_kernel, shapes[0][0] // tile, len(fields)),
        outs,
        fields,
        ins=[tiles(f, tile) for f in fields],
        out_specs=pair_tiles(outs, tile),
        grid=((shapes[0][0] + shapes[1][0]) // tile,),
        after=after,
    )


def gelu_parts(x):
    c = 0.7978845608028654
    d = c * 0.044715
    square = x * x
    t = jnp.tanh(x * (c + d * square))
    half = 0.5 + 0.5 * t
    slope = half + (0.5 * x) * (1.0 - t * t) * (c + 3.0 * d * square)
    return x * half, slope


def ffn_first_kernel(halves, groups, emits, count, places, *refs):
    g_refs, x_refs, refs = refs[:2], refs[2:4], refs[4:]
    attn_refs, refs = refs[:groups], refs[groups:]
    sources, refs = refs[:halves], refs[halves:]
    unit_ref, scale_ref, out_ref, gn_ref = refs[:4]
    grads, (w_scr, total, sem) = refs[4 : 4 + emits], refs[4 + emits :]
    units = w_scr.shape[1] // 2
    step = pl.program_id(0)

    @pl.when(step == 0)
    def _():
        total[...] = jnp.zeros_like(total)
        load_all(places, sources, w_scr, sem, [(0, 2 * units)])

    middle = pick(count, *x_refs).astype(F32) + sum_of(attn_refs)
    scale, unit = rms_parts(middle)
    unit = unit.astype(BF)
    unit_ref[...] = unit
    scale_ref[...] = jnp.broadcast_to(scale, scale_ref.shape)
    g = pick(count, *g_refs)
    win, wout = w_scr[:, :units], w_scr[:, units:]
    act, slope = gelu_parts(dot(unit, win))
    act = act.astype(BF)
    gpre = (dot(g, wout) * slope).astype(BF)
    lead = places[places.shape[0] - 1].astype(F32)
    out_ref[...] = (dot_cols(act, wout) + lead * middle).astype(BF)
    gn_ref[...] = dot_cols(gpre, win).astype(BF)
    total[:, :units] += dot_rows(unit, gpre)
    total[:, units:] += dot_rows(g, act)

    @pl.when(step == pl.num_programs(0) - 1)
    def _():
        if emits == 2:
            emit(places, total, *grads)
        else:
            grads[0][...] = total[...]


def ffn_first(ring, gs, xs, fields, weights, units, tile=512, after=()):
    rows, width = fields[0].shape
    field = out_of((rows, width), BF)
    outs = [field, out_of((rows, LANES), F32), field, field]
    grads = emitted(ring, width, 2 * units)
    return call(
        functools.partial(
            ffn_first_kernel, len(weights), len(fields), len(grads), xs[0].shape[0] // tile
        ),
        outs + grads,
        [ring.places, *gs, *xs, *fields, *weights],
        ins=[SMEM]
        + pair_tiles(gs, tile)
        + pair_tiles(xs, tile)
        + [tiles(a, tile) for a in fields]
        + [HBM] * len(weights),
        out_specs=[tiles(o, tile) for o in outs] + [fixed(o) for o in grads],
        grid=(rows // tile,),
        scratch=[
            pltpu.VMEM((width, 2 * units), BF),
            pltpu.VMEM((width, 2 * units), F32),
            pltpu.SemaphoreType.DMA((1, ring.dp)),
        ],
        mib=56,
        after=after,
    )


def ffn_next_kernel(halves, count, places, unit_ref, scale_ref, *refs):
    g_refs, (out_in, gn_in), refs = refs[:2], refs[2:4], refs[4:]
    sources, refs = refs[:halves], refs[halves:]
    out_ref, mid_ref, act_ref, gpre_ref, w_scr, sem = refs
    units = w_scr.shape[1] // 2

    @pl.when(pl.program_id(0) == 0)
    def _():
        load(places, sources, w_scr, sem, pl.ds(0, 2 * units))

    win, wout = w_scr[:, :units], w_scr[:, units:]
    unit = unit_ref[...]
    g = pick(count, *g_refs)
    act, slope = gelu_parts(dot(unit, win))
    act = act.astype(BF)
    gpre = (dot(g, wout) * slope).astype(BF)
    act_ref[...] = act
    gpre_ref[...] = gpre
    out_ref[...] = (out_in[...] + dot_cols(act, wout)).astype(BF)
    lead = places[places.shape[0] - 1].astype(F32)
    back = norm_back(gn_in[...] + dot_cols(gpre, win), unit.astype(F32), scale_ref[:, :1])
    mid_ref[...] = (back + lead * g.astype(F32)).astype(BF)


def ffn_next(ring, unit, scale, gs, out, gn, weights, units, tile=512, after=()):
    rows, width = unit.shape
    outs = [out_of((rows, width), BF)] * 2 + [out_of((rows, units), BF)] * 2
    return call(
        functools.partial(ffn_next_kernel, len(weights), gs[0].shape[0] // tile),
        outs,
        [ring.places, unit, scale, *gs, out, gn, *weights],
        ins=[SMEM, tiles(unit, tile), tiles(scale, tile)]
        + pair_tiles(gs, tile)
        + [tiles(out, tile), tiles(gn, tile)]
        + [HBM] * len(weights),
        out_specs=[tiles(o, tile) for o in outs],
        grid=(rows // tile,),
        scratch=[pltpu.VMEM((width, 2 * units), BF), pltpu.SemaphoreType.DMA((ring.dp,))],
        mib=56,
        after=after,
    )


def ffn_grads_kernel(emits, count, places, unit_ref, *refs):
    g_refs, (gpre_ref, act_ref) = refs[:2], refs[2:4]
    grads, total = refs[4:-1], refs[-1]
    step = pl.program_id(0)
    units = act_ref.shape[1]

    @pl.when(step == 0)
    def _():
        total[...] = jnp.zeros_like(total)

    total[:, :units] += dot_rows(unit_ref[...], gpre_ref[...])
    total[:, units:] += dot_rows(pick(count, *g_refs), act_ref[...])

    @pl.when(step == pl.num_programs(0) - 1)
    def _():
        if emits == 2:
            emit(places, total, *grads)
        else:
            grads[0][...] = total[...]


def ffn_grads(ring, unit, gs, gpre, act, tile=512, after=()):
    rows, width = unit.shape
    cols = 2 * act.shape[1]
    outs = emitted(ring, width, cols)
    return call(
        functools.partial(ffn_grads_kernel, len(outs), gs[0].shape[0] // tile),
        outs,
        [ring.places, unit, *gs, gpre, act],
        ins=[SMEM, tiles(unit, tile)]
        + pair_tiles(gs, tile)
        + [tiles(gpre, tile), tiles(act, tile)],
        out_specs=[fixed(o) for o in outs],
        grid=(rows // tile,),
        scratch=[pltpu.VMEM((width, cols), F32)],
        mib=32,
        after=after,
    )


def middle_kernel(halves, groups, pairs, at, places, *refs):
    mid_refs, refs = refs[:groups], refs[groups:]
    o_refs, refs = refs[:pairs], refs[pairs:]
    sources, (go_ref, total_ref, w_scr, sem) = refs[:halves], refs[halves:]
    step = pl.program_id(0)

    @pl.when(step == 0)
    def _():
        total_ref[...] = jnp.zeros_like(total_ref)
        load(places, sources, w_scr, sem, pl.ds(at, pairs * LANES))

    grad = sum_of(mid_refs).astype(BF)
    go_ref[...] = dot(grad, w_scr[...]).astype(BF)
    total_ref[...] += dot_rows(grad, jnp.concatenate([r[...] for r in o_refs], 1))


def middle_back(ring, mids, mixed, weights, at, tile=512, after=()):
    rows, width = mids[0].shape
    pairs = len(mixed)
    cols = pairs * LANES
    go, total = out_of((rows, cols), BF), out_of((width, cols), F32)
    return call(
        functools.partial(middle_kernel, len(weights), len(mids), pairs, at),
        [go, total],
        [ring.places, *mids, *mixed, *weights],
        ins=[SMEM] + [tiles(a, tile) for a in (*mids, *mixed)] + [HBM] * len(weights),
        out_specs=[tiles(go, tile), fixed(total)],
        grid=(rows // tile,),
        scratch=[pltpu.VMEM((width, cols), BF), pltpu.SemaphoreType.DMA((ring.dp,))],
        mib=24,
        after=after,
    )


def input_back_kernel(plan, groups, pairs, count, places, short_ref, long_ref, *refs):
    mid_refs, refs = refs[:groups], refs[groups:]
    g_refs, refs = refs[:pairs], refs[pairs:]
    sources, (part_ref, w_scr, sem) = refs[:-3], refs[-3:]

    @pl.when(pl.program_id(0) == 0)
    def _():
        load_all(places, sources, w_scr, sem, plan)

    part = dot_cols(jnp.concatenate([r[...] for r in g_refs], 1), w_scr[...])
    scale, unit = rms_parts(pick(count, short_ref, long_ref).astype(F32))
    lead = places[places.shape[0] - 1].astype(F32)
    part_ref[...] = (norm_back(part, unit, scale) + lead * sum_of(mid_refs)).astype(BF)


def input_back(ring, xs, mids, grads, weights, plan, tile=512, after=()):
    rows, width = grads[0].shape[0], xs[0].shape[1]
    pairs = len(grads)
    out = out_of((rows, width), BF)
    return call(
        functools.partial(input_back_kernel, plan, len(mids), pairs, xs[0].shape[0] // tile),
        [out],
        [ring.places, *xs, *mids, *grads, *weights],
        ins=[SMEM]
        + pair_tiles(xs, tile)
        + [tiles(a, tile) for a in (*mids, *grads)]
        + [HBM] * len(weights),
        out_specs=[tiles(out, tile)],
        grid=(rows // tile,),
        scratch=[
            pltpu.VMEM((width, 3 * pairs * LANES), BF),
            pltpu.SemaphoreType.DMA((len(plan), ring.dp)),
        ],
        mib=20,
        after=after,
    )[0]


def pad_cols(array, cols):
    return jnp.pad(array, ((0, 0), (0, cols - array.shape[1]))) if cols > array.shape[1] else array


def on_device(
    sizes,
    x_short,
    x_long,
    len_short,
    len_long,
    boundaries,
    q_weight,
    k_weight,
    v_weight,
    out_weight,
    in_weight,
    ff_out_weight,
    attn_gain,
    ffn_gain,
    bias_table,
    cot_short,
    cot_long,
):
    ring = Ring(sizes)
    quarter = ring.quarter
    width = x_short.shape[2]
    buckets, heads = bias_table.shape
    real = heads * DH
    cols = -(-real // LANES) * LANES
    pairs = cols // LANES
    units = in_weight.shape[1] // 2
    batches = [x.shape[:2] for x in (x_short, x_long)]
    lens = (len_short, len_long)

    xs = [x.reshape(-1, width) for x in (x_short, x_long)]
    gs = [g.reshape(-1, width) for g in (cot_short, cot_long)]

    col_a, col_f = (v.astype(F32)[:, None] for v in (attn_gain, ffn_gain))
    padded = [pad_cols(w, cols) for w in (q_weight, k_weight, v_weight, out_weight)]
    scaled = [(w.astype(F32) * col_a).astype(BF) for w in padded[:3]]
    pieces = [[w[:, p * LANES : (p + 1) * LANES] for w in scaled] for p in range(pairs)]
    own = jnp.concatenate([w for piece in pieces for w in piece] + [padded[3]], 1)[None]
    win = (in_weight.astype(F32) * col_f).astype(BF)
    own1, own2 = (
        jnp.concatenate([w[:, at : at + units] for w in (win, ff_out_weight)], 1)[None]
        for at in (0, units)
    )
    step = 3 * LANES
    z = tuple(range(quarter))
    table = jnp.pad(bias_table.T, ((0, 8 - heads), (0, 0)))

    two = (0, 1)
    wide = own.shape[2]
    got = ring.far(own)
    held, own1 = join([own, *got], [(z, 0, wide)], through=[own1])
    got = ring.first(held)
    got1 = ring.far(own1)
    unit = norm(xs, after=[held])
    plan = [(two, 0, step), (two, step, wide)]
    *helds, own2 = join([held, got], plan, after=[unit], through=[own2])
    qkv, kvo = [blocks_of(ring, h, ring.last(h)) for h in helds]
    qkvo = [(qkv, 0)] + [(kvo, p * step) for p in range(pairs - 1)]

    fwd = []
    after = helds
    for p in range(pairs):
        fwd.append(
            attend(ring, batches, lens, boundaries, table, unit, *qkvo[p], p, after=after)
        )
        if p == 0:
            held1, own2 = join(
                [own1, *got1], [(z, 0, 2 * units)], after=[fwd[0][0]], through=[own2]
            )
            got1 = ring.first(held1)
            got2 = ring.far(own2)
            after = [held1]
        if p == min(1, pairs - 1):
            z2 = tuple(2 + i for i in z)
            plan = [(two, 0, 2 * units), (z2, 0, 2 * units)]
            held1, held2 = join([held1, got1, own2, *got2], plan, after=[fwd[p][0]])
            got1, got2 = ring.last(held1), ring.first(held2)
            after = [held2]
    mixed = [f[3] for f in fwd]
    out_w, out_at = kvo, (pairs - 1) * step
    attn = project_out(ring, mixed, out_w, out_at, width, after=[got2, got1])
    fields = [attn] + ring.exchange(attn)
    (held2,) = join([held2, got2], [(two, 0, 2 * units)], after=[attn])
    got2 = ring.last(held2)
    first = blocks_of(ring, held1, got1)
    second = blocks_of(ring, held2, got2)

    unit_f, scale, out, gn, *grad1 = ffn_first(
        ring, gs, xs, fields, first, units, after=[held2]
    )
    keep1, send = halves(ring, grad1)
    got1 = ring.last(send)
    out, mid, act, gpre = ffn_next(ring, unit_f, scale, gs, out, gn, second, units)
    keep1, send, mid, out = fold((keep1, got1, 0), through=[mid, out])
    mids = [mid] + ring.exchange(mid)
    outs = [out] + ring.exchange(out)
    got1 = ring.first(send)
    keep2, send2 = halves(ring, ffn_grads(ring, unit_f, gs, gpre, act, after=[keep1]))
    keep1, *sends, send2 = fold((keep1, got1, 1), after=[keep2], through=[send2])
    got1 = ring.far_all(sends)
    got2 = ring.last(send2)
    go, grad_o = middle_back(ring, mids, mixed, out_w, out_at, after=[keep1])

    grads = []
    totals = []
    sums = jnp.zeros((8, LANES), F32)
    after = [keep1]
    for p in range(pairs):
        last = p == pairs - 1
        before, rest = ((), ()) if last else (totals, [grad_o] if p == pairs - 2 else None)
        g, sums, made = attend_back(
            ring,
            batches,
            lens,
            boundaries,
            table,
            unit,
            go,
            fwd[p],
            p,
            sums,
            before,
            rest,
            last,
            after=after,
        )
        grads.append(g)
        if p < pairs - 2:
            totals.append(made[0])
        if p == 0:
            keep2, send2 = fold((keep2, got2, 0), after=[g])
            got2 = ring.first(send2)
            after = [keep2]
        if p == pairs - 2:
            early, send = made
            keep2, *sends, send = fold((keep2, got2, 1), after=[g, *got1], through=[send])
            got2 = ring.far_all(sends)
            got = ring.last(send)
            after = [keep2]
    keep, send = made
    early, early_send, send = fold((early, got, 0), after=got2, through=[send])
    early_got = ring.first(early_send)
    got = ring.last(send)
    plan = [(0, step), (0, (pairs - 1) * step)]
    weights = [*qkv, *kvo]
    part = input_back(ring, xs, mids, grads, weights, plan, after=[early])
    rows = [slice(0, xs[0].shape[0]), slice(xs[0].shape[0], None)]

    def sums_of(fields):
        return [sum(f[r].astype(F32) for f in fields).astype(BF) for r in rows]

    early, *more = fold(
        (early, early_got, 1), (keep, got, 0), through=[part, *outs]
    )
    sends, (keep, send, part, *outs) = more[: quarter - 1], more[quarter - 1 :]
    early = [early, *ring.far_all(sends)]
    got = ring.first(send)
    parts = [part] + ring.exchange(part)
    ys = sums_of(outs)
    keep, *sends, part = fold((keep, got, 1), after=ys, through=[parts[0]])
    late = [keep, *ring.far_all(sends)]
    grad_xs = sums_of([part] + parts[1:])
    plan = [
        [(0, 0, units), (1, 0, units)],
        [(0, units, 2 * units), (1, units, 2 * units)],
    ]
    grad_in, grad_ff, gain_f = final(
        [[keep1, *got1], [keep2, *got2]], plan, [0], col_f, [in_weight], after=grad_xs
    )
    plan = [
        [(0, p * step + i * LANES, p * step + (i + 1) * LANES) for p in range(pairs - 1)]
        + [(1, i * LANES, (i + 1) * LANES)]
        for i in range(3)
    ]
    plan += [[(0, (pairs - 1) * step, (pairs - 1) * step + cols)], [(1, step, step + LANES)]]
    gq, gk, gv, grad_o, sums, gain = final(
        [early, late], plan, [0, 1, 2], col_a, padded[:3], carry=[gain_f]
    )
    for other in ring.exchange(gain):
        gain = gain + other
    return (
        ys[0].reshape(x_short.shape),
        ys[1].reshape(x_long.shape),
        grad_xs[0].reshape(x_short.shape),
        grad_xs[1].reshape(x_long.shape),
        gq[:, :real],
        gk[:, :real],
        gv[:, :real],
        grad_o[:, :real],
        grad_in,
        grad_ff,
        gain[:, 0],
        gain[:, 1],
        sums[:heads, :buckets].T,
    )


def solution(mesh):
    sizes = (mesh.shape["dp"], mesh.shape["mp"])
    return jax.shard_map(
        functools.partial(on_device, sizes),
        mesh=mesh,
        in_specs=(
            P("dp", None, None),
            P("dp", None, None),
            P("dp"),
            P("dp"),
            P(),
            P("dp", "mp"),
            P("dp", "mp"),
            P("dp", "mp"),
            P("dp", "mp"),
            P("dp", "mp"),
            P("dp", "mp"),
            P("dp"),
            P("dp"),
            P(None, "mp"),
            P("dp", None, None),
            P("dp", None, None),
        ),
        out_specs=(
            P("dp", None, None),
            P("dp", None, None),
            P("dp", None, None),
            P("dp", None, None),
            P("dp", "mp"),
            P("dp", "mp"),
            P("dp", "mp"),
            P("dp", "mp"),
            P("dp", "mp"),
            P("dp", "mp"),
            P("dp"),
            P("dp"),
            P(None, "mp"),
        ),
        check_vma=False,
    )
```

```python
import functools

import jax
import jax.numpy as jnp
from jax import lax
from jax.experimental import pallas as pl
from jax.experimental.pallas import tpu as pltpu
from jax.sharding import PartitionSpec as P

DH = 64
LANES = 128
EPS = 1e-06
NEG = -1000000000.0
BF = jnp.bfloat16
F32 = jnp.float32
ANY = pl.BlockSpec(memory_space=pl.ANY)
HBM = pl.BlockSpec(memory_space=pltpu.HBM)
SMEM = pl.BlockSpec(memory_space=pltpu.SMEM)
VMEM = pl.BlockSpec(memory_space=pltpu.VMEM)


def dot(left, right):
    return jnp.dot(left, right, preferred_element_type=F32)


def dot_rows(left, right):
    return lax.dot_general(left, right, (((0,), (0,)), ((), ())), preferred_element_type=F32)


def dot_cols(left, right):
    return lax.dot_general(left, right, (((1,), (1,)), ((), ())), preferred_element_type=F32)


def tiles(array, rows):
    return pl.BlockSpec((rows,) + array.shape[1:], lambda i: (i,) + (0,) * (len(array.shape) - 1))


def fixed(array):
    return pl.BlockSpec(array.shape, lambda i: (0,) * len(array.shape))


def pair_tiles(pair, rows):
    count = pair[0].shape[0] // rows
    rest = (0,) * (pair[0].ndim - 1)
    shape = (rows,) + pair[0].shape[1:]
    return [
        pl.BlockSpec(shape, lambda i: (jnp.minimum(i, count - 1),) + rest),
        pl.BlockSpec(shape, lambda i: (jnp.maximum(i - count, 0),) + rest),
    ]


def pick(count, first, second):
    return jnp.where(pl.program_id(0) < count, first[...], second[...])


def out_of(shape, kind):
    return jax.ShapeDtypeStruct(tuple(shape), kind)


def call(kernel, outs, args, *, ins=None, out_specs=None, grid=None, scratch=(), us=0.001, mib=4, after=(), through=()):
    ins = list(ins or [VMEM] * len(args))
    out_specs = list(out_specs or [VMEM] * len(outs))
    extra = {} if grid is None else {"grid": grid}
    idle = len(after) + len(through)

    def body(*refs):
        given, made = refs[: len(args)], refs[len(args) + idle :]
        kernel(*given, *made[: len(outs)], *made[len(outs) + len(through) :])

    return pl.pallas_call(
        body,
        out_shape=list(outs) + [out_of(t.shape, t.dtype) for t in through],
        in_specs=ins + [ANY] * idle,
        out_specs=out_specs + [ANY] * len(through),
        scratch_shapes=list(scratch),
        compiler_params=pltpu.CompilerParams(vmem_limit_bytes=mib << 20),
        input_output_aliases={len(args) + len(after) + i: len(outs) + i for i in range(len(through))},
        cost_estimate=pl.CostEstimate(flops=int(us * 1e9), bytes_accessed=1000, transcendentals=0),
        **extra,
    )(*args, *after, *through)


class Ring:
    def __init__(self, sizes):
        self.dp, self.mp = sizes
        self.me = lax.axis_index("dp")
        self.odd = lax.axis_index("mp") & 1
        self.quarter = self.dp // 4
        j = jnp.arange(self.dp, dtype=jnp.int32)
        first = (j // self.quarter) & 1
        last = j // (2 * self.quarter)

        def order(odd):
            low = jnp.where(odd == 0, first + 2 * last, 2 * first + last)
            return self.me ^ (4 * (j % self.quarter) + low)

        self.order = order(self.odd)
        self.orders = [order(self.odd ^ (k & 1)) for k in range(1, self.mp)]
        rel = self.me ^ j
        bit0, bit1 = rel & 1, (rel >> 1) & 1
        first, last = jnp.where(self.odd == 0, bit0, bit1), jnp.where(self.odd == 0, bit1, bit0)
        self.spots = (rel >> 2) + self.quarter * (first + 2 * last)
        lead = (lax.axis_index("mp") == 0).astype(jnp.int32)
        self.places = jnp.concatenate([self.order, lead[None]])

    def far(self, array):
        return [
            lax.ppermute(array, "dp", [(i, i ^ (4 * step)) for i in range(self.dp)])
            for step in range(1, self.quarter)
        ]

    def far_all(self, arrays):
        return [
            lax.ppermute(a, "dp", [(i, i ^ (4 * (step + 1))) for i in range(self.dp)])
            for step, a in enumerate(arrays)
        ]

    def near(self, array, masks):
        pairs = [
            (i * self.mp + c, (i ^ masks[c & 1]) * self.mp + c)
            for i in range(self.dp)
            for c in range(self.mp)
        ]
        return lax.ppermute(array, ("dp", "mp"), pairs)

    def first(self, array):
        return self.near(array, (1, 2))

    def last(self, array):
        return self.near(array, (2, 1))

    def exchange(self, array):
        return [
            lax.ppermute(array, "mp", [(i, i ^ k) for i in range(self.mp)])
            for k in range(1, self.mp)
        ]


def join_kernel(plan, *refs):
    sources, outs = refs[: -len(plan)], refs[-len(plan) :]
    for (chosen, start, stop), out in zip(plan, outs):
        at = 0
        for i in chosen:
            count = sources[i].shape[0]
            out[at : at + count] = sources[i][:, :, start:stop]
            at += count


def join(arrays, plan, after=(), through=()):
    outs = []
    for chosen, start, stop in plan:
        count = sum(arrays[i].shape[0] for i in chosen)
        outs.append(out_of((count, arrays[0].shape[1], stop - start), arrays[0].dtype))
    return call(functools.partial(join_kernel, plan), outs, arrays, after=after, through=through)


def aligned(rows):
    return rows % 16 == 0


def blocks_of(ring, held, got):
    if aligned(held.shape[1]):
        return (held, got)
    blocks = jnp.take(jnp.concatenate([held, got], 0), ring.spots, axis=0)
    return (blocks.reshape((-1,) + held.shape[2:]),)


def load(places, sources, to, at):
    there = slice(at, at + sources[0].shape[-1])
    if len(sources) == 2:
        half, rows, _ = sources[0].shape
        for j in range(2 * half):
            row = pl.multiple_of(places[j] * rows, 16)
            to[pl.ds(row, rows), there] = sources[j // half][j % half]
    else:
        to[:, there] = sources[0][...]
    return there.stop


def columns(array, at, count):
    first = (0,) * (array.ndim - 1)
    return pl.BlockSpec(
        array.shape[:-1] + (count,),
        lambda i: first + (at // count,),
        pipeline_mode=pl.Buffered(1),
    )


def emit(places, total, keep, send, extra=None):
    half, rows, _ = keep.shape
    for j in range(2 * half):
        at = pl.multiple_of(places[j] * rows, 16)
        block = total[pl.ds(at, rows), :]
        if extra is not None:
            block = block + extra
        if j < half:
            keep[j] = block
        else:
            send[j - half] = block.astype(BF)


def emitted(ring, rows, cols):
    share = rows // ring.dp
    if aligned(share):
        shape = (ring.dp // 2, share, cols)
        return [out_of(shape, F32), out_of(shape, BF)]
    return [out_of((rows, cols), F32)]


def halves(ring, outs, extra=None):
    if len(outs) == 2:
        return outs
    blocks = outs[0].reshape(ring.dp, -1, outs[0].shape[1])
    if extra is not None:
        blocks = blocks + extra
    blocks = jnp.take(blocks, ring.order, axis=0)
    return blocks[: ring.dp // 2], blocks[ring.dp // 2 :].astype(BF)


def fold_kernel(modes, *refs):
    ins, outs = refs[: 2 * len(modes)], refs[2 * len(modes) :]
    for mode in modes:
        keep, got = ins[:2]
        ins = ins[2:]
        count = got.shape[0] if mode else got.shape[0] // 2
        if mode:
            outs[0][...] = keep[0] + got[0].astype(F32)
            for j in range(1, count):
                outs[j][...] = (keep[j] + got[j].astype(F32)).astype(BF)
            outs = outs[count:]
        else:
            outs[0][...] = keep[:count] + got[:count].astype(F32)
            outs[1][...] = (keep[count:] + got[count:].astype(F32)).astype(BF)
            outs = outs[2:]


def fold(*items, after=(), through=()):
    outs = []
    args = []
    for keep, got, mode in items:
        args += [keep, got]
        if mode:
            shape = keep.shape[1:]
            outs += [out_of(shape, F32)] + [out_of(shape, BF)] * (keep.shape[0] - 1)
        else:
            shape = (keep.shape[0] // 2,) + keep.shape[1:]
            outs += [out_of(shape, F32), out_of(shape, BF)]
    kernel = functools.partial(fold_kernel, [m for *_, m in items])
    return call(kernel, outs, args, after=after, through=through)


def final_kernel(counts, plan, scaled, carried, gain_ref, *refs):
    carry, refs = refs[:carried], refs[carried:]
    weights, refs = refs[: len(scaled)], refs[len(scaled) :]
    fields = []
    for count in counts:
        total = refs[0][...]
        for r in refs[1:count]:
            total = total + r[...].astype(F32)
        fields.append(total)
        refs = refs[count:]
    outs, gain_out = refs[:-1], refs[-1]
    sums = jnp.zeros(gain_out.shape, F32)
    for i, (out, spans) in enumerate(zip(outs, plan)):
        at = 0
        for f, start, stop in spans:
            value = fields[f][:, start:stop]
            there = slice(at, at + stop - start)
            if i in scaled:
                kept = weights[scaled.index(i)][:, there].astype(F32)
                sums += jnp.sum(value * kept, 1, keepdims=True)
                value = value * gain_ref[...]
            out[:, there] = value
            at += stop - start
    if carried:
        lane = lax.broadcasted_iota(jnp.int32, sums.shape, 1)
        sums = jnp.where(lane == 0, sums, carry[0][...])
    gain_out[...] = sums


def final(items, plan, scaled, gain, weights, carry=(), after=()):
    rows = gain.shape[0]
    outs = [out_of((rows, sum(b - a for _, a, b in spans)), F32) for spans in plan]
    outs.append(out_of((rows, LANES), F32))
    kernel = functools.partial(final_kernel, [len(i) for i in items], plan, scaled, len(carry))
    args = [gain, *carry, *weights, *[a for i in items for a in i]]
    return call(kernel, outs, args, after=after)


def distance_buckets(bounds_ref, dist, buckets):
    size = jnp.abs(dist)
    half = jnp.zeros(dist.shape, jnp.int32)
    for b in range(bounds_ref.shape[0]):
        half += (size >= bounds_ref[b]).astype(jnp.int32)
    return half + jnp.where(dist > 0, buckets // 2, 0)


def bases_kernel(bounds_ref, table_ref, near_ref, far_ref):
    heads, _, width = near_ref.shape
    buckets = table_ref.shape[1]
    row = lax.broadcasted_iota(jnp.int32, (8, width), 0)
    for to, sign in ((near_ref, 1), (far_ref, -1)):
        dist = sign * (lax.broadcasted_iota(jnp.int32, (8, width), 1) - width // 2)
        marks = distance_buckets(bounds_ref, dist, buckets)
        marks = jnp.concatenate([marks] * (buckets // 8), 0)
        onehot = (marks == lax.broadcasted_iota(jnp.int32, (buckets, width), 0)).astype(F32)
        line = dot(table_ref[...], onehot.astype(BF))
        for h in range(heads):
            field = jnp.broadcast_to(line[h : h + 1], (8, width))
            for k in (1, 2, 4):
                field = jnp.where((row & k) != 0, pltpu.roll(field, k, 1), field)
            while field.shape[0] < LANES:
                field = jnp.concatenate([field, pltpu.roll(field, field.shape[0], 1)], 0)
            to[h] = field


def bias_bases(boundaries, table, heads, width, after=()):
    shape = out_of((heads, LANES, width), F32)
    return call(
        bases_kernel, [shape, shape], [boundaries, table], ins=[SMEM, VMEM], mib=16, after=after
    )


def bucket_field(bounds_ref, fields, buckets, first):
    width = fields[0].shape[-1]
    dist = width // 2 - lax.broadcasted_iota(jnp.int32, (8, width), 1)
    marks = distance_buckets(bounds_ref, dist, buckets)
    row = lax.broadcasted_iota(jnp.int32, (8, width), 0)
    line = jnp.zeros((8, width), F32)
    for h, field in enumerate(fields, first):
        while field.shape[0] > 8:
            half = field.shape[0] // 2
            field = field[:half] + pltpu.roll(field[half:], width - half, 1)
        for k in (4, 2, 1):
            field = jnp.where((row & k) != 0, pltpu.roll(field, width - k, 1), field)
        line = jnp.where(row == h, jnp.sum(field, 0, keepdims=True), line)
    lane = lax.broadcasted_iota(jnp.int32, (8, LANES), 1)
    out = jnp.zeros((8, LANES), F32)
    for b in range(buckets):
        total = jnp.sum(jnp.where(marks == b, line, 0.0), 1, keepdims=True)
        out = jnp.where(lane == b, total, out)
    return out


def split_low(values, lane, off, rest):
    high = values.astype(BF).astype(F32)
    mid = (values - high).astype(BF).astype(F32)
    low = values - high - mid
    return jnp.where(
        lane == off,
        high,
        jnp.where(lane == off + 1, mid, jnp.where(lane == off + 2, low, rest)),
    )


def three_ones(lane, off):
    return jnp.where((lane >= off) & (lane < off + 3), 1.0, 0.0)


def slots_of(batches):
    at = 0
    for b, (slots, length) in enumerate(batches):
        for s in range(slots):
            yield b, s, length, slice(at, at + length)
            at += length


def attend_kernel(batches, halves, *refs):
    places, lens = refs[0], refs[1 : 1 + len(batches)]
    refs = refs[1 + len(batches) :]
    normed_ref, near_ref = refs[:2]
    sources = refs[2 : 2 + halves]
    aug_ref, k_ref, v_ref, o_ref, w_scr = refs[2 + halves :]
    width = near_ref.shape[-1]
    load(places, sources, w_scr, 0)
    for b, s, length, span in slots_of(batches):
        valid = lens[b][s]
        lane = lax.broadcasted_iota(jnp.int32, (length, LANES), 1)
        place = lax.broadcasted_iota(jnp.int32, (length, LANES), 0)
        masked = jnp.where(place >= valid, NEG, 0.0)
        qkv = dot(normed_ref[span, :], w_scr[...])
        q, k, v = (qkv[:, i * LANES : (i + 1) * LANES] for i in range(3))
        k_ref[span, :] = k.astype(BF)
        v_ref[span, :] = v.astype(BF)
        mixed = []
        for e in range(2):
            own = (lane >= DH) == (e == 1)
            off = DH * (1 - e)
            marker = jnp.where(lane == off + 3, 1.0, 0.0)
            q_own = jnp.where(own, q, marker).astype(BF)
            k_own = jnp.where(own, k, jnp.where(lane == off + 3, masked, 0.0)).astype(BF)
            v_own = jnp.where(own, v, 1.0).astype(BF)
            start = width // 2
            bias = [
                near_ref[e, :, start - a * LANES : start - a * LANES + length]
                for a in range(length // LANES)
            ]
            scores = dot_cols(q_own, k_own) + jnp.concatenate(bias, 0)
            top = jnp.max(scores, 1, keepdims=True)
            expo = jnp.exp(scores - top)
            sums = dot(expo.astype(BF), v_own)
            total = jnp.where(own, pltpu.roll(sums, DH, 1), sums)
            logsum = top + jnp.log(total)
            extra = split_low(-logsum, lane, off, marker)
            aug_ref[span, e * LANES : (e + 1) * LANES] = jnp.where(own, q, extra).astype(BF)
            mixed.append(sums / total)
        o_ref[span, :] = jnp.where(lane < DH, mixed[0], mixed[1]).astype(BF)


def pair_of(base, pair):
    return pl.BlockSpec((2,) + base.shape[1:], lambda i: (pair, 0, 0))


def attend(ring, batches, lens, near, unit, weights, at, pair, after=()):
    rows, width = unit.shape
    shapes = [out_of((rows, c * LANES), BF) for c in (2, 1, 1, 1)]
    return call(
        functools.partial(attend_kernel, batches, len(weights)),
        shapes,
        [ring.places, *lens, unit, near, *weights],
        ins=[SMEM] * (1 + len(lens))
        + [fixed(unit), pair_of(near, pair)]
        + [columns(w, at, 3 * LANES) for w in weights],
        out_specs=[fixed(s) for s in shapes],
        grid=(1,),
        scratch=[pltpu.VMEM((width, 3 * LANES), BF)],
        mib=16,
        after=after,
    )


def attend_back_kernel(batches, pair, buckets, before, priors, emits, *refs):
    lens, refs = refs[: len(batches)], refs[len(batches) :]
    bounds, places, unit_ref, go_ref, aug_ref, k_ref, v_ref, o_ref, far_ref = refs[:9]
    totals, (table_in, grads_ref, table_ref) = refs[9 : 9 + priors], refs[9 + priors : 12 + priors]
    outs, (gbase_ref, total) = refs[12 + priors : -2], refs[-2:]
    width = far_ref.shape[-1]
    gbase_ref[...] = jnp.zeros_like(gbase_ref)
    for b, s, length, span in slots_of(batches):
        valid = lens[b][s]
        lane = lax.broadcasted_iota(jnp.int32, (length, LANES), 1)
        place = lax.broadcasted_iota(jnp.int32, (length, LANES), 0)
        masked = jnp.where(place >= valid, NEG, 0.0)
        k = k_ref[span, :].astype(F32)
        v = v_ref[span, :].astype(F32)
        go = go_ref[span, :].astype(F32)
        both = go * o_ref[span, :].astype(F32)
        grads = []
        for e in range(2):
            own = (lane >= DH) == (e == 1)
            off = DH * (1 - e)
            q_own = aug_ref[span, e * LANES : (e + 1) * LANES]
            ones = three_ones(lane, off)
            k_own = jnp.where(own, k, jnp.where(lane == off + 3, masked, ones)).astype(BF)
            v_own = jnp.where(own, v, ones).astype(BF)
            delta = jnp.sum(jnp.where(own, both, 0.0), 1, keepdims=True)
            g_own = jnp.where(own, go, split_low(-delta, lane, off, 0.0)).astype(BF)
            cols = [
                slice(width // 2 - a * LANES, width // 2 - a * LANES + length)
                for a in range(length // LANES)
            ]
            bias = jnp.concatenate([far_ref[e, :, c] for c in cols], 0)
            probs = jnp.exp(dot_cols(k_own, q_own) + bias)
            ds = probs * dot_cols(v_own, g_own)
            for a, c in enumerate(cols):
                gbase_ref[e, :, c] += ds[a * LANES : (a + 1) * LANES]
            ds = ds.astype(BF)
            gv = dot(probs.astype(BF), g_own)
            grads.append((dot_rows(ds, k_own), dot(ds, q_own), gv))
        first = lane < DH
        for i, (a, b) in enumerate(zip(*grads)):
            grads_ref[span, i * LANES : (i + 1) * LANES] = jnp.where(first, a, b).astype(BF)
    table = table_in[...] + bucket_field(
        bounds, [gbase_ref[0], gbase_ref[1]], buckets, 2 * pair
    )
    table_ref[...] = table
    part = dot_rows(unit_ref[...], grads_ref[...])
    if not emits:
        outs[0][...] = part
        return
    step = 3 * LANES
    at = 0
    for value in [r[...] for r in totals[:before]] + [part] + [r[...] for r in totals[before:]]:
        total[:, at : at + value.shape[1]] = value
        at += value.shape[1]
    extra = None
    if total.shape[1] > at:
        total[:, at:] = jnp.zeros((total.shape[0], LANES), F32)
    if total.shape[1] > at and emits == 2:
        rows = outs[0].shape[1]
        extra = jnp.concatenate([table, jnp.zeros((rows - 8, LANES), F32)], 0)
        extra = jnp.concatenate([jnp.zeros((rows, at), F32), extra], 1)
    if emits == 2:
        emit(places, total, *outs, extra=extra)
    else:
        outs[0][...] = total[...]


def attend_back(
    ring, batches, lens, boundaries, buckets, far, unit, go, fwd, pair, table, before, rest, last, after=()
):
    rows, width = unit.shape
    step = 3 * LANES
    go_spec = pl.BlockSpec((rows, LANES), lambda i: (0, pair))
    given = rest is None
    priors = [] if given else [*before, *rest]
    cols = step + sum(p.shape[1] for p in priors) + (LANES if last else 0)
    outs = [out_of((rows, step), BF), out_of((8, LANES), F32)]
    made = [out_of((width, step), F32)] if given else emitted(ring, width, cols)
    emits = 0 if given else len(made)
    kernel = functools.partial(
        attend_back_kernel, batches, pair, buckets, len(before), len(priors), emits
    )
    grads, table, *made = call(
        kernel,
        outs + made,
        [*lens, boundaries, ring.places, unit, go, *fwd, far, *priors, table],
        ins=[SMEM] * (len(lens) + 2)
        + [fixed(unit), go_spec]
        + [fixed(a) for a in fwd]
        + [pair_of(far, pair)]
        + [fixed(a) for a in (*priors, table)],
        out_specs=[fixed(o) for o in outs + made],
        grid=(1,),
        scratch=[
            pltpu.VMEM((2,) + far.shape[1:], F32),
            pltpu.VMEM((8, LANES) if given else (width, cols), F32),
        ],
        mib=24,
        after=after,
    )
    if not given:
        share = width // ring.dp
        extra = jnp.pad(table, ((0, share - 8), (cols - LANES, 0))) if last else None
        made = halves(ring, made, extra)
    return grads, table, made


def rms_parts(field):
    scale = lax.rsqrt(jnp.mean(field * field, -1, keepdims=True) + EPS)
    return (scale, field * scale)


def norm_back(grad_unit, unit, scale):
    return scale * (grad_unit - unit * jnp.mean(grad_unit * unit, -1, keepdims=True))


def norm_kernel(count, short_ref, long_ref, unit_ref):
    unit_ref[...] = rms_parts(pick(count, short_ref, long_ref).astype(F32))[1].astype(BF)


def norm(xs, tile=512, after=()):
    out = out_of((xs[0].shape[0] + xs[1].shape[0], xs[0].shape[1]), BF)
    return call(
        functools.partial(norm_kernel, xs[0].shape[0] // tile),
        [out],
        xs,
        ins=pair_tiles(xs, tile),
        out_specs=[tiles(out, tile)],
        grid=(out.shape[0] // tile,),
        mib=8,
        after=after,
    )[0]


def sum_of(refs):
    total = refs[0][...].astype(F32)
    for r in refs[1:]:
        total = total + r[...].astype(F32)
    return total


def add_kernel(count, addends, *refs):
    value = sum_of(refs[:addends]).astype(BF)

    @pl.when(pl.program_id(0) < count)
    def _():
        refs[-2][...] = value

    @pl.when(pl.program_id(0) >= count)
    def _():
        refs[-1][...] = value


def add_all(shapes, fields, tile=512, after=()):
    outs = [out_of(s, BF) for s in shapes]
    return call(
        functools.partial(add_kernel, shapes[0][0] // tile, len(fields)),
        outs,
        fields,
        ins=[tiles(f, tile) for f in fields],
        out_specs=pair_tiles(outs, tile),
        grid=((shapes[0][0] + shapes[1][0]) // tile,),
        after=after,
    )


def gelu_parts(x):
    c = 0.7978845608028654
    d = c * 0.044715
    square = x * x
    t = jnp.tanh(x * (c + d * square))
    half = 0.5 + 0.5 * t
    slope = half + (0.5 * x) * (1.0 - t * t) * (c + 3.0 * d * square)
    return x * half, slope


def ffn_first_kernel(halves, groups, pairs, emits, count, places, *refs):
    all_places, refs = [places, places, *refs[: groups - 1]], refs[groups - 1 :]
    g_refs, x_refs, refs = refs[:2], refs[2:4], refs[4:]
    o_refs, refs = refs[: groups * pairs], refs[groups * pairs :]
    sources, refs = refs[:halves], refs[halves:]
    unit_ref, scale_ref, out_ref, gn_ref = refs[:4]
    grads, (w_scr, total) = refs[4 : 4 + emits], refs[4 + emits :]
    units = total.shape[1] // 2
    step = pl.program_id(0)

    @pl.when(step == 0)
    def _():
        total[...] = jnp.zeros_like(total)
        at = 0
        count = halves // (1 + groups)
        for i, there in enumerate(all_places):
            at = load(there, sources[i * count : (i + 1) * count], w_scr, at)

    mixed = jnp.concatenate([r[...] for r in o_refs], 1)
    middle = pick(count, *x_refs).astype(F32) + dot_cols(mixed, w_scr[:, 2 * units :])
    scale, unit = rms_parts(middle)
    unit = unit.astype(BF)
    unit_ref[...] = unit
    scale_ref[...] = jnp.broadcast_to(scale, scale_ref.shape)
    g = pick(count, *g_refs)
    win, wout = w_scr[:, :units], w_scr[:, units : 2 * units]
    act, slope = gelu_parts(dot(unit, win))
    act = act.astype(BF)
    gpre = (dot(g, wout) * slope).astype(BF)
    lead = places[places.shape[0] - 1].astype(F32)
    out_ref[...] = (dot_cols(act, wout) + lead * middle).astype(BF)
    gn_ref[...] = dot_cols(gpre, win).astype(BF)
    total[:, :units] += dot_rows(unit, gpre)
    total[:, units:] += dot_rows(g, act)

    @pl.when(step == pl.num_programs(0) - 1)
    def _():
        if emits == 2:
            emit(places, total, *grads)
        else:
            grads[0][...] = total[...]


def ffn_first(ring, gs, xs, mixed, weights, out_weights, units, tile=512, after=()):
    rows = mixed[0].shape[0]
    width = xs[0].shape[1]
    groups = len(out_weights)
    pairs = len(mixed) // groups
    field = out_of((rows, width), BF)
    outs = [field, out_of((rows, LANES), F32), field, field]
    grads = emitted(ring, width, 2 * units)
    sources = [*weights, *[w for ws in out_weights for w in ws]]
    kernel = functools.partial(
        ffn_first_kernel, len(sources), groups, pairs, len(grads), xs[0].shape[0] // tile
    )
    return call(
        kernel,
        outs + grads,
        [ring.places, *ring.orders, *gs, *xs, *mixed, *sources],
        ins=[SMEM] * groups
        + pair_tiles(gs, tile)
        + pair_tiles(xs, tile)
        + [tiles(a, tile) for a in mixed]
        + [columns(w, 0, w.shape[-1]) for w in sources],
        out_specs=[tiles(o, tile) for o in outs] + [fixed(o) for o in grads],
        grid=(rows // tile,),
        scratch=[
            pltpu.VMEM((width, 2 * units + len(mixed) * LANES), BF),
            pltpu.VMEM((width, 2 * units), F32),
        ],
        mib=56,
        after=after,
    )


def ffn_next_kernel(halves, count, places, unit_ref, scale_ref, *refs):
    g_refs, (out_in, gn_in), refs = refs[:2], refs[2:4], refs[4:]
    sources, refs = refs[:halves], refs[halves:]
    out_ref, mid_ref, act_ref, gpre_ref, w_scr = refs
    units = w_scr.shape[1] // 2

    @pl.when(pl.program_id(0) == 0)
    def _():
        load(places, sources, w_scr, 0)

    win, wout = w_scr[:, :units], w_scr[:, units:]
    unit = unit_ref[...]
    g = pick(count, *g_refs)
    act, slope = gelu_parts(dot(unit, win))
    act = act.astype(BF)
    gpre = (dot(g, wout) * slope).astype(BF)
    act_ref[...] = act
    gpre_ref[...] = gpre
    out_ref[...] = (out_in[...] + dot_cols(act, wout)).astype(BF)
    lead = places[places.shape[0] - 1].astype(F32)
    back = norm_back(gn_in[...] + dot_cols(gpre, win), unit.astype(F32), scale_ref[:, :1])
    mid_ref[...] = (back + lead * g.astype(F32)).astype(BF)


def ffn_next(ring, unit, scale, gs, out, gn, weights, units, tile=512, after=()):
    rows, width = unit.shape
    outs = [out_of((rows, width), BF)] * 2 + [out_of((rows, units), BF)] * 2
    return call(
        functools.partial(ffn_next_kernel, len(weights), gs[0].shape[0] // tile),
        outs,
        [ring.places, unit, scale, *gs, out, gn, *weights],
        ins=[SMEM, tiles(unit, tile), tiles(scale, tile)]
        + pair_tiles(gs, tile)
        + [tiles(out, tile), tiles(gn, tile)]
        + [columns(w, 0, w.shape[-1]) for w in weights],
        out_specs=[tiles(o, tile) for o in outs],
        grid=(rows // tile,),
        scratch=[pltpu.VMEM((width, 2 * units), BF)],
        mib=56,
        after=after,
    )


def ffn_grads_kernel(emits, count, places, unit_ref, *refs):
    g_refs, (gpre_ref, act_ref) = refs[:2], refs[2:4]
    grads, total = refs[4:-1], refs[-1]
    step = pl.program_id(0)
    units = act_ref.shape[1]

    @pl.when(step == 0)
    def _():
        total[...] = jnp.zeros_like(total)

    total[:, :units] += dot_rows(unit_ref[...], gpre_ref[...])
    total[:, units:] += dot_rows(pick(count, *g_refs), act_ref[...])

    @pl.when(step == pl.num_programs(0) - 1)
    def _():
        if emits == 2:
            emit(places, total, *grads)
        else:
            grads[0][...] = total[...]


def ffn_grads(ring, unit, gs, gpre, act, tile=512, after=()):
    rows, width = unit.shape
    cols = 2 * act.shape[1]
    outs = emitted(ring, width, cols)
    return call(
        functools.partial(ffn_grads_kernel, len(outs), gs[0].shape[0] // tile),
        outs,
        [ring.places, unit, *gs, gpre, act],
        ins=[SMEM, tiles(unit, tile)]
        + pair_tiles(gs, tile)
        + [tiles(gpre, tile), tiles(act, tile)],
        out_specs=[fixed(o) for o in outs],
        grid=(rows // tile,),
        scratch=[pltpu.VMEM((width, cols), F32)],
        mib=32,
        after=after,
    )


def middle_kernel(halves, groups, pairs, places, *refs):
    mid_refs, refs = refs[:groups], refs[groups:]
    o_refs, refs = refs[:pairs], refs[pairs:]
    sources, (go_ref, total_ref, w_scr) = refs[:halves], refs[halves:]
    step = pl.program_id(0)

    @pl.when(step == 0)
    def _():
        total_ref[...] = jnp.zeros_like(total_ref)
        load(places, sources, w_scr, 0)

    grad = sum_of(mid_refs).astype(BF)
    go_ref[...] = dot(grad, w_scr[...]).astype(BF)
    total_ref[...] += dot_rows(grad, jnp.concatenate([r[...] for r in o_refs], 1))


def middle_back(ring, mids, mixed, weights, tile=512, after=()):
    rows, width = mids[0].shape
    pairs = len(mixed)
    cols = pairs * LANES
    go, total = out_of((rows, cols), BF), out_of((width, cols), F32)
    return call(
        functools.partial(middle_kernel, len(weights), len(mids), pairs),
        [go, total],
        [ring.places, *mids, *mixed, *weights],
        ins=[SMEM]
        + [tiles(a, tile) for a in (*mids, *mixed)]
        + [columns(w, 0, cols) for w in weights],
        out_specs=[tiles(go, tile), fixed(total)],
        grid=(rows // tile,),
        scratch=[pltpu.VMEM((width, cols), BF)],
        mib=24,
        after=after,
    )


def input_back_kernel(halves, groups, pairs, count, places, short_ref, long_ref, *refs):
    mid_refs, refs = refs[:groups], refs[groups:]
    g_refs, refs = refs[:pairs], refs[pairs:]
    sources, (part_ref, w_scr) = refs[:-2], refs[-2:]

    @pl.when(pl.program_id(0) == 0)
    def _():
        at = 0
        for i in range(0, len(sources), halves):
            at = load(places, sources[i : i + halves], w_scr, at)

    part = dot_cols(jnp.concatenate([r[...] for r in g_refs], 1), w_scr[...])
    scale, unit = rms_parts(pick(count, short_ref, long_ref).astype(F32))
    lead = places[places.shape[0] - 1].astype(F32)
    part_ref[...] = (norm_back(part, unit, scale) + lead * sum_of(mid_refs)).astype(BF)


def input_back(ring, xs, mids, grads, weights, tile=512, after=()):
    rows, width = grads[0].shape[0], xs[0].shape[1]
    pairs = len(grads)
    out = out_of((rows, width), BF)
    return call(
        functools.partial(
            input_back_kernel, len(weights[0][0]), len(mids), pairs, xs[0].shape[0] // tile
        ),
        [out],
        [ring.places, *xs, *mids, *grads, *[a for blocks, _ in weights for a in blocks]],
        ins=[SMEM]
        + pair_tiles(xs, tile)
        + [tiles(a, tile) for a in (*mids, *grads)]
        + [columns(a, 0, count) for blocks, count in weights for a in blocks],
        out_specs=[tiles(out, tile)],
        grid=(rows // tile,),
        scratch=[pltpu.VMEM((width, 3 * pairs * LANES), BF)],
        mib=20,
        after=after,
    )[0]


def pad_cols(array, cols):
    return jnp.pad(array, ((0, 0), (0, cols - array.shape[1]))) if cols > array.shape[1] else array


def on_device(
    sizes,
    x_short,
    x_long,
    len_short,
    len_long,
    boundaries,
    q_weight,
    k_weight,
    v_weight,
    out_weight,
    in_weight,
    ff_out_weight,
    attn_gain,
    ffn_gain,
    bias_table,
    cot_short,
    cot_long,
):
    ring = Ring(sizes)
    quarter = ring.quarter
    width = x_short.shape[2]
    buckets, heads = bias_table.shape
    real = heads * DH
    cols = -(-real // LANES) * LANES
    pairs = cols // LANES
    units = in_weight.shape[1] // 2
    batches = [x.shape[:2] for x in (x_short, x_long)]
    lens = (len_short, len_long)

    xs = [x.reshape(-1, width) for x in (x_short, x_long)]
    gs = [g.reshape(-1, width) for g in (cot_short, cot_long)]

    col_a, col_f = (v.astype(F32)[:, None] for v in (attn_gain, ffn_gain))
    padded = [pad_cols(w, cols) for w in (q_weight, k_weight, v_weight, out_weight)]
    scaled = [(w.astype(F32) * col_a).astype(BF) for w in padded[:3]]
    pieces = [[w[:, p * LANES : (p + 1) * LANES] for w in scaled] for p in range(pairs)]
    own = jnp.concatenate([w for piece in pieces for w in piece] + [padded[3]], 1)[None]
    win = (in_weight.astype(F32) * col_f).astype(BF)
    own1, own2 = (
        jnp.concatenate([w[:, at : at + units] for w in (win, ff_out_weight)], 1)[None]
        for at in (0, units)
    )
    step = 3 * LANES
    z = tuple(range(quarter))
    table = jnp.pad(bias_table.T, ((0, 8 - heads), (0, 0)))

    two = (0, 1)
    wide = own.shape[2]
    got = ring.far(own)
    span = 2 * max(length for _, length in batches)
    near, far = bias_bases(boundaries, table, cols // DH, span, after=[own])
    held, own1 = join([own, *got], [(z, 0, wide)], after=[near], through=[own1])
    got = ring.first(held)
    got1 = ring.far(own1)
    unit = norm(xs, after=[held])
    plan = [(two, 0, step), (two, step, wide)]
    *helds, own2 = join([held, got], plan, after=[unit], through=[own2])
    qkv, more = [blocks_of(ring, h, ring.last(h)) for h in helds]
    out_at = (pairs - 1) * step
    out_w = [m[..., out_at:] for m in more]
    qkvs = [(qkv, 0)] + [(more, p * step) for p in range(pairs - 1)]
    out_ws = [out_w] + list(zip(*[ring.exchange(w) for w in out_w]))

    fwd = []
    after = helds
    for p in range(pairs):
        fwd.append(
            attend(ring, batches, lens, near, unit, *qkvs[p], p, after=after)
        )
        if p == 0:
            held1, own2 = join(
                [own1, *got1], [(z, 0, 2 * units)], after=[fwd[0][0]], through=[own2]
            )
            got1 = ring.first(held1)
            got2 = ring.far(own2)
            after = [held1]
        if p == min(1, pairs - 1):
            z2 = tuple(2 + i for i in z)
            plan = [(two, 0, 2 * units), (z2, 0, 2 * units)]
            held1, held2 = join([held1, got1, own2, *got2], plan, after=[fwd[p][0]])
            got1, got2 = ring.last(held1), ring.first(held2)
            after = [held2]
    mixed = [f[3] for f in fwd]
    others = list(zip(*[ring.exchange(o) for o in mixed]))
    (held2,) = join([held2, got2], [(two, 0, 2 * units)], after=[fwd[-1][0]])
    got2 = ring.last(held2)
    first = blocks_of(ring, held1, got1)
    second = blocks_of(ring, held2, got2)

    unit_f, scale, out, gn, *grad1 = ffn_first(
        ring, gs, xs, [*mixed, *[o for g in others for o in g]], first, out_ws, units, after=[held2]
    )
    keep1, send = halves(ring, grad1)
    got1 = ring.last(send)
    out, mid, act, gpre = ffn_next(ring, unit_f, scale, gs, out, gn, second, units)
    keep1, send, mid, out = fold((keep1, got1, 0), through=[mid, out])
    mids = [mid] + ring.exchange(mid)
    outs = [out] + ring.exchange(out)
    got1 = ring.first(send)
    keep2, send2 = halves(ring, ffn_grads(ring, unit_f, gs, gpre, act, after=[keep1]))
    keep1, *sends, send2 = fold((keep1, got1, 1), after=[keep2], through=[send2])
    got1 = ring.far_all(sends)
    got2 = ring.last(send2)
    go, grad_o = middle_back(ring, mids, mixed, out_w, after=[keep1])

    grads = []
    totals = []
    sums = jnp.zeros((8, LANES), F32)
    after = [keep1]
    for p in range(pairs):
        last = p == pairs - 1
        before, rest = ((), ()) if last else (totals, [grad_o] if p == pairs - 2 else None)
        g, sums, made = attend_back(
            ring,
            batches,
            lens,
            boundaries,
            buckets,
            far,
            unit,
            go,
            fwd[p],
            p,
            sums,
            before,
            rest,
            last,
            after=after,
        )
        grads.append(g)
        if p < pairs - 2:
            totals.append(made[0])
        if p == 0:
            keep2, send2 = fold((keep2, got2, 0), after=[g])
            got2 = ring.first(send2)
            after = [keep2]
        if p == pairs - 2:
            early, send = made
            keep2, *sends, send = fold((keep2, got2, 1), after=[g, *got1], through=[send])
            got2 = ring.far_all(sends)
            got = ring.last(send)
            after = [keep2]
    keep, send = made
    early, early_send, send = fold((early, got, 0), after=got2, through=[send])
    early_got = ring.first(early_send)
    got = ring.last(send)
    weights = [(qkv, step), (more, (pairs - 1) * step)]
    part = input_back(ring, xs, mids, grads, weights, after=[early])
    rows = [slice(0, xs[0].shape[0]), slice(xs[0].shape[0], None)]

    def sums_of(fields):
        return [sum(f[r].astype(F32) for f in fields).astype(BF) for r in rows]

    early, *made = fold(
        (early, early_got, 1), (keep, got, 0), through=[part]
    )
    sends, (keep, send, part) = made[: quarter - 1], made[quarter - 1 :]
    early = [early, *ring.far_all(sends)]
    got = ring.first(send)
    parts = [part] + ring.exchange(part)
    ys = sums_of(outs)
    keep, *sends, part = fold((keep, got, 1), after=ys, through=[parts[0]])
    late = [keep, *ring.far_all(sends)]
    grad_xs = sums_of([part] + parts[1:])
    plan = [
        [(0, 0, units), (1, 0, units)],
        [(0, units, 2 * units), (1, units, 2 * units)],
    ]
    grad_in, grad_ff, gain_f = final(
        [[keep1, *got1], [keep2, *got2]], plan, [0], col_f, [in_weight], after=grad_xs
    )
    plan = [
        [(0, p * step + i * LANES, p * step + (i + 1) * LANES) for p in range(pairs - 1)]
        + [(1, i * LANES, (i + 1) * LANES)]
        for i in range(3)
    ]
    plan += [[(0, (pairs - 1) * step, (pairs - 1) * step + cols)], [(1, step, step + LANES)]]
    gq, gk, gv, grad_o, sums, gain = final(
        [early, late], plan, [0, 1, 2], col_a, padded[:3], carry=[gain_f]
    )
    for other in ring.exchange(gain):
        gain = gain + other
    return (
        ys[0].reshape(x_short.shape),
        ys[1].reshape(x_long.shape),
        grad_xs[0].reshape(x_short.shape),
        grad_xs[1].reshape(x_long.shape),
        gq[:, :real],
        gk[:, :real],
        gv[:, :real],
        grad_o[:, :real],
        grad_in,
        grad_ff,
        gain[:, 0],
        gain[:, 1],
        sums[:heads, :buckets].T,
    )


def solution(mesh):
    sizes = (mesh.shape["dp"], mesh.shape["mp"])
    return jax.shard_map(
        functools.partial(on_device, sizes),
        mesh=mesh,
        in_specs=(
            P("dp", None, None),
            P("dp", None, None),
            P("dp"),
            P("dp"),
            P(),
            P("dp", "mp"),
            P("dp", "mp"),
            P("dp", "mp"),
            P("dp", "mp"),
            P("dp", "mp"),
            P("dp", "mp"),
            P("dp"),
            P("dp"),
            P(None, "mp"),
            P("dp", None, None),
            P("dp", None, None),
        ),
        out_specs=(
            P("dp", None, None),
            P("dp", None, None),
            P("dp", None, None),
            P("dp", None, None),
            P("dp", "mp"),
            P("dp", "mp"),
            P("dp", "mp"),
            P("dp", "mp"),
            P("dp", "mp"),
            P("dp", "mp"),
            P("dp"),
            P("dp"),
            P(None, "mp"),
        ),
        check_vma=False,
    )
```

```python
import functools

import jax
import jax.numpy as jnp
from jax import lax
from jax.experimental import pallas as pl
from jax.experimental.pallas import tpu as pltpu
from jax.sharding import PartitionSpec as P

DH = 64
LANES = 128
EPS = 1e-06
NEG = -1000000000.0
BF = jnp.bfloat16
F32 = jnp.float32
ANY = pl.BlockSpec(memory_space=pl.ANY)
SMEM = pl.BlockSpec(memory_space=pltpu.SMEM)
VMEM = pl.BlockSpec(memory_space=pltpu.VMEM)


def dot(left, right):
    return jnp.dot(left, right, preferred_element_type=F32)


def dot_rows(left, right):
    return lax.dot_general(left, right, (((0,), (0,)), ((), ())), preferred_element_type=F32)


def dot_cols(left, right):
    return lax.dot_general(left, right, (((1,), (1,)), ((), ())), preferred_element_type=F32)


def tiles(array, rows):
    return pl.BlockSpec((rows,) + array.shape[1:], lambda i: (i,) + (0,) * (len(array.shape) - 1))


def fixed(array):
    return pl.BlockSpec(array.shape, lambda i: (0,) * len(array.shape))


def pair_tiles(pair, rows):
    count = pair[0].shape[0] // rows
    rest = (0,) * (pair[0].ndim - 1)
    shape = (rows,) + pair[0].shape[1:]
    return [
        pl.BlockSpec(shape, lambda i: (jnp.minimum(i, count - 1),) + rest),
        pl.BlockSpec(shape, lambda i: (jnp.maximum(i - count, 0),) + rest),
    ]


def pick(count, first, second):
    return jnp.where(pl.program_id(0) < count, first[...], second[...])


def out_of(shape, kind):
    return jax.ShapeDtypeStruct(tuple(shape), kind)


MARKS = {}


def mark_of(array):
    return MARKS[id(array)][1] if id(array) in MARKS else array


def call(kernel, outs, args, *, ins=None, out_specs=None, grid=None, scratch=(), mib=4, after=(), through=()):
    ins = list(ins or [VMEM] * len(args))
    out_specs = list(out_specs or [VMEM] * len(outs))
    extra = {} if grid is None else {"grid": grid}
    after = list({id(m): m for m in map(mark_of, after)}.values())
    idle = len(after) + len(through)
    mark = out_of((8, LANES), F32)

    def body(*refs):
        given, made = refs[: len(args)], refs[len(args) + idle :]
        made[len(outs)][...] = jnp.zeros((8, LANES), F32)
        kernel(*given, *made[: len(outs)], *made[len(outs) + 1 + len(through) :])

    made = list(
        pl.pallas_call(
        body,
        out_shape=list(outs) + [mark] + [out_of(t.shape, t.dtype) for t in through],
        in_specs=ins + [ANY] * idle,
        out_specs=out_specs + [VMEM if grid is None else fixed(mark)] + [ANY] * len(through),
        scratch_shapes=list(scratch),
        compiler_params=pltpu.CompilerParams(vmem_limit_bytes=mib << 20),
        input_output_aliases={
            len(args) + len(after) + i: len(outs) + 1 + i for i in range(len(through))
        },
        cost_estimate=pl.CostEstimate(flops=1000, bytes_accessed=1000, transcendentals=0),
        **extra,
    )(*args, *after, *through)
    )
    mark = made.pop(len(outs))
    for array in made:
        MARKS[id(array)] = (array, mark)
    return made


class Ring:
    def __init__(self, sizes):
        self.dp, self.mp = sizes
        self.me = lax.axis_index("dp")
        self.odd = lax.axis_index("mp") & 1
        self.quarter = self.dp // 4
        j = jnp.arange(self.dp, dtype=jnp.int32)
        first = (j // self.quarter) & 1
        last = j // (2 * self.quarter)

        def order(odd):
            low = jnp.where(odd == 0, first + 2 * last, 2 * first + last)
            return self.me ^ (4 * (j % self.quarter) + low)

        self.order = order(self.odd)
        self.orders = [order(self.odd ^ (k & 1)) for k in range(1, self.mp)]
        rel = self.me ^ j
        bit0, bit1 = rel & 1, (rel >> 1) & 1
        first, last = jnp.where(self.odd == 0, bit0, bit1), jnp.where(self.odd == 0, bit1, bit0)
        self.spots = (rel >> 2) + self.quarter * (first + 2 * last)
        lead = (lax.axis_index("mp") == 0).astype(jnp.int32)
        self.places = jnp.concatenate([self.order, lead[None]])

    def far(self, array):
        return [
            lax.ppermute(array, "dp", [(i, i ^ (4 * step)) for i in range(self.dp)])
            for step in range(1, self.quarter)
        ]

    def far_all(self, arrays):
        return [
            lax.ppermute(a, "dp", [(i, i ^ (4 * (step + 1))) for i in range(self.dp)])
            for step, a in enumerate(arrays)
        ]

    def near(self, array, masks):
        pairs = [
            (i * self.mp + c, (i ^ masks[c & 1]) * self.mp + c)
            for i in range(self.dp)
            for c in range(self.mp)
        ]
        return lax.ppermute(array, ("dp", "mp"), pairs)

    def first(self, array):
        return self.near(array, (1, 2))

    def last(self, array):
        return self.near(array, (2, 1))

    def exchange(self, array):
        return [
            lax.ppermute(array, "mp", [(i, i ^ k) for i in range(self.mp)])
            for k in range(1, self.mp)
        ]


def join_kernel(plan, *refs):
    sources, outs = refs[: -len(plan)], refs[-len(plan) :]
    for (chosen, start, stop), out in zip(plan, outs):
        at = 0
        for i in chosen:
            count = sources[i].shape[0]
            out[at : at + count] = sources[i][:, :, start:stop]
            at += count


def join(arrays, plan, after=(), through=()):
    outs = []
    for chosen, start, stop in plan:
        count = sum(arrays[i].shape[0] for i in chosen)
        outs.append(out_of((count, arrays[0].shape[1], stop - start), arrays[0].dtype))
    return call(functools.partial(join_kernel, plan), outs, arrays, after=after, through=through)


def aligned(rows):
    return rows % 16 == 0


def blocks_of(ring, held, got):
    if aligned(held.shape[1]):
        return (held, got)
    blocks = jnp.take(jnp.concatenate([held, got], 0), ring.spots, axis=0)
    return (blocks.reshape((-1,) + held.shape[2:]),)


def load(places, sources, to, at):
    there = slice(at, at + sources[0].shape[-1])
    if len(sources) == 2:
        half, rows, _ = sources[0].shape
        for j in range(2 * half):
            row = pl.multiple_of(places[j] * rows, 16)
            to[pl.ds(row, rows), there] = sources[j // half][j % half]
    else:
        to[:, there] = sources[0][...]
    return there.stop


def columns(array, at, count):
    first = (0,) * (array.ndim - 1)
    return pl.BlockSpec(
        array.shape[:-1] + (count,),
        lambda i: first + (at // count,),
        pipeline_mode=pl.Buffered(1),
    )


def emit(places, total, keep, send, extra=None):
    half, rows, _ = keep.shape
    for j in range(2 * half):
        at = pl.multiple_of(places[j] * rows, 16)
        block = total[pl.ds(at, rows), :]
        if extra is not None:
            block = block + extra
        if j < half:
            keep[j] = block
        else:
            send[j - half] = block.astype(BF)


def emitted(ring, rows, cols):
    share = rows // ring.dp
    if aligned(share):
        shape = (ring.dp // 2, share, cols)
        return [out_of(shape, F32), out_of(shape, BF)]
    return [out_of((rows, cols), F32)]


def halves(ring, outs, extra=None):
    if len(outs) == 2:
        return outs
    blocks = outs[0].reshape(ring.dp, -1, outs[0].shape[1])
    if extra is not None:
        blocks = blocks + extra
    blocks = jnp.take(blocks, ring.order, axis=0)
    return blocks[: ring.dp // 2], blocks[ring.dp // 2 :].astype(BF)


def fold_kernel(modes, *refs):
    ins, outs = refs[: 2 * len(modes)], refs[2 * len(modes) :]
    for mode in modes:
        keep, got = ins[:2]
        ins = ins[2:]
        count = got.shape[0] if mode else got.shape[0] // 2
        if mode:
            outs[0][...] = keep[0] + got[0].astype(F32)
            for j in range(1, count):
                outs[j][...] = (keep[j] + got[j].astype(F32)).astype(BF)
            outs = outs[count:]
        else:
            outs[0][...] = keep[:count] + got[:count].astype(F32)
            outs[1][...] = (keep[count:] + got[count:].astype(F32)).astype(BF)
            outs = outs[2:]


def fold(*items, after=(), through=()):
    outs = []
    args = []
    for keep, got, mode in items:
        args += [keep, got]
        if mode:
            shape = keep.shape[1:]
            outs += [out_of(shape, F32)] + [out_of(shape, BF)] * (keep.shape[0] - 1)
        else:
            shape = (keep.shape[0] // 2,) + keep.shape[1:]
            outs += [out_of(shape, F32), out_of(shape, BF)]
    kernel = functools.partial(fold_kernel, [m for *_, m in items])
    return call(kernel, outs, args, after=after, through=through)


def final_kernel(counts, plan, scaled, carried, gain_ref, *refs):
    carry, refs = refs[:carried], refs[carried:]
    weights, refs = refs[: len(scaled)], refs[len(scaled) :]
    fields = []
    for count in counts:
        total = refs[0][...]
        for r in refs[1:count]:
            total = total + r[...].astype(F32)
        fields.append(total)
        refs = refs[count:]
    outs, gain_out = refs[:-1], refs[-1]
    sums = jnp.zeros(gain_out.shape, F32)
    for i, (out, spans) in enumerate(zip(outs, plan)):
        at = 0
        for f, start, stop in spans:
            value = fields[f][:, start:stop]
            there = slice(at, at + stop - start)
            if i in scaled:
                kept = weights[scaled.index(i)][:, there].astype(F32)
                sums += jnp.sum(value * kept, 1, keepdims=True)
                value = value * gain_ref[...]
            out[:, there] = value
            at += stop - start
    if carried:
        lane = lax.broadcasted_iota(jnp.int32, sums.shape, 1)
        sums = jnp.where(lane == 0, sums, carry[0][...])
    gain_out[...] = sums


def final(items, plan, scaled, gain, weights, carry=(), after=()):
    rows = gain.shape[0]
    outs = [out_of((rows, sum(b - a for _, a, b in spans)), F32) for spans in plan]
    outs.append(out_of((rows, LANES), F32))
    kernel = functools.partial(final_kernel, [len(i) for i in items], plan, scaled, len(carry))
    args = [gain, *carry, *weights, *[a for i in items for a in i]]
    return call(kernel, outs, args, after=after)


def distance_buckets(bounds_ref, dist, buckets):
    size = jnp.abs(dist)
    half = jnp.zeros(dist.shape, jnp.int32)
    for b in range(bounds_ref.shape[0]):
        half += (size >= bounds_ref[b]).astype(jnp.int32)
    return half + jnp.where(dist > 0, buckets // 2, 0)


def bases_kernel(bounds_ref, table_ref, near_ref, far_ref):
    heads, _, width = near_ref.shape
    buckets = table_ref.shape[1]
    row = lax.broadcasted_iota(jnp.int32, (8, width), 0)
    for to, sign in ((near_ref, 1), (far_ref, -1)):
        dist = sign * (lax.broadcasted_iota(jnp.int32, (8, width), 1) - width // 2)
        marks = distance_buckets(bounds_ref, dist, buckets)
        marks = jnp.concatenate([marks] * (buckets // 8), 0)
        onehot = (marks == lax.broadcasted_iota(jnp.int32, (buckets, width), 0)).astype(F32)
        line = dot(table_ref[...], onehot.astype(BF))
        for h in range(heads):
            field = jnp.broadcast_to(line[h : h + 1], (8, width))
            for k in (1, 2, 4):
                field = jnp.where((row & k) != 0, pltpu.roll(field, k, 1), field)
            while field.shape[0] < LANES:
                field = jnp.concatenate([field, pltpu.roll(field, field.shape[0], 1)], 0)
            to[h] = field.astype(BF)


def bias_bases(boundaries, table, heads, width, after=()):
    shape = out_of((heads, LANES, width), BF)
    return call(
        bases_kernel, [shape, shape], [boundaries, table], ins=[SMEM, VMEM], mib=16, after=after
    )


def bucket_field(bounds_ref, fields, buckets, first):
    width = fields[0].shape[-1]
    dist = width // 2 - lax.broadcasted_iota(jnp.int32, (8, width), 1)
    marks = distance_buckets(bounds_ref, dist, buckets)
    row = lax.broadcasted_iota(jnp.int32, (8, width), 0)
    line = jnp.zeros((8, width), F32)
    for h, field in enumerate(fields, first):
        while field.shape[0] > 8:
            half = field.shape[0] // 2
            field = field[:half] + pltpu.roll(field[half:], width - half, 1)
        for k in (4, 2, 1):
            field = jnp.where((row & k) != 0, pltpu.roll(field, width - k, 1), field)
        line = jnp.where(row == h, jnp.sum(field, 0, keepdims=True), line)
    lane = lax.broadcasted_iota(jnp.int32, (8, LANES), 1)
    out = jnp.zeros((8, LANES), F32)
    for b in range(buckets):
        total = jnp.sum(jnp.where(marks == b, line, 0.0), 1, keepdims=True)
        out = jnp.where(lane == b, total, out)
    return out


def split_low(values, lane, off, rest):
    high = values.astype(BF).astype(F32)
    mid = (values - high).astype(BF).astype(F32)
    low = values - high - mid
    return jnp.where(
        lane == off,
        high,
        jnp.where(lane == off + 1, mid, jnp.where(lane == off + 2, low, rest)),
    )


def three_ones(lane, off):
    return jnp.where((lane >= off) & (lane < off + 3), 1.0, 0.0)


def slots_of(batches):
    at = 0
    for b, (slots, length) in enumerate(batches):
        for s in range(slots):
            yield b, s, length, slice(at, at + length)
            at += length


def attend_kernel(batches, halves, *refs):
    places, lens = refs[0], refs[1 : 1 + len(batches)]
    refs = refs[1 + len(batches) :]
    normed_ref, near_ref = refs[:2]
    sources = refs[2 : 2 + halves]
    aug_ref, k_ref, v_ref, o_ref, w_scr = refs[2 + halves :]
    width = near_ref.shape[-1]
    load(places, sources, w_scr, 0)
    for b, s, length, span in slots_of(batches):
        valid = lens[b][s]
        lane = lax.broadcasted_iota(jnp.int32, (length, LANES), 1)
        place = lax.broadcasted_iota(jnp.int32, (length, LANES), 0)
        masked = jnp.where(place >= valid, NEG, 0.0)
        qkv = dot(normed_ref[span, :], w_scr[...])
        q, k, v = (qkv[:, i * LANES : (i + 1) * LANES] for i in range(3))
        k_ref[span, :] = k.astype(BF)
        v_ref[span, :] = v.astype(BF)
        mixed = []
        for e in range(2):
            own = (lane >= DH) == (e == 1)
            off = DH * (1 - e)
            marker = jnp.where(lane == off + 3, 1.0, 0.0)
            q_own = jnp.where(own, q, marker).astype(BF)
            k_own = jnp.where(own, k, jnp.where(lane == off + 3, masked, 0.0)).astype(BF)
            v_own = jnp.where(own, v, 1.0).astype(BF)
            start = width // 2
            bias = [
                near_ref[e, :, start - a * LANES : start - a * LANES + length]
                for a in range(length // LANES)
            ]
            scores = dot_cols(q_own, k_own) + jnp.concatenate(bias, 0).astype(F32)
            top = jnp.max(scores, 1, keepdims=True)
            expo = jnp.exp(scores - top)
            sums = dot(expo.astype(BF), v_own)
            total = jnp.where(own, pltpu.roll(sums, DH, 1), sums)
            logsum = top + jnp.log(total)
            extra = split_low(-logsum, lane, off, marker)
            aug_ref[span, e * LANES : (e + 1) * LANES] = jnp.where(own, q, extra).astype(BF)
            mixed.append(sums / total)
        o_ref[span, :] = jnp.where(lane < DH, mixed[0], mixed[1]).astype(BF)


def pair_of(base, pair):
    return pl.BlockSpec((2,) + base.shape[1:], lambda i: (pair, 0, 0))


def attend(ring, batches, lens, near, unit, weights, at, pair, after=()):
    rows, width = unit.shape
    shapes = [out_of((rows, c * LANES), BF) for c in (2, 1, 1, 1)]
    return call(
        functools.partial(attend_kernel, batches, len(weights)),
        shapes,
        [ring.places, *lens, unit, near, *weights],
        ins=[SMEM] * (1 + len(lens))
        + [fixed(unit), pair_of(near, pair)]
        + [columns(w, at, 3 * LANES) for w in weights],
        out_specs=[fixed(s) for s in shapes],
        grid=(1,),
        scratch=[pltpu.VMEM((width, 3 * LANES), BF)],
        mib=16,
        after=after,
    )


def attend_back_kernel(batches, pair, buckets, before, priors, emits, *refs):
    lens, refs = refs[: len(batches)], refs[len(batches) :]
    bounds, places, unit_ref, go_ref, aug_ref, k_ref, v_ref, o_ref, far_ref = refs[:9]
    totals, (table_in, grads_ref, table_ref) = refs[9 : 9 + priors], refs[9 + priors : 12 + priors]
    outs, (gbase_ref, total) = refs[12 + priors : -2], refs[-2:]
    width = far_ref.shape[-1]
    gbase_ref[...] = jnp.zeros_like(gbase_ref)
    for b, s, length, span in slots_of(batches):
        valid = lens[b][s]
        lane = lax.broadcasted_iota(jnp.int32, (length, LANES), 1)
        place = lax.broadcasted_iota(jnp.int32, (length, LANES), 0)
        masked = jnp.where(place >= valid, NEG, 0.0)
        k = k_ref[span, :].astype(F32)
        v = v_ref[span, :].astype(F32)
        go = go_ref[span, :].astype(F32)
        both = go * o_ref[span, :].astype(F32)
        grads = []
        for e in range(2):
            own = (lane >= DH) == (e == 1)
            off = DH * (1 - e)
            q_own = aug_ref[span, e * LANES : (e + 1) * LANES]
            ones = three_ones(lane, off)
            k_own = jnp.where(own, k, jnp.where(lane == off + 3, masked, ones)).astype(BF)
            v_own = jnp.where(own, v, ones).astype(BF)
            delta = jnp.sum(jnp.where(own, both, 0.0), 1, keepdims=True)
            g_own = jnp.where(own, go, split_low(-delta, lane, off, 0.0)).astype(BF)
            cols = [
                slice(width // 2 - a * LANES, width // 2 - a * LANES + length)
                for a in range(length // LANES)
            ]
            bias = jnp.concatenate([far_ref[e, :, c] for c in cols], 0)
            probs = jnp.exp(dot_cols(k_own, q_own) + bias.astype(F32))
            ds = probs * dot_cols(v_own, g_own)
            for a, c in enumerate(cols):
                gbase_ref[e, :, c] += ds[a * LANES : (a + 1) * LANES]
            ds = ds.astype(BF)
            gv = dot(probs.astype(BF), g_own)
            grads.append((dot_rows(ds, k_own), dot(ds, q_own), gv))
        first = lane < DH
        for i, (a, b) in enumerate(zip(*grads)):
            grads_ref[span, i * LANES : (i + 1) * LANES] = jnp.where(first, a, b).astype(BF)
    table = table_in[...] + bucket_field(
        bounds, [gbase_ref[0], gbase_ref[1]], buckets, 2 * pair
    )
    table_ref[...] = table
    part = dot_rows(unit_ref[...], grads_ref[...])
    if not emits:
        outs[0][...] = part
        return
    step = 3 * LANES
    at = 0
    for value in [r[...] for r in totals[:before]] + [part] + [r[...] for r in totals[before:]]:
        total[:, at : at + value.shape[1]] = value
        at += value.shape[1]
    extra = None
    if total.shape[1] > at:
        total[:, at:] = jnp.zeros((total.shape[0], LANES), F32)
    if total.shape[1] > at and emits == 2:
        rows = outs[0].shape[1]
        extra = jnp.concatenate([table, jnp.zeros((rows - 8, LANES), F32)], 0)
        extra = jnp.concatenate([jnp.zeros((rows, at), F32), extra], 1)
    if emits == 2:
        emit(places, total, *outs, extra=extra)
    else:
        outs[0][...] = total[...]


def attend_back(
    ring, batches, lens, boundaries, buckets, far, unit, go, fwd, pair, table, before, rest, last, after=()
):
    rows, width = unit.shape
    step = 3 * LANES
    go_spec = pl.BlockSpec((rows, LANES), lambda i: (0, pair))
    given = rest is None
    priors = [] if given else [*before, *rest]
    cols = step + sum(p.shape[1] for p in priors) + (LANES if last else 0)
    outs = [out_of((rows, step), BF), out_of((8, LANES), F32)]
    made = [out_of((width, step), F32)] if given else emitted(ring, width, cols)
    emits = 0 if given else len(made)
    kernel = functools.partial(
        attend_back_kernel, batches, pair, buckets, len(before), len(priors), emits
    )
    grads, table, *made = call(
        kernel,
        outs + made,
        [*lens, boundaries, ring.places, unit, go, *fwd, far, *priors, table],
        ins=[SMEM] * (len(lens) + 2)
        + [fixed(unit), go_spec]
        + [fixed(a) for a in fwd]
        + [pair_of(far, pair)]
        + [fixed(a) for a in (*priors, table)],
        out_specs=[fixed(o) for o in outs + made],
        grid=(1,),
        scratch=[
            pltpu.VMEM((2,) + far.shape[1:], F32),
            pltpu.VMEM((8, LANES) if given else (width, cols), F32),
        ],
        mib=24,
        after=after,
    )
    if not given:
        share = width // ring.dp
        extra = jnp.pad(table, ((0, share - 8), (cols - LANES, 0))) if last else None
        made = halves(ring, made, extra)
    return grads, table, made


def rms_parts(field):
    scale = lax.rsqrt(jnp.mean(field * field, -1, keepdims=True) + EPS)
    return (scale, field * scale)


def norm_back(grad_unit, unit, scale):
    return scale * (grad_unit - unit * jnp.mean(grad_unit * unit, -1, keepdims=True))


def norm_kernel(count, short_ref, long_ref, unit_ref):
    unit_ref[...] = rms_parts(pick(count, short_ref, long_ref).astype(F32))[1].astype(BF)


def norm(xs, tile=512, after=()):
    out = out_of((xs[0].shape[0] + xs[1].shape[0], xs[0].shape[1]), BF)
    return call(
        functools.partial(norm_kernel, xs[0].shape[0] // tile),
        [out],
        xs,
        ins=pair_tiles(xs, tile),
        out_specs=[tiles(out, tile)],
        grid=(out.shape[0] // tile,),
        mib=8,
        after=after,
    )[0]


def sum_of(refs):
    total = refs[0][...].astype(F32)
    for r in refs[1:]:
        total = total + r[...].astype(F32)
    return total


def gelu_parts(x):
    c = 0.7978845608028654
    d = c * 0.044715
    square = x * x
    t = jnp.tanh(x * (c + d * square))
    half = 0.5 + 0.5 * t
    slope = half + (0.5 * x) * (1.0 - t * t) * (c + 3.0 * d * square)
    return x * half, slope


def ffn_first_kernel(halves, groups, pairs, emits, count, places, *refs):
    all_places, refs = [places, places, *refs[: groups - 1]], refs[groups - 1 :]
    g_refs, x_refs, refs = refs[:2], refs[2:4], refs[4:]
    o_refs, refs = refs[: groups * pairs], refs[groups * pairs :]
    sources, refs = refs[:halves], refs[halves:]
    unit_ref, scale_ref, out_ref, gn_ref = refs[:4]
    grads, (w_scr, total) = refs[4 : 4 + emits], refs[4 + emits :]
    units = total.shape[1] // 2
    step = pl.program_id(0)

    @pl.when(step == 0)
    def _():
        total[...] = jnp.zeros_like(total)
        at = 0
        count = halves // (1 + groups)
        for i, there in enumerate(all_places):
            at = load(there, sources[i * count : (i + 1) * count], w_scr, at)

    mixed = jnp.concatenate([r[...] for r in o_refs], 1)
    middle = pick(count, *x_refs).astype(F32) + dot_cols(mixed, w_scr[:, 2 * units :])
    scale, unit = rms_parts(middle)
    unit = unit.astype(BF)
    unit_ref[...] = unit
    scale_ref[...] = jnp.broadcast_to(scale, scale_ref.shape)
    g = pick(count, *g_refs)
    win, wout = w_scr[:, :units], w_scr[:, units : 2 * units]
    act, slope = gelu_parts(dot(unit, win))
    act = act.astype(BF)
    gpre = (dot(g, wout) * slope).astype(BF)
    lead = places[places.shape[0] - 1].astype(F32)
    out_ref[...] = (dot_cols(act, wout) + lead * middle).astype(BF)
    gn_ref[...] = dot_cols(gpre, win).astype(BF)
    total[:, :units] += dot_rows(unit, gpre)
    total[:, units:] += dot_rows(g, act)

    @pl.when(step == pl.num_programs(0) - 1)
    def _():
        if emits == 2:
            emit(places, total, *grads)
        else:
            grads[0][...] = total[...]


def ffn_first(ring, gs, xs, mixed, weights, out_weights, units, tile=512, after=()):
    rows = mixed[0].shape[0]
    width = xs[0].shape[1]
    groups = len(out_weights)
    pairs = len(mixed) // groups
    field = out_of((rows, width), BF)
    outs = [field, out_of((rows, LANES), F32), field, field]
    grads = emitted(ring, width, 2 * units)
    sources = [*weights, *[w for ws in out_weights for w in ws]]
    kernel = functools.partial(
        ffn_first_kernel, len(sources), groups, pairs, len(grads), xs[0].shape[0] // tile
    )
    return call(
        kernel,
        outs + grads,
        [ring.places, *ring.orders, *gs, *xs, *mixed, *sources],
        ins=[SMEM] * groups
        + pair_tiles(gs, tile)
        + pair_tiles(xs, tile)
        + [tiles(a, tile) for a in mixed]
        + [columns(w, 0, w.shape[-1]) for w in sources],
        out_specs=[tiles(o, tile) for o in outs] + [fixed(o) for o in grads],
        grid=(rows // tile,),
        scratch=[
            pltpu.VMEM((width, 2 * units + len(mixed) * LANES), BF),
            pltpu.VMEM((width, 2 * units), F32),
        ],
        mib=46,
        after=after,
    )


def ffn_next_kernel(halves, count, places, unit_ref, scale_ref, *refs):
    g_refs, (out_in, gn_in), refs = refs[:2], refs[2:4], refs[4:]
    sources, refs = refs[:halves], refs[halves:]
    out_ref, mid_ref, act_ref, gpre_ref, w_scr = refs
    units = w_scr.shape[1] // 2

    @pl.when(pl.program_id(0) == 0)
    def _():
        load(places, sources, w_scr, 0)

    win, wout = w_scr[:, :units], w_scr[:, units:]
    unit = unit_ref[...]
    g = pick(count, *g_refs)
    act, slope = gelu_parts(dot(unit, win))
    act = act.astype(BF)
    gpre = (dot(g, wout) * slope).astype(BF)
    act_ref[...] = act
    gpre_ref[...] = gpre
    out_ref[...] = (out_in[...] + dot_cols(act, wout)).astype(BF)
    lead = places[places.shape[0] - 1].astype(F32)
    back = norm_back(gn_in[...] + dot_cols(gpre, win), unit.astype(F32), scale_ref[:, :1])
    mid_ref[...] = (back + lead * g.astype(F32)).astype(BF)


def ffn_next(ring, unit, scale, gs, out, gn, weights, units, tile=512, after=()):
    rows, width = unit.shape
    outs = [out_of((rows, width), BF)] * 2 + [out_of((rows, units), BF)] * 2
    return call(
        functools.partial(ffn_next_kernel, len(weights), gs[0].shape[0] // tile),
        outs,
        [ring.places, unit, scale, *gs, out, gn, *weights],
        ins=[SMEM, tiles(unit, tile), tiles(scale, tile)]
        + pair_tiles(gs, tile)
        + [tiles(out, tile), tiles(gn, tile)]
        + [columns(w, 0, w.shape[-1]) for w in weights],
        out_specs=[tiles(o, tile) for o in outs],
        grid=(rows // tile,),
        scratch=[pltpu.VMEM((width, 2 * units), BF)],
        mib=40,
        after=after,
    )


def ffn_grads_kernel(emits, count, places, unit_ref, *refs):
    g_refs, (gpre_ref, act_ref) = refs[:2], refs[2:4]
    grads, total = refs[4:-1], refs[-1]
    step = pl.program_id(0)
    units = act_ref.shape[1]

    @pl.when(step == 0)
    def _():
        total[...] = jnp.zeros_like(total)

    total[:, :units] += dot_rows(unit_ref[...], gpre_ref[...])
    total[:, units:] += dot_rows(pick(count, *g_refs), act_ref[...])

    @pl.when(step == pl.num_programs(0) - 1)
    def _():
        if emits == 2:
            emit(places, total, *grads)
        else:
            grads[0][...] = total[...]


def ffn_grads(ring, unit, gs, gpre, act, tile=512, after=()):
    rows, width = unit.shape
    cols = 2 * act.shape[1]
    outs = emitted(ring, width, cols)
    return call(
        functools.partial(ffn_grads_kernel, len(outs), gs[0].shape[0] // tile),
        outs,
        [ring.places, unit, *gs, gpre, act],
        ins=[SMEM, tiles(unit, tile)]
        + pair_tiles(gs, tile)
        + [tiles(gpre, tile), tiles(act, tile)],
        out_specs=[fixed(o) for o in outs],
        grid=(rows // tile,),
        scratch=[pltpu.VMEM((width, cols), F32)],
        mib=32,
        after=after,
    )


def middle_kernel(halves, groups, pairs, places, *refs):
    mid_refs, refs = refs[:groups], refs[groups:]
    o_refs, refs = refs[:pairs], refs[pairs:]
    sources, (go_ref, total_ref, w_scr) = refs[:halves], refs[halves:]
    step = pl.program_id(0)

    @pl.when(step == 0)
    def _():
        total_ref[...] = jnp.zeros_like(total_ref)
        load(places, sources, w_scr, 0)

    grad = sum_of(mid_refs).astype(BF)
    go_ref[...] = dot(grad, w_scr[...]).astype(BF)
    total_ref[...] += dot_rows(grad, jnp.concatenate([r[...] for r in o_refs], 1))


def middle_back(ring, mids, mixed, weights, tile=512, after=()):
    rows, width = mids[0].shape
    pairs = len(mixed)
    cols = pairs * LANES
    go, total = out_of((rows, cols), BF), out_of((width, cols), F32)
    return call(
        functools.partial(middle_kernel, len(weights), len(mids), pairs),
        [go, total],
        [ring.places, *mids, *mixed, *weights],
        ins=[SMEM]
        + [tiles(a, tile) for a in (*mids, *mixed)]
        + [columns(w, 0, cols) for w in weights],
        out_specs=[tiles(go, tile), fixed(total)],
        grid=(rows // tile,),
        scratch=[pltpu.VMEM((width, cols), BF)],
        mib=24,
        after=after,
    )


def input_back_kernel(halves, groups, pairs, count, places, short_ref, long_ref, *refs):
    mid_refs, refs = refs[:groups], refs[groups:]
    g_refs, refs = refs[:pairs], refs[pairs:]
    sources, (part_ref, w_scr) = refs[:-2], refs[-2:]

    @pl.when(pl.program_id(0) == 0)
    def _():
        at = 0
        for i in range(0, len(sources), halves):
            at = load(places, sources[i : i + halves], w_scr, at)

    part = dot_cols(jnp.concatenate([r[...] for r in g_refs], 1), w_scr[...])
    scale, unit = rms_parts(pick(count, short_ref, long_ref).astype(F32))
    lead = places[places.shape[0] - 1].astype(F32)
    part_ref[...] = (norm_back(part, unit, scale) + lead * sum_of(mid_refs)).astype(BF)


def input_back(ring, xs, mids, grads, weights, tile=512, after=()):
    rows, width = grads[0].shape[0], xs[0].shape[1]
    pairs = len(grads)
    out = out_of((rows, width), BF)
    return call(
        functools.partial(
            input_back_kernel, len(weights[0][0]), len(mids), pairs, xs[0].shape[0] // tile
        ),
        [out],
        [ring.places, *xs, *mids, *grads, *[a for blocks, _ in weights for a in blocks]],
        ins=[SMEM]
        + pair_tiles(xs, tile)
        + [tiles(a, tile) for a in (*mids, *grads)]
        + [columns(a, 0, count) for blocks, count in weights for a in blocks],
        out_specs=[tiles(out, tile)],
        grid=(rows // tile,),
        scratch=[pltpu.VMEM((width, 3 * pairs * LANES), BF)],
        mib=20,
        after=after,
    )[0]


def pad_cols(array, cols):
    return jnp.pad(array, ((0, 0), (0, cols - array.shape[1]))) if cols > array.shape[1] else array


def on_device(
    sizes,
    x_short,
    x_long,
    len_short,
    len_long,
    boundaries,
    q_weight,
    k_weight,
    v_weight,
    out_weight,
    in_weight,
    ff_out_weight,
    attn_gain,
    ffn_gain,
    bias_table,
    cot_short,
    cot_long,
):
    MARKS.clear()
    ring = Ring(sizes)
    quarter = ring.quarter
    width = x_short.shape[2]
    buckets, heads = bias_table.shape
    real = heads * DH
    cols = -(-real // LANES) * LANES
    pairs = cols // LANES
    units = in_weight.shape[1] // 2
    batches = [x.shape[:2] for x in (x_short, x_long)]
    lens = (len_short, len_long)

    xs = [x.reshape(-1, width) for x in (x_short, x_long)]
    gs = [g.reshape(-1, width) for g in (cot_short, cot_long)]

    col_a, col_f = (v.astype(F32)[:, None] for v in (attn_gain, ffn_gain))
    padded = [pad_cols(w, cols) for w in (q_weight, k_weight, v_weight, out_weight)]
    scaled = [(w.astype(F32) * col_a).astype(BF) for w in padded[:3]]
    pieces = [[w[:, p * LANES : (p + 1) * LANES] for w in scaled] for p in range(pairs)]
    own = jnp.concatenate([w for piece in pieces for w in piece] + [padded[3]], 1)[None]
    win = (in_weight.astype(F32) * col_f).astype(BF)
    own1, own2 = (
        jnp.concatenate([w[:, at : at + units] for w in (win, ff_out_weight)], 1)[None]
        for at in (0, units)
    )
    step = 3 * LANES
    z = tuple(range(quarter))
    table = jnp.pad(bias_table.T, ((0, 8 - heads), (0, 0)))

    two = (0, 1)
    wide = own.shape[2]
    got = ring.far(own)
    span = 2 * max(length for _, length in batches)
    near, far = bias_bases(boundaries, table, cols // DH, span, after=[own])
    held, own1 = join([own, *got], [(z, 0, wide)], after=[near], through=[own1])
    got = ring.first(held)
    got1 = ring.far(own1)
    unit = norm(xs, after=[held])
    plan = [(two, 0, step), (two, step, wide)]
    *helds, own2 = join([held, got], plan, after=[unit], through=[own2])
    qkv, more = [blocks_of(ring, h, ring.last(h)) for h in helds]
    out_at = (pairs - 1) * step
    out_w = [m[..., out_at:] for m in more]
    qkvs = [(qkv, 0)] + [(more, p * step) for p in range(pairs - 1)]
    out_ws = [out_w] + list(zip(*[ring.exchange(w) for w in out_w]))

    fwd = []
    after = helds
    for p in range(pairs):
        fwd.append(
            attend(ring, batches, lens, near, unit, *qkvs[p], p, after=after)
        )
        if p == 0:
            held1, own2 = join(
                [own1, *got1], [(z, 0, 2 * units)], after=[fwd[0][0]], through=[own2]
            )
            got1 = ring.first(held1)
            got2 = ring.far(own2)
            after = [held1, *out_w]
        if p == min(1, pairs - 1):
            z2 = tuple(2 + i for i in z)
            plan = [(two, 0, 2 * units), (z2, 0, 2 * units)]
            held1, held2 = join([held1, got1, own2, *got2], plan, after=[fwd[p][0]])
            got1, got2 = ring.last(held1), ring.first(held2)
            after = [held2]
    mixed = [f[3] for f in fwd]
    others = list(zip(*[ring.exchange(o) for o in mixed]))
    (held2,) = join([held2, got2], [(two, 0, 2 * units)], after=[fwd[-1][0]])
    got2 = ring.last(held2)
    first = blocks_of(ring, held1, got1)
    second = blocks_of(ring, held2, got2)

    unit_f, scale, out, gn, *grad1 = ffn_first(
        ring, gs, xs, [*mixed, *[o for g in others for o in g]], first, out_ws, units, after=[held2]
    )
    keep1, send = halves(ring, grad1)
    got1 = ring.last(send)
    out, mid, act, gpre = ffn_next(ring, unit_f, scale, gs, out, gn, second, units)
    keep1, send, mid, out = fold((keep1, got1, 0), through=[mid, out])
    mids = [mid] + ring.exchange(mid)
    outs = [out] + ring.exchange(out)
    got1 = ring.first(send)
    keep2, send2 = halves(ring, ffn_grads(ring, unit_f, gs, gpre, act, after=[keep1]))
    keep1, *sends, send2 = fold((keep1, got1, 1), after=[keep2], through=[send2])
    got1 = ring.far_all(sends)
    got2 = ring.last(send2)
    go, grad_o = middle_back(ring, mids, mixed, out_w, after=[keep1])

    grads = []
    totals = []
    sums = jnp.zeros((8, LANES), F32)
    after = [keep1]
    for p in range(pairs):
        last = p == pairs - 1
        before, rest = ((), ()) if last else (totals, [grad_o] if p == pairs - 2 else None)
        g, sums, made = attend_back(
            ring,
            batches,
            lens,
            boundaries,
            buckets,
            far,
            unit,
            go,
            fwd[p],
            p,
            sums,
            before,
            rest,
            last,
            after=after,
        )
        grads.append(g)
        if p < pairs - 2:
            totals.append(made[0])
        if p == 0:
            keep2, send2 = fold((keep2, got2, 0), after=[g])
            got2 = ring.first(send2)
            after = [keep2]
        if p == pairs - 2:
            early, send = made
            keep2, *sends, send = fold((keep2, got2, 1), after=[g, *got1], through=[send])
            got2 = ring.far_all(sends)
            got = ring.last(send)
            after = [keep2]
    keep, send = made
    early, early_send, send = fold((early, got, 0), after=got2, through=[send])
    early_got = ring.first(early_send)
    got = ring.last(send)
    weights = [(qkv, step), (more, (pairs - 1) * step)]
    part = input_back(ring, xs, mids, grads, weights, after=[early])
    rows = [slice(0, xs[0].shape[0]), slice(xs[0].shape[0], None)]

    def sums_of(fields):
        return [sum(f[r].astype(F32) for f in fields).astype(BF) for r in rows]

    early, *made = fold(
        (early, early_got, 1), (keep, got, 0), through=[part]
    )
    sends, (keep, send, part) = made[: quarter - 1], made[quarter - 1 :]
    early = [early, *ring.far_all(sends)]
    got = ring.first(send)
    parts = [part] + ring.exchange(part)
    keep, *sends, part, out = fold((keep, got, 1), after=[keep], through=[parts[0], outs[0]])
    ys = sums_of([out] + outs[1:])
    late = [keep, *ring.far_all(sends)]
    grad_xs = sums_of([part] + parts[1:])
    plan = [
        [(0, 0, units), (1, 0, units)],
        [(0, units, 2 * units), (1, units, 2 * units)],
    ]
    grad_in, grad_ff, gain_f = final(
        [[keep1, *got1], [keep2, *got2]], plan, [0], col_f, [in_weight], after=[*grad_xs, *ys]
    )
    plan = [
        [(0, p * step + i * LANES, p * step + (i + 1) * LANES) for p in range(pairs - 1)]
        + [(1, i * LANES, (i + 1) * LANES)]
        for i in range(3)
    ]
    plan += [[(0, (pairs - 1) * step, (pairs - 1) * step + cols)], [(1, step, step + LANES)]]
    gq, gk, gv, grad_o, sums, gain = final(
        [early, late], plan, [0, 1, 2], col_a, padded[:3], carry=[gain_f]
    )
    for other in ring.exchange(gain):
        gain = gain + other
    return (
        ys[0].reshape(x_short.shape),
        ys[1].reshape(x_long.shape),
        grad_xs[0].reshape(x_short.shape),
        grad_xs[1].reshape(x_long.shape),
        gq[:, :real],
        gk[:, :real],
        gv[:, :real],
        grad_o[:, :real],
        grad_in,
        grad_ff,
        gain[:, 0],
        gain[:, 1],
        sums[:heads, :buckets].T,
    )


def solution(mesh):
    sizes = (mesh.shape["dp"], mesh.shape["mp"])
    return jax.shard_map(
        functools.partial(on_device, sizes),
        mesh=mesh,
        in_specs=(
            P("dp", None, None),
            P("dp", None, None),
            P("dp"),
            P("dp"),
            P(),
            P("dp", "mp"),
            P("dp", "mp"),
            P("dp", "mp"),
            P("dp", "mp"),
            P("dp", "mp"),
            P("dp", "mp"),
            P("dp"),
            P("dp"),
            P(None, "mp"),
            P("dp", None, None),
            P("dp", None, None),
        ),
        out_specs=(
            P("dp", None, None),
            P("dp", None, None),
            P("dp", None, None),
            P("dp", None, None),
            P("dp", "mp"),
            P("dp", "mp"),
            P("dp", "mp"),
            P("dp", "mp"),
            P("dp", "mp"),
            P("dp", "mp"),
            P("dp"),
            P("dp"),
            P(None, "mp"),
        ),
        check_vma=False,
    )
```

```python
import functools

import jax
import jax.numpy as jnp
from jax import lax
from jax.experimental import pallas as pl
from jax.experimental.pallas import tpu as pltpu
from jax.sharding import PartitionSpec as P

DH = 64
LANES = 128
EPS = 1e-06
NEG = -1000000000.0
BF = jnp.bfloat16
C1 = 1.5
C2 = 6.0
F32 = jnp.float32
ANY = pl.BlockSpec(memory_space=pl.ANY)
SMEM = pl.BlockSpec(memory_space=pltpu.SMEM)
VMEM = pl.BlockSpec(memory_space=pltpu.VMEM)


def dot(left, right):
    return jnp.dot(left, right, preferred_element_type=F32)


def dot_rows(left, right):
    return lax.dot_general(left, right, (((0,), (0,)), ((), ())), preferred_element_type=F32)


def dot_cols(left, right):
    return lax.dot_general(left, right, (((1,), (1,)), ((), ())), preferred_element_type=F32)


def tiles(array, rows):
    return pl.BlockSpec((rows,) + array.shape[1:], lambda i: (i,) + (0,) * (len(array.shape) - 1))


def fixed(array):
    return pl.BlockSpec(array.shape, lambda i: (0,) * len(array.shape))


def pair_tiles(pair, rows):
    count = pair[0].shape[0] // rows
    rest = (0,) * (pair[0].ndim - 1)
    shape = (rows,) + pair[0].shape[1:]
    return [
        pl.BlockSpec(shape, lambda i: (jnp.minimum(i, count - 1),) + rest),
        pl.BlockSpec(shape, lambda i: (jnp.maximum(i - count, 0),) + rest),
    ]


def pick(count, first, second):
    return jnp.where(pl.program_id(0) < count, first[...], second[...])


def out_of(shape, kind):
    return jax.ShapeDtypeStruct(tuple(shape), kind)


MARKS = {}


def mark_of(array):
    return MARKS[id(array)][1] if id(array) in MARKS else array


def call(kernel, outs, args, *, ins=None, out_specs=None, grid=None, scratch=(), us=0.001, mib=4, after=(), through=()):
    ins = list(ins or [VMEM] * len(args))
    out_specs = list(out_specs or [VMEM] * len(outs))
    extra = {} if grid is None else {"grid": grid}
    after = list({id(m): m for m in map(mark_of, after)}.values())
    idle = len(after) + len(through)
    mark = out_of((8, LANES), F32)

    def body(*refs):
        given, made = refs[: len(args)], refs[len(args) + idle :]
        made[len(outs)][...] = jnp.zeros((8, LANES), F32)
        kernel(*given, *made[: len(outs)], *made[len(outs) + 1 + len(through) :])

    made = list(
        pl.pallas_call(
        body,
        out_shape=list(outs) + [mark] + [out_of(t.shape, t.dtype) for t in through],
        in_specs=ins + [ANY] * idle,
        out_specs=out_specs + [VMEM if grid is None else fixed(mark)] + [ANY] * len(through),
        scratch_shapes=list(scratch),
        compiler_params=pltpu.CompilerParams(vmem_limit_bytes=mib << 20),
        input_output_aliases={
            len(args) + len(after) + i: len(outs) + 1 + i for i in range(len(through))
        },
        cost_estimate=pl.CostEstimate(flops=int(us * 1e9), bytes_accessed=1000, transcendentals=0),
        **extra,
    )(*args, *after, *through)
    )
    mark = made.pop(len(outs))
    for array in made:
        MARKS[id(array)] = (array, mark)
    return made


class Ring:
    def __init__(self, sizes):
        self.dp, self.mp = sizes
        self.me = lax.axis_index("dp")
        self.odd = lax.axis_index("mp") & 1
        self.quarter = self.dp // 4
        j = jnp.arange(self.dp, dtype=jnp.int32)
        first = (j // self.quarter) & 1
        last = j // (2 * self.quarter)

        def order(odd):
            low = jnp.where(odd == 0, first + 2 * last, 2 * first + last)
            return self.me ^ (4 * (j % self.quarter) + low)

        self.order = order(self.odd)
        self.orders = [order(self.odd ^ (k & 1)) for k in range(1, self.mp)]
        rel = self.me ^ j
        bit0, bit1 = rel & 1, (rel >> 1) & 1
        first, last = jnp.where(self.odd == 0, bit0, bit1), jnp.where(self.odd == 0, bit1, bit0)
        self.spots = (rel >> 2) + self.quarter * (first + 2 * last)
        lead = (lax.axis_index("mp") == 0).astype(jnp.int32)
        self.places = jnp.concatenate([self.order, lead[None]])

    def far(self, array):
        return [
            lax.ppermute(array, "dp", [(i, i ^ (4 * step)) for i in range(self.dp)])
            for step in range(1, self.quarter)
        ]

    def far_all(self, arrays):
        return [
            lax.ppermute(a, "dp", [(i, i ^ (4 * (step + 1))) for i in range(self.dp)])
            for step, a in enumerate(arrays)
        ]

    def near(self, array, masks):
        pairs = [
            (i * self.mp + c, (i ^ masks[c & 1]) * self.mp + c)
            for i in range(self.dp)
            for c in range(self.mp)
        ]
        return lax.ppermute(array, ("dp", "mp"), pairs)

    def first(self, array):
        return self.near(array, (1, 2))

    def last(self, array):
        return self.near(array, (2, 1))

    def exchange(self, array):
        return [
            lax.ppermute(array, "mp", [(i, i ^ k) for i in range(self.mp)])
            for k in range(1, self.mp)
        ]


def join_kernel(plan, *refs):
    sources, outs = refs[: -len(plan)], refs[-len(plan) :]
    for (chosen, start, stop), out in zip(plan, outs):
        at = 0
        for i in chosen:
            count = sources[i].shape[0]
            out[at : at + count] = sources[i][:, :, start:stop]
            at += count


def join(arrays, plan, after=(), through=()):
    outs = []
    for chosen, start, stop in plan:
        count = sum(arrays[i].shape[0] for i in chosen)
        outs.append(out_of((count, arrays[0].shape[1], stop - start), arrays[0].dtype))
    return call(functools.partial(join_kernel, plan), outs, arrays, after=after, through=through)


def aligned(rows):
    return rows % 16 == 0


def blocks_of(ring, held, got):
    if aligned(held.shape[1]):
        return (held, got)
    blocks = jnp.take(jnp.concatenate([held, got], 0), ring.spots, axis=0)
    return (blocks.reshape((-1,) + held.shape[2:]),)


def load(places, sources, to, at):
    there = slice(at, at + sources[0].shape[-1])
    if len(sources) == 2:
        half, rows, _ = sources[0].shape
        for j in range(2 * half):
            row = pl.multiple_of(places[j] * rows, 16)
            to[pl.ds(row, rows), there] = sources[j // half][j % half]
    else:
        to[:, there] = sources[0][...]
    return there.stop


def columns(array, at, count):
    first = (0,) * (array.ndim - 1)
    return pl.BlockSpec(
        array.shape[:-1] + (count,),
        lambda i: first + (at // count,),
        pipeline_mode=pl.Buffered(1),
    )


def emit(places, total, keep, send, extra=None):
    half, rows, _ = keep.shape
    for j in range(2 * half):
        at = pl.multiple_of(places[j] * rows, 16)
        block = total[pl.ds(at, rows), :]
        if extra is not None:
            block = block + extra
        if j < half:
            keep[j] = block
        else:
            send[j - half] = block.astype(BF)


def emitted(ring, rows, cols):
    share = rows // ring.dp
    if aligned(share):
        shape = (ring.dp // 2, share, cols)
        return [out_of(shape, F32), out_of(shape, BF)]
    return [out_of((rows, cols), F32)]


def halves(ring, outs, extra=None):
    if len(outs) == 2:
        return outs
    blocks = outs[0].reshape(ring.dp, -1, outs[0].shape[1])
    if extra is not None:
        blocks = blocks + extra
    blocks = jnp.take(blocks, ring.order, axis=0)
    return blocks[: ring.dp // 2], blocks[ring.dp // 2 :].astype(BF)


def fold_kernel(modes, *refs):
    ins, outs = refs[: 2 * len(modes)], refs[2 * len(modes) :]
    for mode in modes:
        keep, got = ins[:2]
        ins = ins[2:]
        count = got.shape[0] if mode else got.shape[0] // 2
        if mode:
            outs[0][...] = keep[0] + got[0].astype(F32)
            for j in range(1, count):
                outs[j][...] = (keep[j] + got[j].astype(F32)).astype(BF)
            outs = outs[count:]
        else:
            outs[0][...] = keep[:count] + got[:count].astype(F32)
            outs[1][...] = (keep[count:] + got[count:].astype(F32)).astype(BF)
            outs = outs[2:]


def fold(*items, after=(), through=()):
    outs = []
    args = []
    for keep, got, mode in items:
        args += [keep, got]
        if mode:
            shape = keep.shape[1:]
            outs += [out_of(shape, F32)] + [out_of(shape, BF)] * (keep.shape[0] - 1)
        else:
            shape = (keep.shape[0] // 2,) + keep.shape[1:]
            outs += [out_of(shape, F32), out_of(shape, BF)]
    kernel = functools.partial(fold_kernel, [m for *_, m in items])
    return call(kernel, outs, args, after=after, through=through)


def final_kernel(counts, plan, scaled, carried, gain_ref, *refs):
    carry, refs = refs[:carried], refs[carried:]
    weights, refs = refs[: len(scaled)], refs[len(scaled) :]
    fields = []
    for count in counts:
        total = refs[0][...]
        for r in refs[1:count]:
            total = total + r[...].astype(F32)
        fields.append(total)
        refs = refs[count:]
    outs, gain_out = refs[:-1], refs[-1]
    sums = jnp.zeros(gain_out.shape, F32)
    for i, (out, spans) in enumerate(zip(outs, plan)):
        at = 0
        for f, start, stop in spans:
            value = fields[f][:, start:stop]
            there = slice(at, at + stop - start)
            if i in scaled:
                kept = weights[scaled.index(i)][:, there].astype(F32)
                sums += jnp.sum(value * kept, 1, keepdims=True)
                value = value * gain_ref[...]
            out[:, there] = value
            at += stop - start
    if carried:
        lane = lax.broadcasted_iota(jnp.int32, sums.shape, 1)
        sums = jnp.where(lane == 0, sums, carry[0][...])
    gain_out[...] = sums


def final(items, plan, scaled, gain, weights, carry=(), after=()):
    rows = gain.shape[0]
    outs = [out_of((rows, sum(b - a for _, a, b in spans)), F32) for spans in plan]
    outs.append(out_of((rows, LANES), F32))
    kernel = functools.partial(final_kernel, [len(i) for i in items], plan, scaled, len(carry))
    args = [gain, *carry, *weights, *[a for i in items for a in i]]
    return call(kernel, outs, args, after=after)


def distance_buckets(bounds_ref, dist, buckets):
    size = jnp.abs(dist)
    half = jnp.zeros(dist.shape, jnp.int32)
    for b in range(bounds_ref.shape[0]):
        half += (size >= bounds_ref[b]).astype(jnp.int32)
    return half + jnp.where(dist > 0, buckets // 2, 0)


def bases_kernel(bounds_ref, table_ref, near_ref, far_ref):
    heads, _, width = near_ref.shape
    buckets = table_ref.shape[1]
    row = lax.broadcasted_iota(jnp.int32, (8, width), 0)
    for to, sign in ((near_ref, 1), (far_ref, -1)):
        dist = sign * (lax.broadcasted_iota(jnp.int32, (8, width), 1) - width // 2)
        marks = distance_buckets(bounds_ref, dist, buckets)
        marks = jnp.concatenate([marks] * (buckets // 8), 0)
        onehot = (marks == lax.broadcasted_iota(jnp.int32, (buckets, width), 0)).astype(F32)
        line = dot(table_ref[...], onehot.astype(BF))
        for h in range(heads):
            field = jnp.broadcast_to(line[h : h + 1], (8, width))
            for k in (1, 2, 4):
                field = jnp.where((row & k) != 0, pltpu.roll(field, k, 1), field)
            while field.shape[0] < LANES:
                field = jnp.concatenate([field, pltpu.roll(field, field.shape[0], 1)], 0)
            to[h] = field.astype(BF)


def bias_bases(boundaries, table, heads, width, after=()):
    shape = out_of((heads, LANES, width), BF)
    return call(
        bases_kernel, [shape, shape], [boundaries, table], ins=[SMEM, VMEM], mib=16, after=after
    )


def bucket_field(bounds_ref, fields, buckets, first):
    width = fields[0].shape[-1]
    dist = width // 2 - lax.broadcasted_iota(jnp.int32, (8, width), 1)
    marks = distance_buckets(bounds_ref, dist, buckets)
    row = lax.broadcasted_iota(jnp.int32, (8, width), 0)
    line = jnp.zeros((8, width), F32)
    for h, field in enumerate(fields, first):
        while field.shape[0] > 8:
            half = field.shape[0] // 2
            field = field[:half] + pltpu.roll(field[half:], width - half, 1)
        for k in (4, 2, 1):
            field = jnp.where((row & k) != 0, pltpu.roll(field, width - k, 1), field)
        line = jnp.where(row == h, jnp.sum(field, 0, keepdims=True), line)
    lane = lax.broadcasted_iota(jnp.int32, (8, LANES), 1)
    out = jnp.zeros((8, LANES), F32)
    for b in range(buckets):
        total = jnp.sum(jnp.where(marks == b, line, 0.0), 1, keepdims=True)
        out = jnp.where(lane == b, total, out)
    return out


def split_low(values, lane, off, rest):
    high = values.astype(BF).astype(F32)
    mid = (values - high).astype(BF).astype(F32)
    low = values - high - mid
    return jnp.where(
        lane == off,
        high,
        jnp.where(lane == off + 1, mid, jnp.where(lane == off + 2, low, rest)),
    )


def three_ones(lane, off):
    return jnp.where((lane >= off) & (lane < off + 3), 1.0, 0.0)


def slots_of(batches):
    at = 0
    for b, (slots, length) in enumerate(batches):
        for s in range(slots):
            yield b, s, length, slice(at, at + length)
            at += length


def attend_kernel(batches, halves, *refs):
    places, lens = refs[0], refs[1 : 1 + len(batches)]
    refs = refs[1 + len(batches) :]
    normed_ref, near_ref = refs[:2]
    sources = refs[2 : 2 + halves]
    aug_ref, k_ref, v_ref, o_ref, w_scr = refs[2 + halves :]
    width = near_ref.shape[-1]
    load(places, sources, w_scr, 0)
    for b, s, length, span in slots_of(batches):
        valid = lens[b][s]
        lane = lax.broadcasted_iota(jnp.int32, (length, LANES), 1)
        place = lax.broadcasted_iota(jnp.int32, (length, LANES), 0)
        masked = jnp.where(place >= valid, NEG, 0.0)
        qkv = dot(normed_ref[span, :], w_scr[...])
        q, k, v = (qkv[:, i * LANES : (i + 1) * LANES] for i in range(3))
        k_ref[span, :] = k.astype(BF)
        v_ref[span, :] = v.astype(BF)
        mixed = []
        for e in range(2):
            own = (lane >= DH) == (e == 1)
            off = DH * (1 - e)
            marker = jnp.where(lane == off + 3, 1.0, 0.0)
            q_own = jnp.where(own, q, marker).astype(BF)
            k_own = jnp.where(own, k, jnp.where(lane == off + 3, masked, 0.0)).astype(BF)
            v_own = jnp.where(own, v, 1.0).astype(BF)
            start = width // 2
            bias = [
                near_ref[e, :, start - a * LANES : start - a * LANES + length]
                for a in range(length // LANES)
            ]
            scores = dot_cols(q_own, k_own) + jnp.concatenate(bias, 0).astype(F32)
            top = jnp.max(scores, 1, keepdims=True)
            expo = jnp.exp(scores - top)
            sums = dot(expo.astype(BF), v_own)
            total = jnp.where(own, pltpu.roll(sums, DH, 1), sums)
            logsum = top + jnp.log(total)
            extra = split_low(-logsum, lane, off, marker)
            aug_ref[span, e * LANES : (e + 1) * LANES] = jnp.where(own, q, extra).astype(BF)
            mixed.append(sums / total)
        o_ref[span, :] = jnp.where(lane < DH, mixed[0], mixed[1]).astype(BF)


def pair_of(base, pair):
    return pl.BlockSpec((2,) + base.shape[1:], lambda i: (pair, 0, 0))


def attend(ring, batches, lens, near, unit, weights, at, pair, us, after=()):
    rows, width = unit.shape
    shapes = [pltpu.HBM((rows, c * LANES), BF) for c in (2, 1, 1)]
    shapes.append(out_of((rows, LANES), BF))
    return call(
        functools.partial(attend_kernel, batches, len(weights)),
        shapes,
        [ring.places, *lens, unit, near, *weights],
        ins=[SMEM] * (1 + len(lens))
        + [fixed(unit), pair_of(near, pair)]
        + [columns(w, at, 3 * LANES) for w in weights],
        out_specs=[fixed(s) for s in shapes],
        grid=(1,),
        scratch=[pltpu.VMEM((width, 3 * LANES), BF)],
        us=us,
        mib=16,
        after=after,
    )


def attend_back_kernel(batches, pair, buckets, before, priors, emits, *refs):
    lens, refs = refs[: len(batches)], refs[len(batches) :]
    bounds, places, unit_ref, go_ref, aug_ref, k_ref, v_ref, o_ref, far_ref = refs[:9]
    totals, (table_in, grads_ref, table_ref) = refs[9 : 9 + priors], refs[9 + priors : 12 + priors]
    outs, (gbase_ref, total) = refs[12 + priors : -2], refs[-2:]
    width = far_ref.shape[-1]
    gbase_ref[...] = jnp.zeros_like(gbase_ref)
    for b, s, length, span in slots_of(batches):
        valid = lens[b][s]
        lane = lax.broadcasted_iota(jnp.int32, (length, LANES), 1)
        place = lax.broadcasted_iota(jnp.int32, (length, LANES), 0)
        masked = jnp.where(place >= valid, NEG, 0.0)
        k = k_ref[span, :].astype(F32)
        v = v_ref[span, :].astype(F32)
        go = go_ref[span, :].astype(F32)
        both = go * o_ref[span, :].astype(F32)
        grads = []
        for e in range(2):
            own = (lane >= DH) == (e == 1)
            off = DH * (1 - e)
            q_own = aug_ref[span, e * LANES : (e + 1) * LANES]
            ones = three_ones(lane, off)
            k_own = jnp.where(own, k, jnp.where(lane == off + 3, masked, ones)).astype(BF)
            v_own = jnp.where(own, v, ones).astype(BF)
            delta = jnp.sum(jnp.where(own, both, 0.0), 1, keepdims=True)
            g_own = jnp.where(own, go, split_low(-delta, lane, off, 0.0)).astype(BF)
            cols = [
                slice(width // 2 - a * LANES, width // 2 - a * LANES + length)
                for a in range(length // LANES)
            ]
            bias = jnp.concatenate([far_ref[e, :, c] for c in cols], 0)
            probs = jnp.exp(dot_cols(k_own, q_own) + bias.astype(F32))
            ds = probs * dot_cols(v_own, g_own)
            for a, c in enumerate(cols):
                gbase_ref[e, :, c] += ds[a * LANES : (a + 1) * LANES]
            ds = ds.astype(BF)
            gv = dot(probs.astype(BF), g_own)
            grads.append((dot_rows(ds, k_own), dot(ds, q_own), gv))
        first = lane < DH
        for i, (a, b) in enumerate(zip(*grads)):
            grads_ref[span, i * LANES : (i + 1) * LANES] = jnp.where(first, a, b).astype(BF)
    table = table_in[...] + bucket_field(
        bounds, [gbase_ref[0], gbase_ref[1]], buckets, 2 * pair
    )
    table_ref[...] = table
    part = dot_rows(unit_ref[...], grads_ref[...])
    if not emits:
        outs[0][...] = part
        return
    step = 3 * LANES
    at = 0
    for value in [r[...] for r in totals[:before]] + [part] + [r[...] for r in totals[before:]]:
        total[:, at : at + value.shape[1]] = value
        at += value.shape[1]
    extra = None
    if total.shape[1] > at:
        total[:, at:] = jnp.zeros((total.shape[0], LANES), F32)
    if total.shape[1] > at and emits == 2:
        rows = outs[0].shape[1]
        extra = jnp.concatenate([table, jnp.zeros((rows - 8, LANES), F32)], 0)
        extra = jnp.concatenate([jnp.zeros((rows, at), F32), extra], 1)
    if emits == 2:
        emit(places, total, *outs, extra=extra)
    else:
        outs[0][...] = total[...]


def attend_back(
    ring, batches, lens, boundaries, buckets, far, unit, go, fwd, pair, table, before, rest, last, after=()
):
    rows, width = unit.shape
    step = 3 * LANES
    go_spec = pl.BlockSpec((rows, LANES), lambda i: (0, pair))
    given = rest is None
    priors = [] if given else [*before, *rest]
    cols = step + sum(p.shape[1] for p in priors) + (LANES if last else 0)
    outs = [out_of((rows, step), BF), out_of((8, LANES), F32)]
    made = [out_of((width, step), F32)] if given else emitted(ring, width, cols)
    emits = 0 if given else len(made)
    kernel = functools.partial(
        attend_back_kernel, batches, pair, buckets, len(before), len(priors), emits
    )
    grads, table, *made = call(
        kernel,
        outs + made,
        [*lens, boundaries, ring.places, unit, go, *fwd, far, *priors, table],
        ins=[SMEM] * (len(lens) + 2)
        + [fixed(unit), go_spec]
        + [fixed(a) for a in fwd]
        + [pair_of(far, pair)]
        + [fixed(a) for a in (*priors, table)],
        out_specs=[fixed(o) for o in outs + made],
        grid=(1,),
        scratch=[
            pltpu.VMEM((2,) + far.shape[1:], F32),
            pltpu.VMEM((8, LANES) if given else (width, cols), F32),
        ],
        mib=24,
        after=after,
    )
    if not given:
        share = width // ring.dp
        extra = jnp.pad(table, ((0, share - 8), (cols - LANES, 0))) if last else None
        made = halves(ring, made, extra)
    return grads, table, made


def rms_parts(field):
    scale = lax.rsqrt(jnp.mean(field * field, -1, keepdims=True) + EPS)
    return (scale, field * scale)


def norm_back(grad_unit, unit, scale):
    return scale * (grad_unit - unit * jnp.mean(grad_unit * unit, -1, keepdims=True))


def norm_kernel(count, short_ref, long_ref, unit_ref):
    unit_ref[...] = rms_parts(pick(count, short_ref, long_ref).astype(F32))[1].astype(BF)


def norm(xs, tile=512, after=()):
    out = out_of((xs[0].shape[0] + xs[1].shape[0], xs[0].shape[1]), BF)
    return call(
        functools.partial(norm_kernel, xs[0].shape[0] // tile),
        [out],
        xs,
        ins=pair_tiles(xs, tile),
        out_specs=[tiles(out, tile)],
        grid=(out.shape[0] // tile,),
        mib=8,
        after=after,
    )[0]


def sum_of(refs):
    total = refs[0][...].astype(F32)
    for r in refs[1:]:
        total = total + r[...].astype(F32)
    return total


def gelu_parts(x):
    c = 0.7978845608028654
    d = c * 0.044715
    square = x * x
    t = jnp.tanh(x * (c + d * square))
    half = 0.5 + 0.5 * t
    slope = half + (0.5 * x) * (1.0 - t * t) * (c + 3.0 * d * square)
    return x * half, slope


def ffn_first_kernel(halves, groups, pairs, emits, count, places, *refs):
    all_places, refs = [places, places, *refs[: groups - 1]], refs[groups - 1 :]
    g_refs, x_refs, refs = refs[:2], refs[2:4], refs[4:]
    o_refs, refs = refs[: groups * pairs], refs[groups * pairs :]
    sources, refs = refs[:halves], refs[halves:]
    unit_ref, scale_ref, out_ref, gn_ref = refs[:4]
    grads, (w_scr, total) = refs[4 : 4 + emits], refs[4 + emits :]
    units = total.shape[1] // 2
    step = pl.program_id(0)

    @pl.when(step == 0)
    def _():
        total[...] = jnp.zeros_like(total)
        at = 0
        count = halves // (1 + groups)
        for i, there in enumerate(all_places):
            at = load(there, sources[i * count : (i + 1) * count], w_scr, at)

    mixed = jnp.concatenate([r[...] for r in o_refs], 1)
    middle = pick(count, *x_refs).astype(F32) + dot_cols(mixed, w_scr[:, 2 * units :])
    scale, unit = rms_parts(middle)
    unit = unit.astype(BF)
    unit_ref[...] = unit
    scale_ref[...] = jnp.broadcast_to(scale, scale_ref.shape)
    g = pick(count, *g_refs)
    win, wout = w_scr[:, :units], w_scr[:, units : 2 * units]
    act, slope = gelu_parts(dot(unit, win))
    act = act.astype(BF)
    gpre = (dot(g, wout) * slope).astype(BF)
    lead = places[places.shape[0] - 1].astype(F32)
    out_ref[...] = (dot_cols(act, wout) + lead * middle).astype(BF)
    gn_ref[...] = dot_cols(gpre, win).astype(BF)
    total[:, :units] += dot_rows(unit, gpre)
    total[:, units:] += dot_rows(g, act)

    @pl.when(step == pl.num_programs(0) - 1)
    def _():
        if emits == 2:
            emit(places, total, *grads)
        else:
            grads[0][...] = total[...]


def ffn_first(ring, gs, xs, mixed, weights, out_weights, units, tile=512, after=()):
    rows = mixed[0].shape[0]
    width = xs[0].shape[1]
    groups = len(out_weights)
    pairs = len(mixed) // groups
    field = out_of((rows, width), BF)
    outs = [field, out_of((rows, LANES), F32), field, field]
    grads = emitted(ring, width, 2 * units)
    sources = [*weights, *[w for ws in out_weights for w in ws]]
    kernel = functools.partial(
        ffn_first_kernel, len(sources), groups, pairs, len(grads), xs[0].shape[0] // tile
    )
    return call(
        kernel,
        outs + grads,
        [ring.places, *ring.orders, *gs, *xs, *mixed, *sources],
        ins=[SMEM] * groups
        + pair_tiles(gs, tile)
        + pair_tiles(xs, tile)
        + [tiles(a, tile) for a in mixed]
        + [columns(w, 0, w.shape[-1]) for w in sources],
        out_specs=[tiles(o, tile) for o in outs] + [fixed(o) for o in grads],
        grid=(rows // tile,),
        scratch=[
            pltpu.VMEM((width, 2 * units + len(mixed) * LANES), BF),
            pltpu.VMEM((width, 2 * units), F32),
        ],
        mib=46,
        after=after,
    )


def ffn_next_kernel(halves, count, places, unit_ref, scale_ref, *refs):
    g_refs, (out_in, gn_in), refs = refs[:2], refs[2:4], refs[4:]
    sources, refs = refs[:halves], refs[halves:]
    out_ref, mid_ref, act_ref, gpre_ref, w_scr = refs
    units = w_scr.shape[1] // 2

    @pl.when(pl.program_id(0) == 0)
    def _():
        load(places, sources, w_scr, 0)

    win, wout = w_scr[:, :units], w_scr[:, units:]
    unit = unit_ref[...]
    g = pick(count, *g_refs)
    act, slope = gelu_parts(dot(unit, win))
    act = act.astype(BF)
    gpre = (dot(g, wout) * slope).astype(BF)
    act_ref[...] = act
    gpre_ref[...] = gpre
    out_ref[...] = (out_in[...] + dot_cols(act, wout)).astype(BF)
    lead = places[places.shape[0] - 1].astype(F32)
    back = norm_back(gn_in[...] + dot_cols(gpre, win), unit.astype(F32), scale_ref[:, :1])
    mid_ref[...] = (back + lead * g.astype(F32)).astype(BF)


def ffn_next(ring, unit, scale, gs, out, gn, weights, units, tile=512, after=()):
    rows, width = unit.shape
    outs = [out_of((rows, width), BF)] * 2 + [out_of((rows, units), BF)] * 2
    return call(
        functools.partial(ffn_next_kernel, len(weights), gs[0].shape[0] // tile),
        outs,
        [ring.places, unit, scale, *gs, out, gn, *weights],
        ins=[SMEM, tiles(unit, tile), tiles(scale, tile)]
        + pair_tiles(gs, tile)
        + [tiles(out, tile), tiles(gn, tile)]
        + [columns(w, 0, w.shape[-1]) for w in weights],
        out_specs=[tiles(o, tile) for o in outs],
        grid=(rows // tile,),
        scratch=[pltpu.VMEM((width, 2 * units), BF)],
        mib=40,
        after=after,
    )


def ffn_grads_kernel(emits, count, places, unit_ref, *refs):
    g_refs, (gpre_ref, act_ref) = refs[:2], refs[2:4]
    grads, total = refs[4:-1], refs[-1]
    step = pl.program_id(0)
    units = act_ref.shape[1]

    @pl.when(step == 0)
    def _():
        total[...] = jnp.zeros_like(total)

    total[:, :units] += dot_rows(unit_ref[...], gpre_ref[...])
    total[:, units:] += dot_rows(pick(count, *g_refs), act_ref[...])

    @pl.when(step == pl.num_programs(0) - 1)
    def _():
        if emits == 2:
            emit(places, total, *grads)
        else:
            grads[0][...] = total[...]


def ffn_grads(ring, unit, gs, gpre, act, tile=512, after=()):
    rows, width = unit.shape
    cols = 2 * act.shape[1]
    outs = emitted(ring, width, cols)
    return call(
        functools.partial(ffn_grads_kernel, len(outs), gs[0].shape[0] // tile),
        outs,
        [ring.places, unit, *gs, gpre, act],
        ins=[SMEM, tiles(unit, tile)]
        + pair_tiles(gs, tile)
        + [tiles(gpre, tile), tiles(act, tile)],
        out_specs=[fixed(o) for o in outs],
        grid=(rows // tile,),
        scratch=[pltpu.VMEM((width, cols), F32)],
        mib=32,
        after=after,
    )


def middle_kernel(halves, groups, pairs, places, *refs):
    mid_refs, refs = refs[:groups], refs[groups:]
    o_refs, refs = refs[:pairs], refs[pairs:]
    sources, (go_ref, total_ref, w_scr) = refs[:halves], refs[halves:]
    step = pl.program_id(0)

    @pl.when(step == 0)
    def _():
        total_ref[...] = jnp.zeros_like(total_ref)
        load(places, sources, w_scr, 0)

    grad = sum_of(mid_refs).astype(BF)
    go_ref[...] = dot(grad, w_scr[...]).astype(BF)
    total_ref[...] += dot_rows(grad, jnp.concatenate([r[...] for r in o_refs], 1))


def middle_back(ring, mids, mixed, weights, tile=512, after=()):
    rows, width = mids[0].shape
    pairs = len(mixed)
    cols = pairs * LANES
    go, total = out_of((rows, cols), BF), out_of((width, cols), F32)
    return call(
        functools.partial(middle_kernel, len(weights), len(mids), pairs),
        [go, total],
        [ring.places, *mids, *mixed, *weights],
        ins=[SMEM]
        + [tiles(a, tile) for a in (*mids, *mixed)]
        + [columns(w, 0, cols) for w in weights],
        out_specs=[tiles(go, tile), fixed(total)],
        grid=(rows // tile,),
        scratch=[pltpu.VMEM((width, cols), BF)],
        mib=24,
        after=after,
    )


def input_back_kernel(halves, groups, pairs, count, places, short_ref, long_ref, *refs):
    mid_refs, refs = refs[:groups], refs[groups:]
    g_refs, refs = refs[:pairs], refs[pairs:]
    sources, (part_ref, w_scr) = refs[:-2], refs[-2:]

    @pl.when(pl.program_id(0) == 0)
    def _():
        at = 0
        for i in range(0, len(sources), halves):
            at = load(places, sources[i : i + halves], w_scr, at)

    part = dot_cols(jnp.concatenate([r[...] for r in g_refs], 1), w_scr[...])
    scale, unit = rms_parts(pick(count, short_ref, long_ref).astype(F32))
    lead = places[places.shape[0] - 1].astype(F32)
    part_ref[...] = (norm_back(part, unit, scale) + lead * sum_of(mid_refs)).astype(BF)


def input_back(ring, xs, mids, grads, weights, tile=512, after=()):
    rows, width = grads[0].shape[0], xs[0].shape[1]
    pairs = len(grads)
    out = out_of((rows, width), BF)
    return call(
        functools.partial(
            input_back_kernel, len(weights[0][0]), len(mids), pairs, xs[0].shape[0] // tile
        ),
        [out],
        [ring.places, *xs, *mids, *grads, *[a for blocks, _ in weights for a in blocks]],
        ins=[SMEM]
        + pair_tiles(xs, tile)
        + [tiles(a, tile) for a in (*mids, *grads)]
        + [columns(a, 0, count) for blocks, count in weights for a in blocks],
        out_specs=[tiles(out, tile)],
        grid=(rows // tile,),
        scratch=[pltpu.VMEM((width, 3 * pairs * LANES), BF)],
        mib=20,
        after=after,
    )[0]


def pad_cols(array, cols):
    return jnp.pad(array, ((0, 0), (0, cols - array.shape[1]))) if cols > array.shape[1] else array


def on_device(
    sizes,
    x_short,
    x_long,
    len_short,
    len_long,
    boundaries,
    q_weight,
    k_weight,
    v_weight,
    out_weight,
    in_weight,
    ff_out_weight,
    attn_gain,
    ffn_gain,
    bias_table,
    cot_short,
    cot_long,
):
    MARKS.clear()
    ring = Ring(sizes)
    quarter = ring.quarter
    width = x_short.shape[2]
    buckets, heads = bias_table.shape
    real = heads * DH
    cols = -(-real // LANES) * LANES
    pairs = cols // LANES
    units = in_weight.shape[1] // 2
    batches = [x.shape[:2] for x in (x_short, x_long)]
    lens = (len_short, len_long)

    xs = [x.reshape(-1, width) for x in (x_short, x_long)]
    gs = [g.reshape(-1, width) for g in (cot_short, cot_long)]

    col_a, col_f = (v.astype(F32)[:, None] for v in (attn_gain, ffn_gain))
    padded = [pad_cols(w, cols) for w in (q_weight, k_weight, v_weight, out_weight)]
    scaled = [(w.astype(F32) * col_a).astype(BF) for w in padded[:3]]
    pieces = [[w[:, p * LANES : (p + 1) * LANES] for w in scaled] for p in range(pairs)]
    own = jnp.concatenate([w for piece in pieces for w in piece] + [padded[3]], 1)[None]
    win = (in_weight.astype(F32) * col_f).astype(BF)
    own1, own2 = (
        jnp.concatenate([w[:, at : at + units] for w in (win, ff_out_weight)], 1)[None]
        for at in (0, units)
    )
    step = 3 * LANES
    z = tuple(range(quarter))
    table = jnp.pad(bias_table.T, ((0, 8 - heads), (0, 0)))

    two = (0, 1)
    wide = own.shape[2]
    got = ring.far(own)
    span = 2 * max(length for _, length in batches)
    near, far = bias_bases(boundaries, table, cols // DH, span, after=[own])
    held, own1 = join([own, *got], [(z, 0, wide)], after=[near], through=[own1])
    got = ring.first(held)
    got1 = ring.far(own1)
    unit = norm(xs, after=[held])
    plan = [(two, 0, step), (two, step, wide)]
    *helds, own2 = join([held, got], plan, after=[unit], through=[own2])
    qkv, more = [blocks_of(ring, h, ring.last(h)) for h in helds]
    out_at = (pairs - 1) * step
    out_w = [m[..., out_at:] for m in more]
    qkvs = [(qkv, 0)] + [(more, p * step) for p in range(pairs - 1)]
    out_ws = [out_w] + list(zip(*[ring.exchange(w) for w in out_w]))

    fwd = []
    after = helds
    for p in range(pairs):
        fwd.append(
            attend(
                ring,
                batches,
                lens,
                near,
                unit,
                *qkvs[p],
                p,
                C2 if p == pairs - 1 else C1 if p == 1 else 0.001,
                after=after,
            )
        )
        if p == 0:
            held1, own2 = join(
                [own1, *got1], [(z, 0, 2 * units)], after=[fwd[0][0]], through=[own2]
            )
            got1 = ring.first(held1)
            got2 = ring.far(own2)
            (held1,) = join([held1, got1], [(two, 0, 2 * units)])
            got1 = ring.last(held1)
            after = [held1, *out_w]
        if p == min(1, pairs - 1):
            (held2,) = join([own2, *got2], [(z, 0, 2 * units)], after=[fwd[p][0]])
            got2 = ring.first(held2)
            after = [held2]
    mixed = [f[3] for f in fwd]
    others = list(zip(*[ring.exchange(o) for o in mixed]))
    (held2,) = join([held2, got2], [(two, 0, 2 * units)], after=[fwd[-1][0]])
    got2 = ring.last(held2)
    first = blocks_of(ring, held1, got1)
    second = blocks_of(ring, held2, got2)

    unit_f, scale, out, gn, *grad1 = ffn_first(
        ring, gs, xs, [*mixed, *[o for g in others for o in g]], first, out_ws, units, after=[held2]
    )
    keep1, send = halves(ring, grad1)
    got1 = ring.last(send)
    out, mid, act, gpre = ffn_next(ring, unit_f, scale, gs, out, gn, second, units)
    keep1, send, mid, out = fold((keep1, got1, 0), through=[mid, out])
    mids = [mid] + ring.exchange(mid)
    outs = [out] + ring.exchange(out)
    got1 = ring.first(send)
    keep2, send2 = halves(ring, ffn_grads(ring, unit_f, gs, gpre, act, after=[keep1]))
    keep1, *sends, send2 = fold((keep1, got1, 1), after=[keep2], through=[send2])
    got1 = ring.far_all(sends)
    got2 = ring.last(send2)
    go, grad_o = middle_back(ring, mids, mixed, out_w, after=[keep1])

    grads = []
    totals = []
    sums = jnp.zeros((8, LANES), F32)
    after = [keep1]
    for p in range(pairs):
        last = p == pairs - 1
        before, rest = ((), ()) if last else (totals, [grad_o] if p == pairs - 2 else None)
        g, sums, made = attend_back(
            ring,
            batches,
            lens,
            boundaries,
            buckets,
            far,
            unit,
            go,
            fwd[p],
            p,
            sums,
            before,
            rest,
            last,
            after=after,
        )
        grads.append(g)
        if p < pairs - 2:
            totals.append(made[0])
        if p == 0:
            keep2, send2 = fold((keep2, got2, 0), after=[g])
            got2 = ring.first(send2)
            after = [keep2]
        if p == pairs - 2:
            early, send = made
            keep2, *sends, send = fold((keep2, got2, 1), after=[g, *got1], through=[send])
            got2 = ring.far_all(sends)
            got = ring.last(send)
            after = [keep2]
    keep, send = made
    early, early_send, send = fold((early, got, 0), after=got2, through=[send])
    early_got = ring.first(early_send)
    got = ring.last(send)
    weights = [(qkv, step), (more, (pairs - 1) * step)]
    part = input_back(ring, xs, mids, grads, weights, after=[early])
    rows = [slice(0, xs[0].shape[0]), slice(xs[0].shape[0], None)]

    def sums_of(fields):
        return [sum(f[r].astype(F32) for f in fields).astype(BF) for r in rows]

    early, *made = fold(
        (early, early_got, 1), (keep, got, 0), through=[part]
    )
    sends, (keep, send, part) = made[: quarter - 1], made[quarter - 1 :]
    early = [early, *ring.far_all(sends)]
    got = ring.first(send)
    parts = [part] + ring.exchange(part)
    keep, *sends, part, out = fold((keep, got, 1), after=[keep], through=[parts[0], outs[0]])
    ys = sums_of([out] + outs[1:])
    late = [keep, *ring.far_all(sends)]
    grad_xs = sums_of([part] + parts[1:])
    plan = [
        [(0, 0, units), (1, 0, units)],
        [(0, units, 2 * units), (1, units, 2 * units)],
    ]
    grad_in, grad_ff, gain_f = final(
        [[keep1, *got1], [keep2, *got2]], plan, [0], col_f, [in_weight], after=[*grad_xs, *ys]
    )
    plan = [
        [(0, p * step + i * LANES, p * step + (i + 1) * LANES) for p in range(pairs - 1)]
        + [(1, i * LANES, (i + 1) * LANES)]
        for i in range(3)
    ]
    plan += [[(0, (pairs - 1) * step, (pairs - 1) * step + cols)], [(1, step, step + LANES)]]
    gq, gk, gv, grad_o, sums, gain = final(
        [early, late], plan, [0, 1, 2], col_a, padded[:3], carry=[gain_f]
    )
    for other in ring.exchange(gain):
        gain = gain + other
    return (
        ys[0].reshape(x_short.shape),
        ys[1].reshape(x_long.shape),
        grad_xs[0].reshape(x_short.shape),
        grad_xs[1].reshape(x_long.shape),
        gq[:, :real],
        gk[:, :real],
        gv[:, :real],
        grad_o[:, :real],
        grad_in,
        grad_ff,
        gain[:, 0],
        gain[:, 1],
        sums[:heads, :buckets].T,
    )


def solution(mesh):
    sizes = (mesh.shape["dp"], mesh.shape["mp"])
    return jax.shard_map(
        functools.partial(on_device, sizes),
        mesh=mesh,
        in_specs=(
            P("dp", None, None),
            P("dp", None, None),
            P("dp"),
            P("dp"),
            P(),
            P("dp", "mp"),
            P("dp", "mp"),
            P("dp", "mp"),
            P("dp", "mp"),
            P("dp", "mp"),
            P("dp", "mp"),
            P("dp"),
            P("dp"),
            P(None, "mp"),
            P("dp", None, None),
            P("dp", None, None),
        ),
        out_specs=(
            P("dp", None, None),
            P("dp", None, None),
            P("dp", None, None),
            P("dp", None, None),
            P("dp", "mp"),
            P("dp", "mp"),
            P("dp", "mp"),
            P("dp", "mp"),
            P("dp", "mp"),
            P("dp", "mp"),
            P("dp"),
            P("dp"),
            P(None, "mp"),
        ),
        check_vma=False,
    )
```

```python
import functools

import jax
import jax.numpy as jnp
from jax import lax
from jax.experimental import pallas as pl
from jax.experimental.pallas import tpu as pltpu
from jax.sharding import PartitionSpec as P

DH = 64
LANES = 128
EPS = 1e-06
NEG = -1000000000.0
BF = jnp.bfloat16
C1 = 1.5
C2 = 6.0
F32 = jnp.float32
ANY = pl.BlockSpec(memory_space=pl.ANY)
SMEM = pl.BlockSpec(memory_space=pltpu.SMEM)
VMEM = pl.BlockSpec(memory_space=pltpu.VMEM)


def dot(left, right):
    return jnp.dot(left, right, preferred_element_type=F32)


def dot_rows(left, right):
    return lax.dot_general(left, right, (((0,), (0,)), ((), ())), preferred_element_type=F32)


def dot_cols(left, right):
    return lax.dot_general(left, right, (((1,), (1,)), ((), ())), preferred_element_type=F32)


def tiles(array, rows):
    return pl.BlockSpec((rows,) + array.shape[1:], lambda i: (i,) + (0,) * (len(array.shape) - 1))


def fixed(array):
    return pl.BlockSpec(array.shape, lambda i: (0,) * len(array.shape))


def pair_tiles(pair, rows):
    count = pair[0].shape[0] // rows
    rest = (0,) * (pair[0].ndim - 1)
    shape = (rows,) + pair[0].shape[1:]
    return [
        pl.BlockSpec(shape, lambda i: (jnp.minimum(i, count - 1),) + rest),
        pl.BlockSpec(shape, lambda i: (jnp.maximum(i - count, 0),) + rest),
    ]


def pick(count, first, second):
    return jnp.where(pl.program_id(0) < count, first[...], second[...])


def out_of(shape, kind):
    return jax.ShapeDtypeStruct(tuple(shape), kind)


MARKS = {}


def mark_of(array):
    return MARKS[id(array)][1] if id(array) in MARKS else array


def call(kernel, outs, args, *, ins=None, out_specs=None, grid=None, scratch=(), us=0.001, mib=4, after=(), through=()):
    ins = list(ins or [VMEM] * len(args))
    out_specs = list(out_specs or [VMEM] * len(outs))
    extra = {} if grid is None else {"grid": grid}
    after = list({id(m): m for m in map(mark_of, after)}.values())
    idle = len(after) + len(through)
    mark = out_of((8, LANES), F32)

    def body(*refs):
        given, made = refs[: len(args)], refs[len(args) + idle :]
        made[len(outs)][...] = jnp.zeros((8, LANES), F32)
        kernel(*given, *made[: len(outs)], *made[len(outs) + 1 + len(through) :])

    made = list(
        pl.pallas_call(
        body,
        out_shape=list(outs) + [mark] + [out_of(t.shape, t.dtype) for t in through],
        in_specs=ins + [ANY] * idle,
        out_specs=out_specs + [VMEM if grid is None else fixed(mark)] + [ANY] * len(through),
        scratch_shapes=list(scratch),
        compiler_params=pltpu.CompilerParams(vmem_limit_bytes=mib << 20),
        input_output_aliases={
            len(args) + len(after) + i: len(outs) + 1 + i for i in range(len(through))
        },
        cost_estimate=pl.CostEstimate(flops=int(us * 1e9), bytes_accessed=1000, transcendentals=0),
        **extra,
    )(*args, *after, *through)
    )
    mark = made.pop(len(outs))
    for array in made:
        MARKS[id(array)] = (array, mark)
    return made


class Ring:
    def __init__(self, sizes):
        self.dp, self.mp = sizes
        self.me = lax.axis_index("dp")
        self.odd = lax.axis_index("mp") & 1
        self.quarter = self.dp // 4
        j = jnp.arange(self.dp, dtype=jnp.int32)
        first = (j // self.quarter) & 1
        last = j // (2 * self.quarter)

        def order(odd):
            low = jnp.where(odd == 0, first + 2 * last, 2 * first + last)
            return self.me ^ (4 * (j % self.quarter) + low)

        self.order = order(self.odd)
        self.orders = [order(self.odd ^ (k & 1)) for k in range(1, self.mp)]
        rel = self.me ^ j
        bit0, bit1 = rel & 1, (rel >> 1) & 1
        first, last = jnp.where(self.odd == 0, bit0, bit1), jnp.where(self.odd == 0, bit1, bit0)
        self.spots = (rel >> 2) + self.quarter * (first + 2 * last)
        lead = (lax.axis_index("mp") == 0).astype(jnp.int32)
        self.places = jnp.concatenate([self.order, lead[None]])

    def far(self, array):
        return [
            lax.ppermute(array, "dp", [(i, i ^ (4 * step)) for i in range(self.dp)])
            for step in range(1, self.quarter)
        ]

    def far_all(self, arrays):
        return [
            lax.ppermute(a, "dp", [(i, i ^ (4 * (step + 1))) for i in range(self.dp)])
            for step, a in enumerate(arrays)
        ]

    def near(self, array, masks):
        pairs = [
            (i * self.mp + c, (i ^ masks[c & 1]) * self.mp + c)
            for i in range(self.dp)
            for c in range(self.mp)
        ]
        return lax.ppermute(array, ("dp", "mp"), pairs)

    def first(self, array):
        return self.near(array, (1, 2))

    def last(self, array):
        return self.near(array, (2, 1))

    def exchange(self, array):
        return [
            lax.ppermute(array, "mp", [(i, i ^ k) for i in range(self.mp)])
            for k in range(1, self.mp)
        ]


def join_kernel(plan, *refs):
    sources, outs = refs[: -len(plan)], refs[-len(plan) :]
    for (chosen, start, stop), out in zip(plan, outs):
        at = 0
        for i in chosen:
            count = sources[i].shape[0]
            out[at : at + count] = sources[i][:, :, start:stop]
            at += count


def join(arrays, plan, after=(), through=()):
    outs = []
    for chosen, start, stop in plan:
        count = sum(arrays[i].shape[0] for i in chosen)
        outs.append(out_of((count, arrays[0].shape[1], stop - start), arrays[0].dtype))
    return call(functools.partial(join_kernel, plan), outs, arrays, after=after, through=through)


def aligned(rows):
    return rows % 16 == 0


def blocks_of(ring, held, got):
    if aligned(held.shape[1]):
        return (held, got)
    blocks = jnp.take(jnp.concatenate([held, got], 0), ring.spots, axis=0)
    return (blocks.reshape((-1,) + held.shape[2:]),)


def load(places, sources, to, at):
    there = slice(at, at + sources[0].shape[-1])
    if len(sources) == 2:
        half, rows, _ = sources[0].shape
        for j in range(2 * half):
            row = pl.multiple_of(places[j] * rows, 16)
            to[pl.ds(row, rows), there] = sources[j // half][j % half]
    else:
        to[:, there] = sources[0][...]
    return there.stop


def columns(array, at, count):
    first = (0,) * (array.ndim - 1)
    return pl.BlockSpec(
        array.shape[:-1] + (count,),
        lambda i: first + (at // count,),
        pipeline_mode=pl.Buffered(1),
    )


def emit(places, total, keep, send, extra=None):
    half, rows, _ = keep.shape
    for j in range(2 * half):
        at = pl.multiple_of(places[j] * rows, 16)
        block = total[pl.ds(at, rows), :]
        if extra is not None:
            block = block + extra
        if j < half:
            keep[j] = block
        else:
            send[j - half] = block.astype(BF)


def emitted(ring, rows, cols):
    share = rows // ring.dp
    if aligned(share):
        shape = (ring.dp // 2, share, cols)
        return [out_of(shape, F32), out_of(shape, BF)]
    return [out_of((rows, cols), F32)]


def halves(ring, outs, extra=None):
    if len(outs) == 2:
        return outs
    blocks = outs[0].reshape(ring.dp, -1, outs[0].shape[1])
    if extra is not None:
        blocks = blocks + extra
    blocks = jnp.take(blocks, ring.order, axis=0)
    return blocks[: ring.dp // 2], blocks[ring.dp // 2 :].astype(BF)


def fold_kernel(modes, *refs):
    ins, outs = refs[: 2 * len(modes)], refs[2 * len(modes) :]
    for mode in modes:
        keep, got = ins[:2]
        ins = ins[2:]
        count = got.shape[0] if mode else got.shape[0] // 2
        if mode:
            outs[0][...] = keep[0] + got[0].astype(F32)
            for j in range(1, count):
                outs[j][...] = (keep[j] + got[j].astype(F32)).astype(BF)
            outs = outs[count:]
        else:
            outs[0][...] = keep[:count] + got[:count].astype(F32)
            outs[1][...] = (keep[count:] + got[count:].astype(F32)).astype(BF)
            outs = outs[2:]


def fold(*items, after=(), through=()):
    outs = []
    args = []
    for keep, got, mode in items:
        args += [keep, got]
        if mode:
            shape = keep.shape[1:]
            outs += [out_of(shape, F32)] + [out_of(shape, BF)] * (keep.shape[0] - 1)
        else:
            shape = (keep.shape[0] // 2,) + keep.shape[1:]
            outs += [out_of(shape, F32), out_of(shape, BF)]
    kernel = functools.partial(fold_kernel, [m for *_, m in items])
    return call(kernel, outs, args, after=after, through=through)


def final_kernel(counts, plan, scaled, carried, gain_ref, *refs):
    carry, refs = refs[:carried], refs[carried:]
    weights, refs = refs[: len(scaled)], refs[len(scaled) :]
    fields = []
    for count in counts:
        total = refs[0][...]
        for r in refs[1:count]:
            total = total + r[...].astype(F32)
        fields.append(total)
        refs = refs[count:]
    outs, gain_out = refs[:-1], refs[-1]
    sums = jnp.zeros(gain_out.shape, F32)
    for i, (out, spans) in enumerate(zip(outs, plan)):
        at = 0
        for f, start, stop in spans:
            value = fields[f][:, start:stop]
            there = slice(at, at + stop - start)
            if i in scaled:
                kept = weights[scaled.index(i)][:, there].astype(F32)
                sums += jnp.sum(value * kept, 1, keepdims=True)
                value = value * gain_ref[...]
            out[:, there] = value
            at += stop - start
    if carried:
        lane = lax.broadcasted_iota(jnp.int32, sums.shape, 1)
        sums = jnp.where(lane == 0, sums, carry[0][...])
    gain_out[...] = sums


def final(items, plan, scaled, gain, weights, carry=(), after=()):
    rows = gain.shape[0]
    outs = [out_of((rows, sum(b - a for _, a, b in spans)), F32) for spans in plan]
    outs.append(out_of((rows, LANES), F32))
    kernel = functools.partial(final_kernel, [len(i) for i in items], plan, scaled, len(carry))
    args = [gain, *carry, *weights, *[a for i in items for a in i]]
    return call(kernel, outs, args, after=after)


def distance_buckets(bounds_ref, dist, buckets):
    size = jnp.abs(dist)
    half = jnp.zeros(dist.shape, jnp.int32)
    for b in range(bounds_ref.shape[0]):
        half += (size >= bounds_ref[b]).astype(jnp.int32)
    return half + jnp.where(dist > 0, buckets // 2, 0)


def bases_kernel(bounds_ref, table_ref, near_ref, far_ref):
    heads, _, width = near_ref.shape
    buckets = table_ref.shape[1]
    row = lax.broadcasted_iota(jnp.int32, (8, width), 0)
    for to, sign in ((near_ref, 1), (far_ref, -1)):
        dist = sign * (lax.broadcasted_iota(jnp.int32, (8, width), 1) - width // 2)
        marks = distance_buckets(bounds_ref, dist, buckets)
        marks = jnp.concatenate([marks] * (buckets // 8), 0)
        onehot = (marks == lax.broadcasted_iota(jnp.int32, (buckets, width), 0)).astype(F32)
        line = dot(table_ref[...], onehot.astype(BF))
        for h in range(heads):
            field = jnp.broadcast_to(line[h : h + 1], (8, width))
            for k in (1, 2, 4):
                field = jnp.where((row & k) != 0, pltpu.roll(field, k, 1), field)
            while field.shape[0] < LANES:
                field = jnp.concatenate([field, pltpu.roll(field, field.shape[0], 1)], 0)
            to[h] = field.astype(BF)


def bias_bases(boundaries, table, heads, width, after=()):
    shape = out_of((heads, LANES, width), BF)
    return call(
        bases_kernel, [shape, shape], [boundaries, table], ins=[SMEM, VMEM], mib=16, after=after
    )


def bucket_field(bounds_ref, fields, buckets, first):
    width = fields[0].shape[-1]
    dist = width // 2 - lax.broadcasted_iota(jnp.int32, (8, width), 1)
    marks = distance_buckets(bounds_ref, dist, buckets)
    row = lax.broadcasted_iota(jnp.int32, (8, width), 0)
    line = jnp.zeros((8, width), F32)
    for h, field in enumerate(fields, first):
        while field.shape[0] > 8:
            half = field.shape[0] // 2
            field = field[:half] + pltpu.roll(field[half:], width - half, 1)
        for k in (4, 2, 1):
            field = jnp.where((row & k) != 0, pltpu.roll(field, width - k, 1), field)
        line = jnp.where(row == h, jnp.sum(field, 0, keepdims=True), line)
    lane = lax.broadcasted_iota(jnp.int32, (8, LANES), 1)
    out = jnp.zeros((8, LANES), F32)
    for b in range(buckets):
        total = jnp.sum(jnp.where(marks == b, line, 0.0), 1, keepdims=True)
        out = jnp.where(lane == b, total, out)
    return out


def split_low(values, lane, off, rest):
    high = values.astype(BF).astype(F32)
    mid = (values - high).astype(BF).astype(F32)
    low = values - high - mid
    return jnp.where(
        lane == off,
        high,
        jnp.where(lane == off + 1, mid, jnp.where(lane == off + 2, low, rest)),
    )


def three_ones(lane, off):
    return jnp.where((lane >= off) & (lane < off + 3), 1.0, 0.0)


def slots_of(batches):
    at = 0
    for b, (slots, length) in enumerate(batches):
        for s in range(slots):
            yield b, s, length, slice(at, at + length)
            at += length


def attend_kernel(batches, halves, *refs):
    places, lens = refs[0], refs[1 : 1 + len(batches)]
    refs = refs[1 + len(batches) :]
    normed_ref, near_ref = refs[:2]
    sources = refs[2 : 2 + halves]
    aug_ref, k_ref, v_ref, o_ref, w_scr = refs[2 + halves :]
    width = near_ref.shape[-1]
    load(places, sources, w_scr, 0)
    for b, s, length, span in slots_of(batches):
        valid = lens[b][s]
        lane = lax.broadcasted_iota(jnp.int32, (length, LANES), 1)
        place = lax.broadcasted_iota(jnp.int32, (length, LANES), 0)
        masked = jnp.where(place >= valid, NEG, 0.0)
        qkv = dot(normed_ref[span, :], w_scr[...])
        q, k, v = (qkv[:, i * LANES : (i + 1) * LANES] for i in range(3))
        k_ref[span, :] = k.astype(BF)
        v_ref[span, :] = v.astype(BF)
        mixed = []
        for e in range(2):
            own = (lane >= DH) == (e == 1)
            off = DH * (1 - e)
            marker = jnp.where(lane == off + 3, 1.0, 0.0)
            q_own = jnp.where(own, q, marker).astype(BF)
            k_own = jnp.where(own, k, jnp.where(lane == off + 3, masked, 0.0)).astype(BF)
            v_own = jnp.where(own, v, 1.0).astype(BF)
            start = width // 2
            bias = [
                near_ref[e, :, start - a * LANES : start - a * LANES + length]
                for a in range(length // LANES)
            ]
            scores = dot_cols(q_own, k_own) + jnp.concatenate(bias, 0).astype(F32)
            top = jnp.max(scores, 1, keepdims=True)
            expo = jnp.exp(scores - top)
            sums = dot(expo.astype(BF), v_own)
            total = jnp.where(own, pltpu.roll(sums, DH, 1), sums)
            logsum = top + jnp.log(total)
            extra = split_low(-logsum, lane, off, marker)
            aug_ref[span, e * LANES : (e + 1) * LANES] = jnp.where(own, q, extra).astype(BF)
            mixed.append(sums / total)
        o_ref[span, :] = jnp.where(lane < DH, mixed[0], mixed[1]).astype(BF)


def pair_of(base, pair):
    return pl.BlockSpec((2,) + base.shape[1:], lambda i: (pair, 0, 0))


def attend(ring, batches, lens, near, unit, weights, at, pair, us, after=()):
    rows, width = unit.shape
    shapes = [pltpu.HBM((rows, c * LANES), BF) for c in (2, 1, 1)]
    shapes.append(out_of((rows, LANES), BF))
    return call(
        functools.partial(attend_kernel, batches, len(weights)),
        shapes,
        [ring.places, *lens, unit, near, *weights],
        ins=[SMEM] * (1 + len(lens))
        + [fixed(unit), pair_of(near, pair)]
        + [columns(w, at, 3 * LANES) for w in weights],
        out_specs=[fixed(s) for s in shapes],
        grid=(1,),
        scratch=[pltpu.VMEM((width, 3 * LANES), BF)],
        us=us,
        mib=14,
        after=after,
    )


def attend_back_kernel(batches, pair, buckets, before, priors, emits, *refs):
    lens, refs = refs[: len(batches)], refs[len(batches) :]
    bounds, places, unit_ref, go_ref, aug_ref, k_ref, v_ref, o_ref, far_ref = refs[:9]
    totals, (table_in, grads_ref, table_ref) = refs[9 : 9 + priors], refs[9 + priors : 12 + priors]
    outs, (gbase_ref, total) = refs[12 + priors : -2], refs[-2:]
    width = far_ref.shape[-1]
    gbase_ref[...] = jnp.zeros_like(gbase_ref)
    for b, s, length, span in slots_of(batches):
        valid = lens[b][s]
        lane = lax.broadcasted_iota(jnp.int32, (length, LANES), 1)
        place = lax.broadcasted_iota(jnp.int32, (length, LANES), 0)
        masked = jnp.where(place >= valid, NEG, 0.0)
        k = k_ref[span, :].astype(F32)
        v = v_ref[span, :].astype(F32)
        go = go_ref[span, :].astype(F32)
        both = go * o_ref[span, :].astype(F32)
        grads = []
        for e in range(2):
            own = (lane >= DH) == (e == 1)
            off = DH * (1 - e)
            q_own = aug_ref[span, e * LANES : (e + 1) * LANES]
            ones = three_ones(lane, off)
            k_own = jnp.where(own, k, jnp.where(lane == off + 3, masked, ones)).astype(BF)
            v_own = jnp.where(own, v, ones).astype(BF)
            delta = jnp.sum(jnp.where(own, both, 0.0), 1, keepdims=True)
            g_own = jnp.where(own, go, split_low(-delta, lane, off, 0.0)).astype(BF)
            cols = [
                slice(width // 2 - a * LANES, width // 2 - a * LANES + length)
                for a in range(length // LANES)
            ]
            bias = jnp.concatenate([far_ref[e, :, c] for c in cols], 0)
            probs = jnp.exp(dot_cols(k_own, q_own) + bias.astype(F32))
            ds = probs * dot_cols(v_own, g_own)
            for a, c in enumerate(cols):
                gbase_ref[e, :, c] += ds[a * LANES : (a + 1) * LANES]
            ds = ds.astype(BF)
            gv = dot(probs.astype(BF), g_own)
            grads.append((dot_rows(ds, k_own), dot(ds, q_own), gv))
        first = lane < DH
        for i, (a, b) in enumerate(zip(*grads)):
            grads_ref[span, i * LANES : (i + 1) * LANES] = jnp.where(first, a, b).astype(BF)
    table = table_in[...] + bucket_field(
        bounds, [gbase_ref[0], gbase_ref[1]], buckets, 2 * pair
    )
    table_ref[...] = table
    part = dot_rows(unit_ref[...], grads_ref[...])
    if not emits:
        outs[0][...] = part
        return
    step = 3 * LANES
    at = 0
    for value in [r[...] for r in totals[:before]] + [part] + [r[...] for r in totals[before:]]:
        total[:, at : at + value.shape[1]] = value
        at += value.shape[1]
    extra = None
    if total.shape[1] > at:
        total[:, at:] = jnp.zeros((total.shape[0], LANES), F32)
    if total.shape[1] > at and emits == 2:
        rows = outs[0].shape[1]
        extra = jnp.concatenate([table, jnp.zeros((rows - 8, LANES), F32)], 0)
        extra = jnp.concatenate([jnp.zeros((rows, at), F32), extra], 1)
    if emits == 2:
        emit(places, total, *outs, extra=extra)
    else:
        outs[0][...] = total[...]


def attend_back(
    ring, batches, lens, boundaries, buckets, far, unit, go, fwd, pair, table, before, rest, last, after=()
):
    rows, width = unit.shape
    step = 3 * LANES
    go_spec = pl.BlockSpec((rows, LANES), lambda i: (0, pair))
    given = rest is None
    priors = [] if given else [*before, *rest]
    cols = step + sum(p.shape[1] for p in priors) + (LANES if last else 0)
    outs = [out_of((rows, step), BF), out_of((8, LANES), F32)]
    made = [out_of((width, step), F32)] if given else emitted(ring, width, cols)
    emits = 0 if given else len(made)
    kernel = functools.partial(
        attend_back_kernel, batches, pair, buckets, len(before), len(priors), emits
    )
    grads, table, *made = call(
        kernel,
        outs + made,
        [*lens, boundaries, ring.places, unit, go, *fwd, far, *priors, table],
        ins=[SMEM] * (len(lens) + 2)
        + [fixed(unit), go_spec]
        + [fixed(a) for a in fwd]
        + [pair_of(far, pair)]
        + [fixed(a) for a in (*priors, table)],
        out_specs=[fixed(o) for o in outs + made],
        grid=(1,),
        scratch=[
            pltpu.VMEM((2,) + far.shape[1:], F32),
            pltpu.VMEM((8, LANES) if given else (width, cols), F32),
        ],
        mib=20,
        after=after,
    )
    if not given:
        share = width // ring.dp
        extra = jnp.pad(table, ((0, share - 8), (cols - LANES, 0))) if last else None
        made = halves(ring, made, extra)
    return grads, table, made


def rms_parts(field):
    scale = lax.rsqrt(jnp.mean(field * field, -1, keepdims=True) + EPS)
    return (scale, field * scale)


def norm_back(grad_unit, unit, scale):
    return scale * (grad_unit - unit * jnp.mean(grad_unit * unit, -1, keepdims=True))


def norm_kernel(count, short_ref, long_ref, unit_ref):
    unit_ref[...] = rms_parts(pick(count, short_ref, long_ref).astype(F32))[1].astype(BF)


def norm(xs, tile=512, after=()):
    out = out_of((xs[0].shape[0] + xs[1].shape[0], xs[0].shape[1]), BF)
    return call(
        functools.partial(norm_kernel, xs[0].shape[0] // tile),
        [out],
        xs,
        ins=pair_tiles(xs, tile),
        out_specs=[tiles(out, tile)],
        grid=(out.shape[0] // tile,),
        mib=8,
        after=after,
    )[0]


def sum_of(refs):
    total = refs[0][...].astype(F32)
    for r in refs[1:]:
        total = total + r[...].astype(F32)
    return total


def gelu_parts(x):
    c = 0.7978845608028654
    d = c * 0.044715
    square = x * x
    t = jnp.tanh(x * (c + d * square))
    half = 0.5 + 0.5 * t
    slope = half + (0.5 * x) * (1.0 - t * t) * (c + 3.0 * d * square)
    return x * half, slope


def ffn_first_kernel(halves, groups, pairs, emits, count, places, *refs):
    all_places, refs = [places, places, *refs[: groups - 1]], refs[groups - 1 :]
    g_refs, x_refs, refs = refs[:2], refs[2:4], refs[4:]
    o_refs, refs = refs[: groups * pairs], refs[groups * pairs :]
    sources, refs = refs[:halves], refs[halves:]
    unit_ref, scale_ref, out_ref, gn_ref = refs[:4]
    grads, (w_scr, total) = refs[4 : 4 + emits], refs[4 + emits :]
    units = total.shape[1] // 2
    step = pl.program_id(0)

    @pl.when(step == 0)
    def _():
        total[...] = jnp.zeros_like(total)
        at = 0
        count = halves // (1 + groups)
        for i, there in enumerate(all_places):
            at = load(there, sources[i * count : (i + 1) * count], w_scr, at)

    mixed = jnp.concatenate([r[...] for r in o_refs], 1)
    middle = pick(count, *x_refs).astype(F32) + dot_cols(mixed, w_scr[:, 2 * units :])
    scale, unit = rms_parts(middle)
    unit = unit.astype(BF)
    unit_ref[...] = unit
    scale_ref[...] = jnp.broadcast_to(scale, scale_ref.shape)
    g = pick(count, *g_refs)
    win, wout = w_scr[:, :units], w_scr[:, units : 2 * units]
    act, slope = gelu_parts(dot(unit, win))
    act = act.astype(BF)
    gpre = (dot(g, wout) * slope).astype(BF)
    lead = places[places.shape[0] - 1].astype(F32)
    out_ref[...] = (dot_cols(act, wout) + lead * middle).astype(BF)
    gn_ref[...] = dot_cols(gpre, win).astype(BF)
    total[:, :units] += dot_rows(unit, gpre)
    total[:, units:] += dot_rows(g, act)

    @pl.when(step == pl.num_programs(0) - 1)
    def _():
        if emits == 2:
            emit(places, total, *grads)
        else:
            grads[0][...] = total[...]


def ffn_first(ring, gs, xs, mixed, weights, out_weights, units, tile=512, after=()):
    rows = mixed[0].shape[0]
    width = xs[0].shape[1]
    groups = len(out_weights)
    pairs = len(mixed) // groups
    field = out_of((rows, width), BF)
    outs = [field, out_of((rows, LANES), F32), field, field]
    grads = emitted(ring, width, 2 * units)
    sources = [*weights, *[w for ws in out_weights for w in ws]]
    kernel = functools.partial(
        ffn_first_kernel, len(sources), groups, pairs, len(grads), xs[0].shape[0] // tile
    )
    return call(
        kernel,
        outs + grads,
        [ring.places, *ring.orders, *gs, *xs, *mixed, *sources],
        ins=[SMEM] * groups
        + pair_tiles(gs, tile)
        + pair_tiles(xs, tile)
        + [tiles(a, tile) for a in mixed]
        + [columns(w, 0, w.shape[-1]) for w in sources],
        out_specs=[tiles(o, tile) for o in outs] + [fixed(o) for o in grads],
        grid=(rows // tile,),
        scratch=[
            pltpu.VMEM((width, 2 * units + len(mixed) * LANES), BF),
            pltpu.VMEM((width, 2 * units), F32),
        ],
        mib=46,
        after=after,
    )


def ffn_next_kernel(halves, count, places, unit_ref, scale_ref, *refs):
    g_refs, (out_in, gn_in), refs = refs[:2], refs[2:4], refs[4:]
    sources, refs = refs[:halves], refs[halves:]
    out_ref, mid_ref, act_ref, gpre_ref, w_scr = refs
    units = w_scr.shape[1] // 2

    @pl.when(pl.program_id(0) == 0)
    def _():
        load(places, sources, w_scr, 0)

    win, wout = w_scr[:, :units], w_scr[:, units:]
    unit = unit_ref[...]
    g = pick(count, *g_refs)
    act, slope = gelu_parts(dot(unit, win))
    act = act.astype(BF)
    gpre = (dot(g, wout) * slope).astype(BF)
    act_ref[...] = act
    gpre_ref[...] = gpre
    out_ref[...] = (out_in[...] + dot_cols(act, wout)).astype(BF)
    lead = places[places.shape[0] - 1].astype(F32)
    back = norm_back(gn_in[...] + dot_cols(gpre, win), unit.astype(F32), scale_ref[:, :1])
    mid_ref[...] = (back + lead * g.astype(F32)).astype(BF)


def ffn_next(ring, unit, scale, gs, out, gn, weights, units, tile=512, after=()):
    rows, width = unit.shape
    outs = [out_of((rows, width), BF)] * 2 + [out_of((rows, units), BF)] * 2
    return call(
        functools.partial(ffn_next_kernel, len(weights), gs[0].shape[0] // tile),
        outs,
        [ring.places, unit, scale, *gs, out, gn, *weights],
        ins=[SMEM, tiles(unit, tile), tiles(scale, tile)]
        + pair_tiles(gs, tile)
        + [tiles(out, tile), tiles(gn, tile)]
        + [columns(w, 0, w.shape[-1]) for w in weights],
        out_specs=[tiles(o, tile) for o in outs],
        grid=(rows // tile,),
        scratch=[pltpu.VMEM((width, 2 * units), BF)],
        mib=40,
        after=after,
    )


def ffn_grads_kernel(emits, count, places, unit_ref, *refs):
    g_refs, (gpre_ref, act_ref) = refs[:2], refs[2:4]
    grads, total = refs[4:-1], refs[-1]
    step = pl.program_id(0)
    units = act_ref.shape[1]

    @pl.when(step == 0)
    def _():
        total[...] = jnp.zeros_like(total)

    total[:, :units] += dot_rows(unit_ref[...], gpre_ref[...])
    total[:, units:] += dot_rows(pick(count, *g_refs), act_ref[...])

    @pl.when(step == pl.num_programs(0) - 1)
    def _():
        if emits == 2:
            emit(places, total, *grads)
        else:
            grads[0][...] = total[...]


def ffn_grads(ring, unit, gs, gpre, act, tile=512, after=()):
    rows, width = unit.shape
    cols = 2 * act.shape[1]
    outs = emitted(ring, width, cols)
    return call(
        functools.partial(ffn_grads_kernel, len(outs), gs[0].shape[0] // tile),
        outs,
        [ring.places, unit, *gs, gpre, act],
        ins=[SMEM, tiles(unit, tile)]
        + pair_tiles(gs, tile)
        + [tiles(gpre, tile), tiles(act, tile)],
        out_specs=[fixed(o) for o in outs],
        grid=(rows // tile,),
        scratch=[pltpu.VMEM((width, cols), F32)],
        mib=26,
        after=after,
    )


def middle_kernel(halves, groups, pairs, places, *refs):
    mid_refs, refs = refs[:groups], refs[groups:]
    o_refs, refs = refs[:pairs], refs[pairs:]
    sources, (go_ref, total_ref, w_scr) = refs[:halves], refs[halves:]
    step = pl.program_id(0)

    @pl.when(step == 0)
    def _():
        total_ref[...] = jnp.zeros_like(total_ref)
        load(places, sources, w_scr, 0)

    grad = sum_of(mid_refs).astype(BF)
    go_ref[...] = dot(grad, w_scr[...]).astype(BF)
    total_ref[...] += dot_rows(grad, jnp.concatenate([r[...] for r in o_refs], 1))


def middle_back(ring, mids, mixed, weights, tile=512, after=()):
    rows, width = mids[0].shape
    pairs = len(mixed)
    cols = pairs * LANES
    go, total = out_of((rows, cols), BF), out_of((width, cols), F32)
    return call(
        functools.partial(middle_kernel, len(weights), len(mids), pairs),
        [go, total],
        [ring.places, *mids, *mixed, *weights],
        ins=[SMEM]
        + [tiles(a, tile) for a in (*mids, *mixed)]
        + [columns(w, 0, cols) for w in weights],
        out_specs=[tiles(go, tile), fixed(total)],
        grid=(rows // tile,),
        scratch=[pltpu.VMEM((width, cols), BF)],
        mib=20,
        after=after,
    )


def input_back_kernel(halves, groups, pairs, count, places, short_ref, long_ref, *refs):
    mid_refs, refs = refs[:groups], refs[groups:]
    g_refs, refs = refs[:pairs], refs[pairs:]
    sources, (part_ref, w_scr) = refs[:-2], refs[-2:]

    @pl.when(pl.program_id(0) == 0)
    def _():
        at = 0
        for i in range(0, len(sources), halves):
            at = load(places, sources[i : i + halves], w_scr, at)

    part = dot_cols(jnp.concatenate([r[...] for r in g_refs], 1), w_scr[...])
    scale, unit = rms_parts(pick(count, short_ref, long_ref).astype(F32))
    lead = places[places.shape[0] - 1].astype(F32)
    part_ref[...] = (norm_back(part, unit, scale) + lead * sum_of(mid_refs)).astype(BF)


def input_back(ring, xs, mids, grads, weights, tile=512, after=()):
    rows, width = grads[0].shape[0], xs[0].shape[1]
    pairs = len(grads)
    out = out_of((rows, width), BF)
    return call(
        functools.partial(
            input_back_kernel, len(weights[0][0]), len(mids), pairs, xs[0].shape[0] // tile
        ),
        [out],
        [ring.places, *xs, *mids, *grads, *[a for blocks, _ in weights for a in blocks]],
        ins=[SMEM]
        + pair_tiles(xs, tile)
        + [tiles(a, tile) for a in (*mids, *grads)]
        + [columns(a, 0, count) for blocks, count in weights for a in blocks],
        out_specs=[tiles(out, tile)],
        grid=(rows // tile,),
        scratch=[pltpu.VMEM((width, 3 * pairs * LANES), BF)],
        mib=16,
        after=after,
    )[0]


def pad_cols(array, cols):
    return jnp.pad(array, ((0, 0), (0, cols - array.shape[1]))) if cols > array.shape[1] else array


def on_device(
    sizes,
    x_short,
    x_long,
    len_short,
    len_long,
    boundaries,
    q_weight,
    k_weight,
    v_weight,
    out_weight,
    in_weight,
    ff_out_weight,
    attn_gain,
    ffn_gain,
    bias_table,
    cot_short,
    cot_long,
):
    MARKS.clear()
    ring = Ring(sizes)
    quarter = ring.quarter
    width = x_short.shape[2]
    buckets, heads = bias_table.shape
    real = heads * DH
    cols = -(-real // LANES) * LANES
    pairs = cols // LANES
    units = in_weight.shape[1] // 2
    batches = [x.shape[:2] for x in (x_short, x_long)]
    lens = (len_short, len_long)

    xs = [x.reshape(-1, width) for x in (x_short, x_long)]
    gs = [g.reshape(-1, width) for g in (cot_short, cot_long)]

    col_a, col_f = (v.astype(F32)[:, None] for v in (attn_gain, ffn_gain))
    padded = [pad_cols(w, cols) for w in (q_weight, k_weight, v_weight, out_weight)]
    scaled = [(w.astype(F32) * col_a).astype(BF) for w in padded[:3]]
    pieces = [[w[:, p * LANES : (p + 1) * LANES] for w in scaled] for p in range(pairs)]
    own = jnp.concatenate([w for piece in pieces for w in piece] + [padded[3]], 1)[None]
    win = (in_weight.astype(F32) * col_f).astype(BF)
    own1, own2 = (
        jnp.concatenate([w[:, at : at + units] for w in (win, ff_out_weight)], 1)[None]
        for at in (0, units)
    )
    step = 3 * LANES
    z = tuple(range(quarter))
    table = jnp.pad(bias_table.T, ((0, 8 - heads), (0, 0)))

    two = (0, 1)
    wide = own.shape[2]
    got = ring.far(own)
    span = 2 * max(length for _, length in batches)
    near, far = bias_bases(boundaries, table, cols // DH, span, after=[own])
    held, own1 = join([own, *got], [(z, 0, wide)], after=[near], through=[own1])
    got = ring.first(held)
    got1 = ring.far(own1)
    unit = norm(xs, after=[held])
    plan = [(two, 0, step), (two, step, wide)]
    *helds, own2 = join([held, got], plan, after=[unit], through=[own2])
    qkv, more = [blocks_of(ring, h, ring.last(h)) for h in helds]
    out_at = (pairs - 1) * step
    out_w = [m[..., out_at:] for m in more]
    qkvs = [(qkv, 0)] + [(more, p * step) for p in range(pairs - 1)]
    out_ws = [out_w] + list(zip(*[ring.exchange(w) for w in out_w]))

    fwd = []
    after = helds
    for p in range(pairs):
        fwd.append(
            attend(
                ring,
                batches,
                lens,
                near,
                unit,
                *qkvs[p],
                p,
                C2 if p == pairs - 1 else C1 if p == 1 else 0.001,
                after=after,
            )
        )
        if p == 0:
            held1, own2 = join(
                [own1, *got1], [(z, 0, 2 * units)], after=[fwd[0][0]], through=[own2]
            )
            got1 = ring.first(held1)
            got2 = ring.far(own2)
            (held1,) = join([held1, got1], [(two, 0, 2 * units)])
            got1 = ring.last(held1)
            after = [held1, *out_w]
        if p == min(1, pairs - 1):
            (held2,) = join([own2, *got2], [(z, 0, 2 * units)], after=[fwd[p][0]])
            got2 = ring.first(held2)
            after = [held2]
    mixed = [f[3] for f in fwd]
    others = list(zip(*[ring.exchange(o) for o in mixed]))
    (held2,) = join([held2, got2], [(two, 0, 2 * units)], after=[fwd[-1][0]])
    got2 = ring.last(held2)
    first = blocks_of(ring, held1, got1)
    second = blocks_of(ring, held2, got2)

    unit_f, scale, out, gn, *grad1 = ffn_first(
        ring, gs, xs, [*mixed, *[o for g in others for o in g]], first, out_ws, units, after=[held2]
    )
    keep1, send = halves(ring, grad1)
    got1 = ring.last(send)
    out, mid, act, gpre = ffn_next(ring, unit_f, scale, gs, out, gn, second, units)
    keep1, send, mid, out = fold((keep1, got1, 0), through=[mid, out])
    mids = [mid] + ring.exchange(mid)
    outs = [out] + ring.exchange(out)
    got1 = ring.first(send)
    keep2, send2 = halves(ring, ffn_grads(ring, unit_f, gs, gpre, act, after=[keep1]))
    keep1, *sends, send2 = fold((keep1, got1, 1), after=[keep2], through=[send2])
    got1 = ring.far_all(sends)
    got2 = ring.last(send2)
    go, grad_o = middle_back(ring, mids, mixed, out_w, after=[keep1])

    grads = []
    totals = []
    sums = jnp.zeros((8, LANES), F32)
    after = [keep1]
    for p in range(pairs):
        last = p == pairs - 1
        before, rest = ((), ()) if last else (totals, [grad_o] if p == pairs - 2 else None)
        g, sums, made = attend_back(
            ring,
            batches,
            lens,
            boundaries,
            buckets,
            far,
            unit,
            go,
            fwd[p],
            p,
            sums,
            before,
            rest,
            last,
            after=after,
        )
        grads.append(g)
        if p < pairs - 2:
            totals.append(made[0])
        if p == 0:
            keep2, send2 = fold((keep2, got2, 0), after=[g])
            got2 = ring.first(send2)
            after = [keep2]
        if p == pairs - 2:
            early, send = made
            keep2, *sends, send = fold((keep2, got2, 1), after=[g, *got1], through=[send])
            got2 = ring.far_all(sends)
            got = ring.last(send)
            after = [keep2]
    keep, send = made
    early, early_send, send = fold((early, got, 0), after=got2, through=[send])
    early_got = ring.first(early_send)
    got = ring.last(send)
    weights = [(qkv, step), (more, (pairs - 1) * step)]
    part = input_back(ring, xs, mids, grads, weights, after=[early])
    rows = [slice(0, xs[0].shape[0]), slice(xs[0].shape[0], None)]

    def sums_of(fields):
        return [sum(f[r].astype(F32) for f in fields).astype(BF) for r in rows]

    early, *made = fold(
        (early, early_got, 1), (keep, got, 0), through=[part]
    )
    sends, (keep, send, part) = made[: quarter - 1], made[quarter - 1 :]
    early = [early, *ring.far_all(sends)]
    got = ring.first(send)
    parts = [part] + ring.exchange(part)
    keep, *sends, part, out = fold((keep, got, 1), after=[keep], through=[parts[0], outs[0]])
    ys = sums_of([out] + outs[1:])
    late = [keep, *ring.far_all(sends)]
    grad_xs = sums_of([part] + parts[1:])
    plan = [
        [(0, 0, units), (1, 0, units)],
        [(0, units, 2 * units), (1, units, 2 * units)],
    ]
    grad_in, grad_ff, gain_f = final(
        [[keep1, *got1], [keep2, *got2]], plan, [0], col_f, [in_weight], after=[*grad_xs, *ys]
    )
    plan = [
        [(0, p * step + i * LANES, p * step + (i + 1) * LANES) for p in range(pairs - 1)]
        + [(1, i * LANES, (i + 1) * LANES)]
        for i in range(3)
    ]
    plan += [[(0, (pairs - 1) * step, (pairs - 1) * step + cols)], [(1, step, step + LANES)]]
    gq, gk, gv, grad_o, sums, gain = final(
        [early, late], plan, [0, 1, 2], col_a, padded[:3], carry=[gain_f]
    )
    for other in ring.exchange(gain):
        gain = gain + other
    return (
        ys[0].reshape(x_short.shape),
        ys[1].reshape(x_long.shape),
        grad_xs[0].reshape(x_short.shape),
        grad_xs[1].reshape(x_long.shape),
        gq[:, :real],
        gk[:, :real],
        gv[:, :real],
        grad_o[:, :real],
        grad_in,
        grad_ff,
        gain[:, 0],
        gain[:, 1],
        sums[:heads, :buckets].T,
    )


def solution(mesh):
    sizes = (mesh.shape["dp"], mesh.shape["mp"])
    return jax.shard_map(
        functools.partial(on_device, sizes),
        mesh=mesh,
        in_specs=(
            P("dp", None, None),
            P("dp", None, None),
            P("dp"),
            P("dp"),
            P(),
            P("dp", "mp"),
            P("dp", "mp"),
            P("dp", "mp"),
            P("dp", "mp"),
            P("dp", "mp"),
            P("dp", "mp"),
            P("dp"),
            P("dp"),
            P(None, "mp"),
            P("dp", None, None),
            P("dp", None, None),
        ),
        out_specs=(
            P("dp", None, None),
            P("dp", None, None),
            P("dp", None, None),
            P("dp", None, None),
            P("dp", "mp"),
            P("dp", "mp"),
            P("dp", "mp"),
            P("dp", "mp"),
            P("dp", "mp"),
            P("dp", "mp"),
            P("dp"),
            P("dp"),
            P(None, "mp"),
        ),
        check_vma=False,
    )
```
